32 devices in a mesh: dap: 32 (over z, y, x, core).
Axes of the slice: x: 2, y: 2, z: 4, core: 2. Of those that a mesh axis runs over, the one named last changes fastest.
Arguments:
- alignment_embedding: bfloat16 [32, 320, 256], P('dap'), may hold values from -6 to 6
- couple_embedding: bfloat16 [320, 320, 128], P('dap'), may hold values from -6 to 6
- amino_strand: int32 [320], replicated, may hold values from 0 to 3, never falling along the last dimension, each value on 1 to 160 neighbouring positions
- amino_validity: int32 [320], replicated, may hold values from 0 to 1, as said below
- alignment_validity: int32 [32, 320], replicated, may hold values from 0 to 1, as said below
- separation_embedding: float32 [66, 128], replicated, may hold values from -3 to 3
- couple_shift_scaling: float32 [128], replicated, may hold values from 0.25 to 1.75
- couple_shift_factors: bfloat16 [128, 8], replicated, may hold values from -0.5 to 0.5
- horizontal_scaling_factor: float32 [256], replicated, may hold values from 0.25 to 1.75
- horizontal_entry_factors: bfloat16 [256, 4, 256], replicated, may hold values from -1 to 1
- horizontal_exit_factors: bfloat16 [256, 256], replicated, may hold values from -0.375 to 0.375
- vertical_scaling_factor: float32 [256], replicated, may hold values from 0.25 to 1.75
- vertical_entry_factors: bfloat16 [256, 4, 256], replicated, may hold values from -1 to 1
- vertical_exit_factors: bfloat16 [256, 256], replicated, may hold values from -0.375 to 0.375
- alignment_feedforward_scaling: float32 [256], replicated, may hold values from 0.25 to 1.75
- alignment_widen_factors: bfloat16 [256, 1024], replicated, may hold values from -0.375 to 0.375
- alignment_narrow_factors: bfloat16 [1024, 256], replicated, may hold values from -0.1875 to 0.1875
- product_scaling_factor: float32 [256], replicated, may hold values from 0.25 to 1.75
- product_twin_factors: bfloat16 [256, 64], replicated, may hold values from -0.375 to 0.375
- product_exit_factors: bfloat16 [1024, 128], replicated, may hold values from -0.75 to 0.75
- couple_feedforward_scaling: float32 [128], replicated, may hold values from 0.25 to 1.75
- couple_widen_factors: bfloat16 [128, 512], replicated, may hold values from -0.5 to 0.5
- couple_narrow_factors: bfloat16 [512, 128], replicated, may hold values from -0.25 to 0.25
Outputs:
- updated_sequences: bfloat16 [32, 320, 256], P(None, 'dap')
- updated_pairs: bfloat16 [320, 320, 128], P('dap')
The draws below stay inside these ranges and needn't reach their ends.
Inputs may be any that keep to these rules, and one draw needn't show every extreme that they name: `amino_validity`: 1 on a leading run of 160 or more residues, 0 after it; the last residue is 0. `alignment_validity`: row 0 and residue 0 are 1 throughout.
All inputs are finite; a program needn't handle non-finite values.
Results may differ from the reference program's by a relative error of at most 0.013.
Values may be sent and summed in bfloat16 or wider, within the bound.
No kernel may reach another device: no remote copies, remote signals or barrier semaphores. Data moves between devices by JAX's collectives and lax.ppermute only.
A program may use at most 192 MiB of HBM per device.

```python
import math
import jax
import jax.numpy as jnp
import numpy as np
from jax import lax

ALIGNED_FEATURES = 256
D_Z = 128
FOCUS_COUNT = 8
FOCUS_WIDTH = 32
PRODUCT_FEATURES = 32
ALIGNED_WIDENED = 1024
PAIR_HIDDEN = 512
SHARD_LENGTH = 10
CUT_LENGTH = 320
ALIGNED_COUNT = 32
BINS = 66
N_DAP = 32


def tilted(starting_amount):
    return jnp.clip(jnp.stack([starting_amount[:, 0], starting_amount[:, 1], starting_amount[:, 2], starting_amount[:, 3]], 1), -1.0, 1.0)


def draw_amino_validity(key, part):
    key = jax.random.fold_in(key, 3)
    length = jax.random.randint(key, (), CUT_LENGTH // 2, CUT_LENGTH)
    return (jnp.arange(CUT_LENGTH) < length).astype(jnp.int32)


def draw_alignment_validity(key, part):
    key = jax.random.fold_in(key, 5)
    content_arrays = jax.random.randint(key, (ALIGNED_COUNT, CUT_LENGTH), 0, 5)
    horizontal_lines = jnp.arange(ALIGNED_COUNT)[:, None] == 0
    cols = jnp.arange(CUT_LENGTH)[None, :] == 0
    return ((content_arrays > 0) | horizontal_lines | cols).astype(jnp.int32)


def draw_horizontal_entry_factors(key, part):
    key = jax.random.fold_in(key, 7)
    starting_amount = jax.random.normal(key, (ALIGNED_FEATURES, 4, FOCUS_COUNT * FOCUS_WIDTH), jnp.float32) * ALIGNED_FEATURES ** (-0.5)
    return tilted(starting_amount).astype(jnp.bfloat16)


def draw_vertical_entry_factors(key, part):
    key = jax.random.fold_in(key, 11)
    starting_amount = jax.random.normal(key, (ALIGNED_FEATURES, 4, FOCUS_COUNT * FOCUS_WIDTH), jnp.float32) * ALIGNED_FEATURES ** (-0.5)
    return tilted(starting_amount).astype(jnp.bfloat16)


def steps_of(rng, extent, pieces, low, high):
    level = 1.0
    for dim, blocks in pieces:
        heights = jax.random.uniform(jax.random.fold_in(jax.random.fold_in(rng, 6), dim), (blocks,), jnp.float32, low / len(pieces), high / len(pieces))
        level = level * jnp.repeat(jnp.exp(heights), extent[dim] // blocks).reshape((-1,) + (1,) * (len(extent) - 1 - dim))
    return level


def split_up(count, total, reach, slope):
    loads = [(1 << 20) // math.isqrt(standing ** slope) + 1 for standing in range(2, count + 1)]
    surplus, holding = total - reach - (count - 1), [1] * (count - 1)
    while surplus > 0:
        candidates = [i for i in range(count - 1) if holding[i] < reach]
        pool, budget = sum([loads[i] for i in candidates]), surplus
        for i in candidates:
            more = min(reach - holding[i], max(1, budget * loads[i] // pool), surplus)
            holding[i] = holding[i] + more
            surplus = surplus - more
    return np.array([reach] + holding)


def ragged(rng, count, total, most, skew):
    if count == 2:
        one = jax.random.randint(rng, (), max(1, total - most), min(most, total - 1) + 1)
        return jnp.stack([one, total - one])
    tallies = jnp.asarray(split_up(count, total, most, skew), jnp.int32)
    couples = (count - 1) // 2
    donor, sink = tallies[1:1 + 2 * couples:2], tallies[2:2 + 2 * couples:2]
    slack = jnp.minimum(donor - 1, most - sink)
    passed = jax.random.randint(jax.random.fold_in(rng, 1), (couples,), 0, 1 << 20) % (slack + 1)
    tallies = tallies.at[1:1 + 2 * couples:2].set(donor - passed).at[2:2 + 2 * couples:2].set(sink + passed)
    return tallies[jax.random.permutation(jax.random.fold_in(rng, 2), count)]


def noise(own_key, extent, scale, reach, split=(), held_as=jnp.bfloat16):
    values = jax.random.normal(own_key, extent, jnp.float32) * scale
    if len(split) > 0:
        values = steps_of(own_key, extent, split, -0.22, 0.18) * values
    return jnp.clip(values, min=-reach, max=reach).astype(held_as)


def setup_inputs(seed: int = 0) -> dict:
    key_of = jax.random.split(jax.random.key(seed), 24)
    return {
        "alignment_embedding": noise(key_of[0], (ALIGNED_COUNT, CUT_LENGTH, ALIGNED_FEATURES), 1.0, 6.0, ((0, 32),)),
        "couple_embedding": noise(key_of[1], (CUT_LENGTH, CUT_LENGTH, D_Z), 1.0, 6.0, ((0, 32),)),
        "amino_strand": jnp.searchsorted(jnp.cumsum(ragged(key_of[2], 4, CUT_LENGTH, CUT_LENGTH // 2, 0)), jnp.arange(CUT_LENGTH), side="right").astype(jnp.int32),
        "amino_validity": draw_amino_validity(jax.random.fold_in(key_of[23], 71), 0),
        "alignment_validity": draw_alignment_validity(jax.random.fold_in(key_of[23], 71), 0),
        "separation_embedding": noise(key_of[5], (BINS, D_Z), 0.5, 3.0, (), jnp.float32),
        "couple_shift_scaling": jnp.clip(1.0 + 0.15 * jax.random.normal(key_of[6], (D_Z,), jnp.float32), 0.25, 1.75),
        "couple_shift_factors": noise(key_of[7], (D_Z, FOCUS_COUNT), D_Z ** -0.5, 0.5),
        "horizontal_scaling_factor": jnp.clip(1.0 + 0.15 * jax.random.normal(key_of[8], (ALIGNED_FEATURES,), jnp.float32), 0.25, 1.75),
        "horizontal_entry_factors": draw_horizontal_entry_factors(jax.random.fold_in(key_of[23], 71), 0),
        "horizontal_exit_factors": noise(key_of[10], (FOCUS_COUNT * FOCUS_WIDTH, ALIGNED_FEATURES), (FOCUS_COUNT * FOCUS_WIDTH) ** -0.5, 0.375),
        "vertical_scaling_factor": jnp.clip(1.0 + 0.15 * jax.random.normal(key_of[11], (ALIGNED_FEATURES,), jnp.float32), 0.25, 1.75),
        "vertical_entry_factors": draw_vertical_entry_factors(jax.random.fold_in(key_of[23], 71), 0),
        "vertical_exit_factors": noise(key_of[13], (FOCUS_COUNT * FOCUS_WIDTH, ALIGNED_FEATURES), (FOCUS_COUNT * FOCUS_WIDTH) ** -0.5, 0.375),
        "alignment_feedforward_scaling": jnp.clip(1.0 + 0.15 * jax.random.normal(key_of[14], (ALIGNED_FEATURES,), jnp.float32), 0.25, 1.75),
        "alignment_widen_factors": noise(key_of[15], (ALIGNED_FEATURES, ALIGNED_WIDENED), ALIGNED_FEATURES ** -0.5, 0.375),
        "alignment_narrow_factors": noise(key_of[16], (ALIGNED_WIDENED, ALIGNED_FEATURES), ALIGNED_WIDENED ** -0.5, 0.1875),
        "product_scaling_factor": jnp.clip(1.0 + 0.15 * jax.random.normal(key_of[17], (ALIGNED_FEATURES,), jnp.float32), 0.25, 1.75),
        "product_twin_factors": noise(key_of[18], (ALIGNED_FEATURES, 2 * PRODUCT_FEATURES), ALIGNED_FEATURES ** -0.5, 0.375),
        "product_exit_factors": noise(key_of[19], (PRODUCT_FEATURES * PRODUCT_FEATURES, D_Z), (2 * PRODUCT_FEATURES) ** -0.5, 0.75),
        "couple_feedforward_scaling": jnp.clip(1.0 + 0.15 * jax.random.normal(key_of[20], (D_Z,), jnp.float32), 0.25, 1.75),
        "couple_widen_factors": noise(key_of[21], (D_Z, PAIR_HIDDEN), D_Z ** -0.5, 0.5),
        "couple_narrow_factors": noise(key_of[22], (PAIR_HIDDEN, D_Z), PAIR_HIDDEN ** -0.5, 0.25),
    }


EPS = 1e-05
OUTER_EPS = 0.001
MASKED = -1000000000.0
HIGH = lax.Precision.HIGHEST

def apply_layer_norm(input_tensor, gain):
    input_tensor = input_tensor.astype(jnp.float32)
    centred = input_tensor - lax.optimization_barrier(jnp.mean(input_tensor, -1, keepdims=True))
    spread = lax.optimization_barrier(jnp.mean(centred * centred, -1, keepdims=True))
    return centred * lax.rsqrt(spread + EPS) * gain

def accurate_product(former_factor, right):
    return jnp.einsum('...d,de->...e', former_factor.astype(jnp.float32), right.astype(jnp.float32), precision=HIGH)

def linear_project(input_tensor, gain, weights):
    normed = apply_layer_norm(input_tensor, gain).astype(jnp.bfloat16)
    proj = jnp.einsum('rnd,dgc->grnc', normed.astype(jnp.float32), weights.astype(jnp.float32), precision=HIGH)
    horizontal_lines, cols, inner = (input_tensor.shape[0], input_tensor.shape[1], weights.shape[2])

    def heads(t):
        return t.reshape(horizontal_lines, cols, FOCUS_COUNT, inner // FOCUS_COUNT).transpose(2, 0, 1, 3).astype(jnp.bfloat16)
    return (heads(proj[0]), heads(proj[1]), heads(proj[2]), jax.nn.sigmoid(proj[3]))

def gated_attention(query_vectors, key_vectors, content_arrays, gate_logits, lookup_validity_shift, bias):
    scale = query_vectors.shape[-1] ** (-0.5)

    def one_head(args):
        qh, kh, vh, bh = args
        scores = jnp.einsum('ric,rjc->rij', qh.astype(jnp.float32), kh.astype(jnp.float32), precision=HIGH) * scale
        scores = scores + bh[None].astype(jnp.float32)
        scores = jnp.where(lookup_validity_shift[:, None, :] > 0, scores, MASKED)
        top = lax.optimization_barrier(jnp.max(scores, -1, keepdims=True))
        expo = jnp.exp(scores - top)
        weights = (expo / lax.optimization_barrier(jnp.sum(expo, -1, keepdims=True))).astype(jnp.bfloat16)
        return jnp.einsum('rij,rjc->ric', weights.astype(jnp.float32), vh.astype(jnp.float32), precision=HIGH)
    heads_out = lax.map(one_head, (query_vectors, key_vectors, content_arrays, bias))
    merged = heads_out.transpose(1, 2, 0, 3).reshape(gate_logits.shape)
    return (merged * gate_logits).astype(jnp.bfloat16)

def transition_block(input_tensor, gain, w_in, w_out):
    hidden = jax.nn.relu(accurate_product(apply_layer_norm(input_tensor, gain).astype(jnp.bfloat16), w_in)).astype(jnp.bfloat16)
    return input_tensor + accurate_product(hidden, w_out)

def entry_rows(pair_rows, chain_rows, pos_rows, amino_strand, separation_embedding):
    clip_offsets = (separation_embedding.shape[0] - 2) // 2
    positions = jnp.arange(amino_strand.shape[0], dtype=jnp.int32)
    same = chain_rows[:, None] == amino_strand[None, :]
    bins = jnp.where(same, jnp.clip(pos_rows[:, None] - positions[None, :] + clip_offsets, 0, 2 * clip_offsets), 2 * clip_offsets + 1)
    return pair_rows.astype(jnp.float32) + jnp.take(separation_embedding, bins, axis=0)

def reference(alignment_embedding, couple_embedding, amino_strand, amino_validity, alignment_validity, separation_embedding, couple_shift_scaling, couple_shift_factors, horizontal_scaling_factor, horizontal_entry_factors, horizontal_exit_factors, vertical_scaling_factor, vertical_entry_factors, vertical_exit_factors, alignment_feedforward_scaling, alignment_widen_factors, alignment_narrow_factors, product_scaling_factor, product_twin_factors, product_exit_factors, couple_feedforward_scaling, couple_widen_factors, couple_narrow_factors):
    pair_blocks = couple_embedding.reshape(N_DAP, SHARD_LENGTH, CUT_LENGTH, D_Z)
    chain_blocks = amino_strand.reshape(N_DAP, SHARD_LENGTH)
    pos_blocks = jnp.arange(CUT_LENGTH, dtype=jnp.int32).reshape(N_DAP, SHARD_LENGTH)

    def bias_block(args):
        pair_rows, chain_rows, pos_rows = args
        pair_one = entry_rows(pair_rows, chain_rows, pos_rows, amino_strand, separation_embedding)
        normed = apply_layer_norm(pair_one, couple_shift_scaling).astype(jnp.bfloat16)
        return jnp.einsum('ijz,zh->hij', normed.astype(jnp.float32), couple_shift_factors.astype(jnp.float32), precision=HIGH).astype(jnp.bfloat16)
    bias = lax.map(bias_block, (pair_blocks, chain_blocks, pos_blocks))
    bias = bias.transpose(1, 0, 2, 3).reshape(FOCUS_COUNT, CUT_LENGTH, CUT_LENGTH)
    lookup_validity_shift = alignment_validity.astype(jnp.float32) * amino_validity.astype(jnp.float32)[None, :]

    def lone_line(args):
        row, mask_row = args
        query_vectors, key_vectors, content_arrays, gate_logits = linear_project(row[None], horizontal_scaling_factor, horizontal_entry_factors)
        sigmoid_scaled_result = gated_attention(query_vectors, key_vectors, content_arrays, gate_logits, mask_row[None], bias)
        return (row.astype(jnp.float32) + accurate_product(sigmoid_scaled_result, horizontal_exit_factors)[0]).astype(jnp.bfloat16)
    alignment_past_horizontal = lax.map(lone_line, (alignment_embedding, lookup_validity_shift))
    vertical_validity_share = alignment_validity.astype(jnp.float32).T
    vertical_portions = alignment_past_horizontal.transpose(1, 0, 2).reshape(N_DAP, SHARD_LENGTH, ALIGNED_COUNT, ALIGNED_FEATURES)
    validity_portions = vertical_validity_share.reshape(N_DAP, SHARD_LENGTH, ALIGNED_COUNT)

    def vertical_increment(args):
        input_tensor, mask_row_slices = args
        query_vectors, key_vectors, content_arrays, gate_logits = linear_project(input_tensor, vertical_scaling_factor, vertical_entry_factors)
        empty_initialised = jnp.zeros((FOCUS_COUNT, ALIGNED_COUNT, ALIGNED_COUNT), jnp.bfloat16)
        sequence_after_columns = input_tensor.astype(jnp.float32) + accurate_product(gated_attention(query_vectors, key_vectors, content_arrays, gate_logits, mask_row_slices, empty_initialised), vertical_exit_factors)
        return transition_block(sequence_after_columns, alignment_feedforward_scaling, alignment_widen_factors, alignment_narrow_factors)
    alignment_past_feedforward = lax.map(vertical_increment, (vertical_portions, validity_portions)).reshape(CUT_LENGTH, ALIGNED_COUNT, ALIGNED_FEATURES)
    updated_sequences = alignment_past_feedforward.transpose(1, 0, 2).astype(jnp.bfloat16)
    projected_input = (accurate_product(apply_layer_norm(alignment_past_feedforward, product_scaling_factor).astype(jnp.bfloat16), product_twin_factors) * vertical_validity_share[:, :, None]).astype(jnp.bfloat16)
    former_factor = projected_input[:, :, :PRODUCT_FEATURES]
    right = projected_input[:, :, PRODUCT_FEATURES:]
    counts = accurate_product(vertical_validity_share, vertical_validity_share.T)
    former_portions = former_factor.reshape(N_DAP, SHARD_LENGTH, ALIGNED_COUNT, PRODUCT_FEATURES)
    count_blocks = counts.reshape(N_DAP, SHARD_LENGTH, CUT_LENGTH)

    def pair_block(args):
        pair_rows, chain_rows, pos_rows, left_rows, count_rows = args
        pair_one = entry_rows(pair_rows, chain_rows, pos_rows, amino_strand, separation_embedding)

        def one_res(inner):
            left_row, count_row = inner
            outer = jnp.einsum('sc,jse->jce', left_row.astype(jnp.float32), right.astype(jnp.float32), precision=HIGH)
            outer = outer.reshape(CUT_LENGTH, PRODUCT_FEATURES * PRODUCT_FEATURES).astype(jnp.bfloat16)
            return accurate_product(outer, product_exit_factors) / (count_row[:, None] + OUTER_EPS)
        pair_two = pair_one + lax.map(one_res, (left_rows, count_rows))

        def one_pair_row(row):
            return transition_block(row, couple_feedforward_scaling, couple_widen_factors, couple_narrow_factors)
        return lax.map(one_pair_row, pair_two).astype(jnp.bfloat16)
    updated_pairs = lax.map(pair_block, (pair_blocks, chain_blocks, pos_blocks, former_portions, count_blocks)).reshape(CUT_LENGTH, CUT_LENGTH, D_Z)
    return (updated_sequences, updated_pairs)
```

```python
import functools

import jax
import jax.numpy as jnp
from jax import lax
from jax.experimental import pallas as pl
from jax.experimental.pallas import tpu as pltpu
from jax.sharding import PartitionSpec as P

HEADS = 8
SUB = 8
EPS = 1e-05
OUTER_EPS = 0.001
MASKED = -1000000000.0
LOG2E = 1.4426950408889634
F32 = jnp.float32
BF16 = jnp.bfloat16
VMEM_LIMIT = 56 * 1024 * 1024


def dot(a, b):
    return jnp.dot(a, b, preferred_element_type=F32)


def dot_nt(a, b):
    return lax.dot_general(a, b, (((1,), (1,)), ((), ())), preferred_element_type=F32)


def dot_tn(a, b):
    return lax.dot_general(a, b, (((0,), (0,)), ((), ())), preferred_element_type=F32)


def layer_norm(x, gain):
    centred = x - jnp.mean(x, -1, keepdims=True)
    spread = jnp.mean(centred * centred, -1, keepdims=True)
    return centred * lax.rsqrt(spread + EPS) * gain


def iota(shape, dim):
    return lax.broadcasted_iota(jnp.int32, shape, dim)


def div_const(x, d, limit):
    m = 65536 // d + 1
    assert all((v * m) >> 16 == v // d for v in range(limit)) and limit * m < 2**31
    return (x * m) >> 16


def one_hot(match):
    return jnp.where(match, 1.0, 0.0).astype(BF16)


def chunks(total, step, body):
    if total == step:
        body(0)
    else:
        lax.fori_loop(0, total // step, lambda c, x: (body(pl.multiple_of(c * step, step)), x)[1], 0)


def pair_kernel(
    idx, chain, pair, chain_row, table, gain, factors, pair_one, bias, shifted, chain_wide, *, rows, length, bins
):
    step = pl.program_id(0)
    reach = (bins - 2) // 2

    @pl.when(step == 0)
    def _():
        k = iota((2 * length, bins), 0)
        wanted = jnp.clip(length - k + reach, 0, 2 * reach)
        pick = jnp.where(wanted == iota((2 * length, bins), 1), 1.0, 0.0)
        shifted[...] = jnp.dot(pick, table[...], precision=lax.Precision.HIGHEST, preferred_element_type=F32)
        eye = iota((length, length), 0) == iota((length, length), 1)
        column = jnp.sum(jnp.where(eye, chain_row[...].astype(F32), 0.0), axis=1, keepdims=True)
        chain_wide[...] = jnp.broadcast_to(column, chain_wide.shape)

    other = table[bins - 1 : bins, :]
    block = pair.shape[0]
    for r in range(block):
        i = idx[0] * rows + step * block + r
        near = shifted[pl.ds(length - i, length), :]
        same = chain_wide[...] == chain[i].astype(F32)
        x = pair[r].astype(F32) + jnp.where(same, near, other)
        pair_one[r] = x
        normed = layer_norm(x, gain[...]).astype(BF16)
        bias[r] = dot_nt(factors[...], normed).astype(BF16)


def pair_call(idx, chain, pair, table, gain, factors):
    rows, length, depth = pair.shape
    block = 5 if rows % 5 == 0 else 1
    bins = table.shape[0]
    smem = pl.BlockSpec(memory_space=pltpu.SMEM)
    whole = lambda *shape: pl.BlockSpec(shape, lambda s: (0,) * len(shape))
    return pl.pallas_call(
        functools.partial(pair_kernel, rows=rows, length=length, bins=bins),
        grid=(rows // block,),
        in_specs=[
            smem,
            smem,
            pl.BlockSpec((block, length, depth), lambda s: (s, 0, 0)),
            whole(1, length),
            whole(bins, depth),
            whole(1, depth),
            whole(HEADS, depth),
        ],
        out_specs=[
            pl.BlockSpec((block, length, depth), lambda s: (s, 0, 0)),
            pl.BlockSpec((block, HEADS, length), lambda s: (s, 0, 0)),
        ],
        out_shape=[
            jax.ShapeDtypeStruct((rows, length, depth), F32),
            jax.ShapeDtypeStruct((rows, HEADS, length), BF16),
        ],
        scratch_shapes=[pltpu.VMEM((2 * length, depth), F32), pltpu.VMEM((length, depth), F32)],
        compiler_params=pltpu.CompilerParams(vmem_limit_bytes=VMEM_LIMIT),
        cost_estimate=pl.CostEstimate(flops=4 * rows * length * depth * HEADS, bytes_accessed=4000000, transcendentals=0),
        name="pair_bias",
    )(idx, chain, pair, chain[None, :], table, gain[None, :], factors.T)


def row_kernel(idx, *refs, sub, far, rows, length, width):
    row_refs, refs = refs[:sub], refs[sub:]
    bias_refs, refs = refs[:far], refs[far:]
    validity, amino, gain, entry, exit_, out, keys, values, bias, own_normed, own_rows, query, gate, gated = refs
    me = idx[0]
    z, p = me // sub, me % sub
    own = far * rows
    scale = (width // HEADS) ** -0.5 * LOG2E

    r = iota((own, length), 0)
    block = div_const(r, rows, own)
    residue = ((z ^ block) * sub + p) * rows + r - block * rows
    pick = one_hot(residue == iota((own, length), 1))

    step = min(length, 320)
    for k in range(sub):

        def project(start, k=k):
            normed = layer_norm(row_refs[k][0, pl.ds(start, step), :].astype(F32), gain[...]).astype(BF16)
            both = dot(normed, entry[:, width : 3 * width])
            keys[k, pl.ds(start, step), :] = both[:, :width].astype(BF16)
            values[k, pl.ds(start, step), :] = both[:, width:].astype(BF16)
            part = pick if length == step else one_hot(residue[:, :step] == iota((own, step), 1) + start)
            q_rows, a_rows = dot(part, normed), dot(part, row_refs[k][0, pl.ds(start, step), :])
            here = pl.ds(k * own, own)
            if length == step:
                own_normed[here, :] = q_rows
                own_rows[here, :] = a_rows
            else:
                fresh = start == 0
                own_normed[here, :] = q_rows + jnp.where(fresh, 0.0, own_normed[here, :])
                own_rows[here, :] = a_rows + jnp.where(fresh, 0.0, own_rows[here, :])

        chunks(length, step, project)

    total = sub * own
    part = min(total, 320)

    def queries(start):
        here = pl.ds(start, part)
        normed = own_normed[here, :].astype(BF16)
        query[here, :] = dot(normed, entry[:, :width]) * scale
        gate[here, :] = jax.nn.sigmoid(dot(normed, entry[:, 3 * width :]))

    chunks(total, part, queries)

    for b in range(far):
        bias[b * rows : (b + 1) * rows] = bias_refs[b][...].astype(F32) * LOG2E

    head_of = iota((HEADS, width), 1) // (width // HEADS)
    head_mask = jnp.where(head_of == iota((HEADS, width), 0), 1.0, 0.0)
    take = 40 if own % 40 == 0 else rows

    def attend(n, k, start):
        s = z * sub + (p ^ k)
        valid = validity[pl.ds(s, 1), :] * amino[...]
        masked = jnp.where(valid > 0, 0.0, MASKED)
        here = pl.ds(pl.multiple_of(n * take, take), take) if not isinstance(n, int) else pl.ds(n * take, take)
        q = (query[here, :][:, None, :] * head_mask[None]).reshape(take * HEADS, width).astype(BF16)
        scores = dot_nt(q, keys[k]) + bias[pl.ds(start, take)].reshape(take * HEADS, length) + masked
        expo = jnp.exp2(scores - jnp.max(scores, -1, keepdims=True))
        total_ = jnp.sum(expo, -1, keepdims=True)
        mixed = dot(expo.astype(BF16), values[k]) / total_
        merged = jnp.sum(mixed.reshape(take, HEADS, width) * head_mask[None], axis=1)
        gated[here, :] = merged * gate[here, :]

    parts = own // take
    if parts == 1:
        for k in range(sub):
            attend(k, k, 0)
    else:
        lax.fori_loop(0, sub * parts, lambda n, x: (attend(n, n // parts, (n % parts) * take), x)[1], 0)

    def leave(start):
        q = iota((part, total), 0) + start
        residue_, row = div_const(q, sub, total), q & (sub - 1)
        swap = one_hot((row ^ p) * own + residue_ == iota((part, total), 1))
        gated_rows = dot(swap, gated[...].astype(BF16)).astype(BF16)
        x = dot(swap, own_rows[...].astype(BF16)) + dot(gated_rows, exit_[...])
        out[pl.ds(start, part), :] = x.astype(BF16)

    chunks(total, part, leave)


def row_call(idx, msa_rows, bias_blocks, validity, amino, gain, entry, exit_):
    sub, far = len(msa_rows), len(bias_blocks)
    _, length, width = msa_rows[0].shape
    rows = bias_blocks[0].shape[0]
    own = far * rows
    vmem = pl.BlockSpec(memory_space=pltpu.VMEM)
    return pl.pallas_call(
        functools.partial(row_kernel, sub=sub, far=far, rows=rows, length=length, width=width),
        in_specs=[pl.BlockSpec(memory_space=pltpu.SMEM)] + [vmem] * (sub + far + 5),
        out_specs=vmem,
        out_shape=jax.ShapeDtypeStruct((own * sub, width), BF16),
        scratch_shapes=[
            pltpu.VMEM((sub, length, width), BF16),
            pltpu.VMEM((sub, length, width), BF16),
            pltpu.VMEM((own, HEADS, length), F32),
            pltpu.VMEM((sub * own, width), F32),
            pltpu.VMEM((sub * own, width), F32),
            pltpu.VMEM((sub * own, width), F32),
            pltpu.VMEM((sub * own, width), F32),
            pltpu.VMEM((sub * own, width), F32),
        ],
        compiler_params=pltpu.CompilerParams(vmem_limit_bytes=VMEM_LIMIT),
        cost_estimate=pl.CostEstimate(flops=10**10, bytes_accessed=4000000, transcendentals=10**6),
        name="row_attention",
    )(idx, *msa_rows, *bias_blocks, validity, amino[None, :], gain[None, :], entry, exit_)


def column_kernel(idx, *refs, sub, far, rows, block, depth, width):
    piece_refs, refs = refs[:far], refs[far:]
    (
        validity,
        col_gain,
        entry,
        exit_,
        ff_gain,
        widen,
        narrow,
        product_gain,
        twin,
        updated,
        left,
        right,
        start_rows,
        gated,
    ) = refs
    me = idx[0]
    z = me // sub
    first = me * rows + pl.program_id(0) * block
    scale = (width // HEADS) ** -0.5 * LOG2E
    total = block * depth
    for b in range(far):
        here = pl.ds(pl.multiple_of((z ^ b) * sub, sub), sub)
        start_rows[:, here, :] = piece_refs[b][...].astype(F32)
    x = start_rows[...].reshape(total, width)
    normed = layer_norm(x, col_gain[...]).astype(BF16)
    proj = dot(normed, entry[...])
    query = proj[:, :width] * scale
    keys = proj[:, width : 2 * width].astype(BF16)
    values = proj[:, 2 * width : 3 * width].astype(BF16)
    gate = jax.nn.sigmoid(proj[:, 3 * width :])

    length = validity.shape[1]
    lanes = 128
    pick = one_hot(iota((length, lanes), 0) == first + iota((length, lanes), 1))
    valid = dot(validity[...].astype(F32).astype(BF16), pick)
    head_of = iota((HEADS, width), 1) // (width // HEADS)
    head_mask = jnp.where(head_of == iota((HEADS, width), 0), 1.0, 0.0)
    for i in range(block):
        here = slice(i * depth, (i + 1) * depth)
        q = (query[here][:, None, :] * head_mask[None]).reshape(depth * HEADS, width).astype(BF16)
        masked = jnp.where(valid[:, i : i + 1] > 0, 0.0, MASKED)
        scores = dot_nt(keys[here], q) + masked
        expo = jnp.exp2(scores - jnp.max(scores, 0, keepdims=True))
        weights = (expo / jnp.sum(expo, 0, keepdims=True)).astype(BF16)
        mixed = dot_tn(weights, values[here])
        merged = jnp.sum(mixed.reshape(depth, HEADS, width) * head_mask[None], axis=1)
        gated[here, :] = merged * gate[here]
    x = x + dot(gated[...].astype(BF16), exit_[...])
    hidden = jnp.maximum(dot(layer_norm(x, ff_gain[...]).astype(BF16), widen[...]), 0.0).astype(BF16)
    x = x + dot(hidden, narrow[...])
    updated[...] = x.astype(BF16).reshape(block, depth, width)
    outer = layer_norm(x, product_gain[...]).astype(BF16)
    both = dot(outer, twin[...])
    channels = twin.shape[1] // 2
    spread = iota((depth, channels * depth), 1)
    channel = spread // depth
    repeat = one_hot(
        iota((2 * channels, channels * depth), 0) - channels == iota((2 * channels, channels * depth), 1) // depth
    )
    mine = jnp.where(spread - channel * depth == iota((depth, channels * depth), 0), 1.0, 0.0)
    for i in range(block):
        here = slice(i * depth, (i + 1) * depth)
        part = (both[here] * valid[:, i : i + 1]).astype(BF16)
        left[here, :] = part[:, :channels]
        right[i : i + 1, :] = jnp.sum(dot(part, repeat) * mine, axis=0, keepdims=True).astype(BF16)


def column_call(idx, pieces, validity, col_gain, entry, exit_, ff_gain, widen, narrow, product_gain, twin):
    far = len(pieces)
    rows, sub, width = pieces[0].shape
    depth, length = validity.shape
    block = rows
    while block * depth > 320 and block % 2 == 0:
        block //= 2
    channels = twin.shape[1] // 2
    vmem = lambda a: pl.BlockSpec(a.shape, lambda s: (0,) * a.ndim)
    rest = [
        validity,
        col_gain[None, :],
        entry,
        exit_,
        ff_gain[None, :],
        widen,
        narrow,
        product_gain[None, :],
        twin,
    ]
    return pl.pallas_call(
        functools.partial(column_kernel, sub=sub, far=far, rows=rows, block=block, depth=depth, width=width),
        grid=(rows // block,),
        in_specs=[pl.BlockSpec(memory_space=pltpu.SMEM)]
        + [pl.BlockSpec((block, sub, width), lambda s: (s, 0, 0))] * far
        + [vmem(a) for a in rest],
        out_specs=[
            pl.BlockSpec((block, depth, width), lambda s: (s, 0, 0)),
            pl.BlockSpec((block * depth, channels), lambda s: (s, 0)),
            pl.BlockSpec((None, block, channels * depth), lambda s: (s, 0, 0)),
        ],
        out_shape=[
            jax.ShapeDtypeStruct((rows, depth, width), BF16),
            jax.ShapeDtypeStruct((rows * depth, channels), BF16),
            jax.ShapeDtypeStruct((rows // block, block, channels * depth), BF16),
        ],
        scratch_shapes=[pltpu.VMEM((block, depth, width), F32), pltpu.VMEM((block * depth, width), F32)],
        compiler_params=pltpu.CompilerParams(vmem_limit_bytes=VMEM_LIMIT),
        cost_estimate=pl.CostEstimate(flops=10**10, bytes_accessed=4000000, transcendentals=10**6),
        name="column_attention",
    )(idx, *pieces, *rest)


def mix_kernel(left, factors, out, *, rows, depth):
    lanes = factors.shape[2]
    for e in range(factors.shape[0]):
        y = dot(left[...], factors[e]).astype(BF16)
        for i in range(rows):
            out[e * depth : (e + 1) * depth, i * lanes : (i + 1) * lanes] = y[i * depth : (i + 1) * depth]


def mix_call(left, factors, rows):
    total, channels = left.shape
    depth = total // rows
    lanes = factors.shape[2]
    block = 8
    return pl.pallas_call(
        functools.partial(mix_kernel, rows=rows, depth=depth),
        grid=(channels // block,),
        in_specs=[
            pl.BlockSpec((total, channels), lambda s: (0, 0)),
            pl.BlockSpec((block, channels, lanes), lambda s: (s, 0, 0)),
        ],
        out_specs=pl.BlockSpec((block * depth, rows * lanes), lambda s: (s, 0)),
        out_shape=jax.ShapeDtypeStruct((channels * depth, rows * lanes), BF16),
        compiler_params=pltpu.CompilerParams(vmem_limit_bytes=VMEM_LIMIT),
        cost_estimate=pl.CostEstimate(flops=10**9, bytes_accessed=4000000, transcendentals=0),
        name="left_mix",
    )(left, factors)


def finish_kernel(
    idx, near, across, mixed, pair_one, validity, gain, widen, narrow, out, right, turned, *, sub, far, rows, length, block
):
    me = idx[0]
    z, p = me // sub, me % sub
    step = pl.program_id(0)
    half = near.shape[0]
    lanes = pair_one.shape[2]
    part = min(length, 320)

    @pl.when(step == 0)
    def _():
        r = iota((part, half), 1)
        b = div_const(r, rows, half)
        i = r - b * rows
        across_sub, across_far = (b // far) * 2, b % far
        home = ((z ^ across_far) * sub + (p ^ across_sub)) * rows + i
        away = ((z ^ across_far) * sub + (p ^ 1 ^ across_sub)) * rows + i

        def arrange(start):
            j = iota((part, half), 0) + start
            here = pl.ds(start, part)
            right[here, :] = (dot(one_hot(j == home), near[...]) + dot(one_hot(j == away), across[...])).astype(BF16)

        chunks(length, part, arrange)
        turned[...] = validity[...].astype(F32).T.astype(BF16)

    i0 = me * rows + step * block
    target = i0 + iota((length, block * lanes), 1) // lanes
    mine = one_hot(iota((length, block * lanes), 0) == target)
    mine = dot(validity[...].astype(F32).astype(BF16), mine).astype(BF16)

    def finish(start):
        here = pl.ds(start, part)
        counts = dot(turned[here, :], mine) + OUTER_EPS
        update = dot(right[here, :], mixed[...]) / counts
        for r in range(block):
            x = pair_one[r, here, :] + update[:, r * lanes : (r + 1) * lanes]
            normed = layer_norm(x, gain[...]).astype(BF16)
            hidden = jnp.maximum(dot(normed, widen[...]), 0.0).astype(BF16)
            out[r, here, :] = (x + dot(hidden, narrow[...])).astype(BF16)

    chunks(length, part, finish)


def finish_call(idx, near, across, mixed, pair_one, validity, gain, widen, narrow, sub, far):
    rows, length, lanes = pair_one.shape
    depth = validity.shape[0]
    block = 2 if rows % 2 == 0 else 1
    product = mixed.shape[0]
    vmem = lambda a: pl.BlockSpec(a.shape, lambda s: (0,) * a.ndim)
    gain = gain[None, :]
    return pl.pallas_call(
        functools.partial(finish_kernel, sub=sub, far=far, rows=rows, length=length, block=block),
        grid=(rows // block,),
        in_specs=[
            pl.BlockSpec(memory_space=pltpu.SMEM),
            vmem(near),
            vmem(across),
            pl.BlockSpec((product, block * lanes), lambda s: (0, s)),
            pl.BlockSpec((block, length, lanes), lambda s: (s, 0, 0)),
            vmem(validity),
            vmem(gain),
            vmem(widen),
            vmem(narrow),
        ],
        out_specs=pl.BlockSpec((block, length, lanes), lambda s: (s, 0, 0)),
        out_shape=jax.ShapeDtypeStruct((rows, length, lanes), BF16),
        scratch_shapes=[pltpu.VMEM((length, product), BF16), pltpu.VMEM((length, depth), BF16)],
        compiler_params=pltpu.CompilerParams(vmem_limit_bytes=VMEM_LIMIT),
        cost_estimate=pl.CostEstimate(flops=10**10, bytes_accessed=4000000, transcendentals=0),
        name="pair_update",
    )(idx, near, across, mixed, pair_one, validity, gain, widen, narrow)


def on_device(
    devices,
    alignment_embedding,
    couple_embedding,
    amino_strand,
    amino_validity,
    alignment_validity,
    separation_embedding,
    couple_shift_scaling,
    couple_shift_factors,
    horizontal_scaling_factor,
    horizontal_entry_factors,
    horizontal_exit_factors,
    vertical_scaling_factor,
    vertical_entry_factors,
    vertical_exit_factors,
    alignment_feedforward_scaling,
    alignment_widen_factors,
    alignment_narrow_factors,
    product_scaling_factor,
    product_twin_factors,
    product_exit_factors,
    couple_feedforward_scaling,
    couple_widen_factors,
    couple_narrow_factors,
):
    far = devices // SUB
    idx = lax.axis_index("dap").astype(jnp.int32).reshape(1)

    def swap(x, distance):
        return lax.ppermute(x, "dap", [(d, d ^ distance) for d in range(devices)])

    width = alignment_embedding.shape[2]
    rows = couple_embedding.shape[0]
    depth = alignment_validity.shape[0]

    msa_rows = [alignment_embedding] * SUB
    for k in range(2, SUB, 2):
        msa_rows[k] = swap(alignment_embedding, k)
    for k in range(0, SUB, 2):
        msa_rows[k + 1] = swap(msa_rows[k], 1)

    pair_one, bias = pair_call(
        idx, amino_strand, couple_embedding, separation_embedding, couple_shift_scaling, couple_shift_factors
    )
    bias_blocks = [bias] + [swap(bias, SUB * k) for k in range(1, far)]
    sent = row_call(
        idx,
        msa_rows,
        bias_blocks,
        alignment_validity,
        amino_validity,
        horizontal_scaling_factor,
        horizontal_entry_factors.reshape(width, 4 * width),
        horizontal_exit_factors,
    ).reshape(far, rows, SUB, width)
    pieces = [sent[0]] + [swap(sent[k], SUB * k) for k in range(1, far)]
    updated, left, right = column_call(
        idx,
        pieces,
        alignment_validity,
        vertical_scaling_factor,
        vertical_entry_factors.reshape(width, 4 * width),
        vertical_exit_factors,
        alignment_feedforward_scaling,
        alignment_widen_factors,
        alignment_narrow_factors,
        product_scaling_factor,
        product_twin_factors,
    )
    channels = left.shape[1]
    right = right.reshape(rows, channels * depth)
    column = jnp.concatenate([right] + [swap(right, SUB * k) for k in range(1, far)], 0)
    near = jnp.concatenate([column] + [swap(column, k) for k in range(2, SUB, 2)], 0)
    across = swap(near, 1)
    factors = product_exit_factors.reshape(channels, channels, -1).transpose(1, 0, 2)
    mixed = mix_call(left, factors, rows)
    updated_pairs = finish_call(
        idx,
        near,
        across,
        mixed,
        pair_one,
        alignment_validity,
        couple_feedforward_scaling,
        couple_widen_factors,
        couple_narrow_factors,
        SUB,
        far,
    )
    return updated.transpose(1, 0, 2), updated_pairs


def solution(mesh):
    split = P("dap", None, None)
    return jax.shard_map(
        functools.partial(on_device, mesh.shape["dap"]),
        mesh=mesh,
        in_specs=(split, split) + (P(),) * 21,
        out_specs=(P(None, "dap", None), split),
        check_vma=False,
    )
```

```python
import functools

import jax
import jax.numpy as jnp
from jax import lax
from jax.experimental import pallas as pl
from jax.experimental.pallas import tpu as pltpu
from jax.sharding import PartitionSpec as P

HEADS = 8
SUB = 8
EPS = 1e-05
OUTER_EPS = 0.001
MASKED = -1000000000.0
LOG2E = 1.4426950408889634
F32 = jnp.float32
BF16 = jnp.bfloat16
VMEM_LIMIT = 56 * 1024 * 1024


def dot(a, b):
    return jnp.dot(a, b, preferred_element_type=F32)


def dot_nt(a, b):
    return lax.dot_general(a, b, (((1,), (1,)), ((), ())), preferred_element_type=F32)


def dot_tn(a, b):
    return lax.dot_general(a, b, (((0,), (0,)), ((), ())), preferred_element_type=F32)


def layer_norm(x, gain):
    centred = x - jnp.mean(x, -1, keepdims=True)
    spread = jnp.mean(centred * centred, -1, keepdims=True)
    return centred * lax.rsqrt(spread + EPS) * gain


def iota(shape, dim):
    return lax.broadcasted_iota(jnp.int32, shape, dim)


def div_const(x, d, limit):
    m = 65536 // d + 1
    assert all((v * m) >> 16 == v // d for v in range(limit)) and limit * m < 2**31
    return (x * m) >> 16


def one_hot(match):
    return jnp.where(match, 1.0, 0.0).astype(BF16)


def chunks(total, step, body):
    if total == step:
        body(0)
    else:
        lax.fori_loop(0, total // step, lambda c, x: (body(pl.multiple_of(c * step, step)), x)[1], 0)


def pair_kernel(
    idx, chain, pair, chain_row, table, gain, factors, pair_one, bias, shifted, chain_wide, *, rows, length, bins
):
    step = pl.program_id(0)
    reach = (bins - 2) // 2

    @pl.when(step == 0)
    def _():
        k = iota((2 * length, bins), 0)
        wanted = jnp.clip(length - k + reach, 0, 2 * reach)
        pick = jnp.where(wanted == iota((2 * length, bins), 1), 1.0, 0.0)
        shifted[...] = jnp.dot(pick, table[...], precision=lax.Precision.HIGHEST, preferred_element_type=F32)
        eye = iota((length, length), 0) == iota((length, length), 1)
        column = jnp.sum(jnp.where(eye, chain_row[...].astype(F32).reshape(1, length), 0.0), axis=1, keepdims=True)
        chain_wide[...] = jnp.broadcast_to(column, chain_wide.shape)

    other = table[bins - 1 : bins, :]
    block = pair.shape[0]
    for r in range(block):
        i = idx[0] * rows + step * block + r
        near = shifted[pl.ds(length - i, length), :]
        same = chain_wide[...] == chain[i].astype(F32)
        x = pair[r].astype(F32) + jnp.where(same, near, other)
        pair_one[r] = x
        normed = layer_norm(x, gain[...]).astype(BF16)
        bias[r] = dot_nt(factors[...], normed).astype(BF16)


def pair_call(idx, chain, pair, table, gain, factors):
    rows, length, depth = pair.shape
    block = 5 if rows % 5 == 0 else 1
    bins = table.shape[0]
    smem = pl.BlockSpec(memory_space=pltpu.SMEM)
    whole = lambda *shape: pl.BlockSpec(shape, lambda s: (0,) * len(shape))
    return pl.pallas_call(
        functools.partial(pair_kernel, rows=rows, length=length, bins=bins),
        grid=(rows // block,),
        in_specs=[
            smem,
            smem,
            pl.BlockSpec((block, length, depth), lambda s: (s, 0, 0)),
            whole(length),
            whole(bins, depth),
            whole(1, depth),
            whole(HEADS, depth),
        ],
        out_specs=[
            pl.BlockSpec((block, length, depth), lambda s: (s, 0, 0)),
            pl.BlockSpec((block, HEADS, length), lambda s: (s, 0, 0)),
        ],
        out_shape=[
            jax.ShapeDtypeStruct((rows, length, depth), F32),
            jax.ShapeDtypeStruct((rows, HEADS, length), BF16),
        ],
        scratch_shapes=[pltpu.VMEM((2 * length, depth), F32), pltpu.VMEM((length, depth), F32)],
        compiler_params=pltpu.CompilerParams(vmem_limit_bytes=VMEM_LIMIT),
        cost_estimate=pl.CostEstimate(flops=4 * rows * length * depth * HEADS, bytes_accessed=4000000, transcendentals=0),
        name="pair_bias",
    )(idx, chain, pair, chain, table, gain[None, :], factors.T)


def project_kernel(idx, *refs, sub, far, rows, length, width):
    row_refs, refs = refs[:4], refs[4:]
    gain, entry, keys, values, query, gate, own_rows, own_normed = refs
    me = idx[0]
    z, p = me // sub, me % sub
    own = far * rows
    scale = (width // HEADS) ** -0.5 * LOG2E

    r = iota((own, length), 0)
    block = div_const(r, rows, own)
    residue = ((z ^ block) * sub + p) * rows + r - block * rows
    pick = one_hot(residue == iota((own, length), 1))

    step = min(length, 320)
    for k in range(sub):
        source = row_refs[k] if k < 2 else row_refs[2 + k % 2]
        place = 0 if k < 2 else k // 2 - 1

        def project(start, k=k, source=source, place=place):
            x = source[place, pl.ds(start, step), :]
            normed = layer_norm(x.astype(F32), gain[...]).astype(BF16)
            both = dot(normed, entry[:, width : 3 * width])
            keys[k, pl.ds(start, step), :] = both[:, :width].astype(BF16)
            values[k, pl.ds(start, step), :] = both[:, width:].astype(BF16)
            part = pick if length == step else one_hot(residue[:, :step] == iota((own, step), 1) + start)
            q_rows, a_rows = dot(part, normed), dot(part, x)
            here = pl.ds(k * own, own)
            if length == step:
                own_normed[here, :] = q_rows
                own_rows[here, :] = a_rows
            else:
                fresh = start == 0
                own_normed[here, :] = q_rows + jnp.where(fresh, 0.0, own_normed[here, :])
                own_rows[here, :] = a_rows + jnp.where(fresh, 0.0, own_rows[here, :])

        chunks(length, step, project)

    total = sub * own
    part = min(total, 320)

    def queries(start):
        here = pl.ds(start, part)
        normed = own_normed[here, :].astype(BF16)
        query[here, :] = dot(normed, entry[:, :width]) * scale
        gate[here, :] = jax.nn.sigmoid(dot(normed, entry[:, 3 * width :]))

    chunks(total, part, queries)


def project_call(idx, msa_rows, gain, entry, far, rows):
    sub = SUB
    _, length, width = msa_rows[0].shape
    own = far * rows
    vmem = pl.BlockSpec(memory_space=pltpu.VMEM)
    wide = jax.ShapeDtypeStruct((sub, length, width), BF16)
    narrow = jax.ShapeDtypeStruct((sub * own, width), F32)
    return pl.pallas_call(
        functools.partial(project_kernel, sub=sub, far=far, rows=rows, length=length, width=width),
        in_specs=[pl.BlockSpec(memory_space=pltpu.SMEM)] + [vmem] * 6,
        out_specs=[vmem] * 5,
        out_shape=[wide, wide, narrow, narrow, narrow],
        scratch_shapes=[pltpu.VMEM((sub * own, width), F32)],
        compiler_params=pltpu.CompilerParams(vmem_limit_bytes=VMEM_LIMIT),
        cost_estimate=pl.CostEstimate(flops=10**9, bytes_accessed=4000000, transcendentals=10**5),
        name="row_project",
    )(idx, *msa_rows, gain[None, :], entry)


def row_kernel(idx, *refs, sub, far, rows, length, width):
    bias_refs, refs = refs[:far], refs[far:]
    keys, values, query, gate, own_rows, validity, amino, exit_ = refs[:8]
    outs, refs = refs[8 : 8 + far], refs[8 + far :]
    bias, gated = refs
    me = idx[0]
    z, p = me // sub, me % sub
    own = far * rows
    total = sub * own
    for b in range(far):
        bias[b * rows : (b + 1) * rows] = bias_refs[b][...].astype(F32) * LOG2E

    head_of = iota((HEADS, width), 1) // (width // HEADS)
    head_mask = jnp.where(head_of == iota((HEADS, width), 0), 1.0, 0.0)
    take = 40 if own % 40 == 0 else rows

    def attend(n, k, start):
        s = z * sub + (p ^ k)
        valid = validity[pl.ds(s, 1), :] * amino[...].reshape(1, length)
        masked = jnp.where(valid > 0, 0.0, MASKED)
        here = pl.ds(pl.multiple_of(n * take, take), take) if not isinstance(n, int) else pl.ds(n * take, take)
        q = (query[here, :][:, None, :] * head_mask[None]).reshape(take * HEADS, width).astype(BF16)
        scores = dot_nt(q, keys[k]) + bias[pl.ds(start, take)].reshape(take * HEADS, length) + masked
        expo = jnp.exp2(scores - jnp.max(scores, -1, keepdims=True))
        total_ = jnp.sum(expo, -1, keepdims=True)
        mixed = dot(expo.astype(BF16), values[k]) / total_
        merged = jnp.sum(mixed.reshape(take, HEADS, width) * head_mask[None], axis=1)
        gated[here, :] = merged * gate[here, :]

    parts = own // take
    if parts == 1:
        for k in range(sub):
            attend(k, k, 0)
    else:
        lax.fori_loop(0, sub * parts, lambda n, x: (attend(n, n // parts, (n % parts) * take), x)[1], 0)

    piece = rows * sub
    for b in range(far):
        q = iota((piece, total), 0) + b * piece
        residue_, row = div_const(q, sub, total), q & (sub - 1)
        swap = one_hot((row ^ p) * own + residue_ == iota((piece, total), 1))
        gated_rows = dot(swap, gated[...].astype(BF16)).astype(BF16)
        x = dot(swap, own_rows[...].astype(BF16)) + dot(gated_rows, exit_[...])
        outs[b][...] = x.astype(BF16).reshape(rows, sub, width)


def row_call(idx, bias_blocks, projected, validity, amino, exit_):
    keys, values, query, gate, own_rows = projected
    sub, far = keys.shape[0], len(bias_blocks)
    _, length, width = keys.shape
    rows = bias_blocks[0].shape[0]
    own = far * rows
    vmem = pl.BlockSpec(memory_space=pltpu.VMEM)
    return pl.pallas_call(
        functools.partial(row_kernel, sub=sub, far=far, rows=rows, length=length, width=width),
        in_specs=[pl.BlockSpec(memory_space=pltpu.SMEM)] + [vmem] * (far + 8),
        out_specs=[vmem] * far,
        out_shape=[jax.ShapeDtypeStruct((rows, sub, width), BF16)] * far,
        scratch_shapes=[
            pltpu.VMEM((own, HEADS, length), F32),
            pltpu.VMEM((sub * own, width), F32),
        ],
        compiler_params=pltpu.CompilerParams(vmem_limit_bytes=VMEM_LIMIT),
        cost_estimate=pl.CostEstimate(flops=10**10, bytes_accessed=4000000, transcendentals=10**6),
        name="row_attention",
    )(idx, *bias_blocks, keys, values, query, gate, own_rows, validity, amino, exit_)


def column_kernel(idx, *refs, sub, far, rows, block, depth, width):
    piece_refs, refs = refs[:far], refs[far:]
    (
        validity,
        col_gain,
        entry,
        exit_,
        ff_gain,
        widen,
        narrow,
        product_gain,
        twin,
        updated,
        left,
        right,
        start_rows,
        gated,
    ) = refs
    me = idx[0]
    z = me // sub
    first = me * rows + pl.program_id(0) * block
    scale = (width // HEADS) ** -0.5 * LOG2E
    total = block * depth
    for b in range(far):
        here = pl.ds(pl.multiple_of((z ^ b) * sub, sub), sub)
        start_rows[:, here, :] = piece_refs[b][...].astype(F32)
    x = start_rows[...].reshape(total, width)
    normed = layer_norm(x, col_gain[...]).astype(BF16)
    proj = dot(normed, entry[...])
    query = proj[:, :width] * scale
    keys = proj[:, width : 2 * width].astype(BF16)
    values = proj[:, 2 * width : 3 * width].astype(BF16)
    gate = jax.nn.sigmoid(proj[:, 3 * width :])

    length = validity.shape[1]
    lanes = 128
    pick = one_hot(iota((length, lanes), 0) == first + iota((length, lanes), 1))
    valid = dot(validity[...].astype(F32).astype(BF16), pick)
    head_of = iota((HEADS, width), 1) // (width // HEADS)
    head_mask = jnp.where(head_of == iota((HEADS, width), 0), 1.0, 0.0)
    for i in range(block):
        here = slice(i * depth, (i + 1) * depth)
        q = (query[here][:, None, :] * head_mask[None]).reshape(depth * HEADS, width).astype(BF16)
        masked = jnp.where(valid[:, i : i + 1] > 0, 0.0, MASKED)
        scores = dot_nt(keys[here], q) + masked
        expo = jnp.exp2(scores - jnp.max(scores, 0, keepdims=True))
        weights = (expo / jnp.sum(expo, 0, keepdims=True)).astype(BF16)
        mixed = dot_tn(weights, values[here])
        merged = jnp.sum(mixed.reshape(depth, HEADS, width) * head_mask[None], axis=1)
        gated[here, :] = merged * gate[here]
    x = x + dot(gated[...].astype(BF16), exit_[...])
    hidden = jnp.maximum(dot(layer_norm(x, ff_gain[...]).astype(BF16), widen[...]), 0.0).astype(BF16)
    x = x + dot(hidden, narrow[...])
    updated[...] = x.astype(BF16).reshape(block, depth, width)
    outer = layer_norm(x, product_gain[...]).astype(BF16)
    both = dot(outer, twin[...])
    channels = twin.shape[1] // 2
    spread = iota((depth, channels * depth), 1)
    channel = spread // depth
    repeat = one_hot(
        iota((2 * channels, channels * depth), 0) - channels == iota((2 * channels, channels * depth), 1) // depth
    )
    mine = jnp.where(spread - channel * depth == iota((depth, channels * depth), 0), 1.0, 0.0)
    for i in range(block):
        here = slice(i * depth, (i + 1) * depth)
        part = (both[here] * valid[:, i : i + 1]).astype(BF16)
        left[here, :] = part[:, :channels]
        right[i : i + 1, :] = jnp.sum(dot(part, repeat) * mine, axis=0, keepdims=True).astype(BF16)


def column_call(idx, pieces, validity, col_gain, entry, exit_, ff_gain, widen, narrow, product_gain, twin):
    far = len(pieces)
    rows, sub, width = pieces[0].shape
    depth, length = validity.shape
    block = rows
    while block * depth > 320 and block % 2 == 0:
        block //= 2
    channels = twin.shape[1] // 2
    vmem = lambda a: pl.BlockSpec(a.shape, lambda s: (0,) * a.ndim)
    rest = [
        validity,
        col_gain[None, :],
        entry,
        exit_,
        ff_gain[None, :],
        widen,
        narrow,
        product_gain[None, :],
        twin,
    ]
    return pl.pallas_call(
        functools.partial(column_kernel, sub=sub, far=far, rows=rows, block=block, depth=depth, width=width),
        grid=(rows // block,),
        in_specs=[pl.BlockSpec(memory_space=pltpu.SMEM)]
        + [pl.BlockSpec((block, sub, width), lambda s: (s, 0, 0))] * far
        + [vmem(a) for a in rest],
        out_specs=[
            pl.BlockSpec((block, depth, width), lambda s: (s, 0, 0)),
            pl.BlockSpec((block * depth, channels), lambda s: (s, 0)),
            pl.BlockSpec((None, block, channels * depth), lambda s: (s, 0, 0)),
        ],
        out_shape=[
            jax.ShapeDtypeStruct((rows, depth, width), BF16),
            jax.ShapeDtypeStruct((rows * depth, channels), BF16),
            jax.ShapeDtypeStruct((rows // block, block, channels * depth), BF16),
        ],
        scratch_shapes=[pltpu.VMEM((block, depth, width), F32), pltpu.VMEM((block * depth, width), F32)],
        compiler_params=pltpu.CompilerParams(vmem_limit_bytes=VMEM_LIMIT),
        cost_estimate=pl.CostEstimate(flops=10**10, bytes_accessed=4000000, transcendentals=10**6),
        name="column_attention",
    )(idx, *pieces, *rest)


def mix_kernel(left, factors, out, *, rows, depth):
    lanes = out.shape[1] // rows
    for e in range(0, out.shape[0] // depth, 2):
        y = dot(left[...], factors[:, e * lanes : (e + 2) * lanes]).astype(BF16)
        for i in range(rows):
            for f in range(2):
                block = y[i * depth : (i + 1) * depth, f * lanes : (f + 1) * lanes]
                out[(e + f) * depth : (e + f + 1) * depth, i * lanes : (i + 1) * lanes] = block


def mix_call(left, factors, rows):
    total, channels = left.shape
    depth = total // rows
    lanes = factors.shape[1] // channels
    block = 8
    return pl.pallas_call(
        functools.partial(mix_kernel, rows=rows, depth=depth),
        grid=(channels // block,),
        in_specs=[
            pl.BlockSpec((total, channels), lambda s: (0, 0)),
            pl.BlockSpec((channels, block * lanes), lambda s: (0, s)),
        ],
        out_specs=pl.BlockSpec((block * depth, rows * lanes), lambda s: (s, 0)),
        out_shape=jax.ShapeDtypeStruct((channels * depth, rows * lanes), BF16),
        compiler_params=pltpu.CompilerParams(vmem_limit_bytes=VMEM_LIMIT),
        cost_estimate=pl.CostEstimate(flops=10**9, bytes_accessed=4000000, transcendentals=0),
        name="left_mix",
    )(left, factors)


def finish_kernel(
    idx, *refs, sub, far, rows, length, block
):
    near_refs, across_refs, refs = refs[: sub // 2], refs[sub // 2 : sub], refs[sub:]
    mixed, pair_one, validity, gain, widen, narrow, out, right, turned = refs
    me = idx[0]
    z, p = me // sub, me % sub
    step = pl.program_id(0)
    half = far * rows * sub // 2
    lanes = pair_one.shape[2]
    part = min(length, 320)

    @pl.when(step == 0)
    def _():
        r = iota((part, half), 1)
        b = div_const(r, rows, half)
        i = r - b * rows
        across_sub = 2 * div_const(b, far, half // rows)
        across_far = b - far * (across_sub >> 1)
        home = ((z ^ across_far) * sub + (p ^ across_sub)) * rows + i
        away = ((z ^ across_far) * sub + (p ^ 1 ^ across_sub)) * rows + i

        near = jnp.concatenate([ref[...].astype(F32) for ref in near_refs], 0).astype(BF16)
        across = jnp.concatenate([ref[...].astype(F32) for ref in across_refs], 0).astype(BF16)

        def arrange(start):
            j = iota((part, half), 0) + start
            here = pl.ds(start, part)
            right[here, :] = (dot(one_hot(j == home), near) + dot(one_hot(j == away), across)).astype(BF16)

        chunks(length, part, arrange)
        turned[...] = validity[...].astype(F32).T.astype(BF16)

    i0 = me * rows + step * block
    target = i0 + iota((length, block * lanes), 1) // lanes
    mine = one_hot(iota((length, block * lanes), 0) == target)
    mine = dot(validity[...].astype(F32).astype(BF16), mine).astype(BF16)

    def finish(start):
        here = pl.ds(start, part)
        counts = dot(turned[here, :], mine) + OUTER_EPS
        update = dot(right[here, :], mixed[...]) / counts
        for r in range(block):
            x = pair_one[r, here, :] + update[:, r * lanes : (r + 1) * lanes]
            normed = layer_norm(x, gain[...]).astype(BF16)
            hidden = jnp.maximum(dot(normed, widen[...]), 0.0).astype(BF16)
            out[r, here, :] = (x + dot(hidden, narrow[...])).astype(BF16)

    chunks(length, part, finish)


def finish_call(idx, near, across, mixed, pair_one, validity, gain, widen, narrow, sub, far):
    rows, length, lanes = pair_one.shape
    depth = validity.shape[0]
    block = 2 if rows % 2 == 0 else 1
    product = mixed.shape[0]
    vmem = lambda a: pl.BlockSpec(a.shape, lambda s: (0,) * a.ndim)
    gain = gain[None, :]
    return pl.pallas_call(
        functools.partial(finish_kernel, sub=sub, far=far, rows=rows, length=length, block=block),
        grid=(rows // block,),
        in_specs=[
            pl.BlockSpec(memory_space=pltpu.SMEM),
            *[vmem(a) for a in near + across],
            pl.BlockSpec((product, block * lanes), lambda s: (0, s)),
            pl.BlockSpec((block, length, lanes), lambda s: (s, 0, 0)),
            vmem(validity),
            vmem(gain),
            vmem(widen),
            vmem(narrow),
        ],
        out_specs=pl.BlockSpec((block, length, lanes), lambda s: (s, 0, 0)),
        out_shape=jax.ShapeDtypeStruct((rows, length, lanes), BF16),
        scratch_shapes=[pltpu.VMEM((length, product), BF16), pltpu.VMEM((length, depth), BF16)],
        compiler_params=pltpu.CompilerParams(vmem_limit_bytes=VMEM_LIMIT),
        cost_estimate=pl.CostEstimate(flops=10**10, bytes_accessed=4000000, transcendentals=0),
        name="pair_update",
    )(idx, *near, *across, mixed, pair_one, validity, gain, widen, narrow)


def on_device(
    devices,
    alignment_embedding,
    couple_embedding,
    amino_strand,
    amino_validity,
    alignment_validity,
    separation_embedding,
    couple_shift_scaling,
    couple_shift_factors,
    horizontal_scaling_factor,
    horizontal_entry_factors,
    horizontal_exit_factors,
    vertical_scaling_factor,
    vertical_entry_factors,
    vertical_exit_factors,
    alignment_feedforward_scaling,
    alignment_widen_factors,
    alignment_narrow_factors,
    product_scaling_factor,
    product_twin_factors,
    product_exit_factors,
    couple_feedforward_scaling,
    couple_widen_factors,
    couple_narrow_factors,
):
    far = devices // SUB
    idx = lax.axis_index("dap").astype(jnp.int32).reshape(1)

    def swap(x, distance):
        return lax.ppermute(x, "dap", [(d, d ^ distance) for d in range(devices)])

    width = alignment_embedding.shape[2]
    rows = couple_embedding.shape[0]
    depth = alignment_validity.shape[0]

    beside = swap(alignment_embedding, 1)
    near = [swap(alignment_embedding, k) for k in range(2, SUB, 2)]
    pair_one, bias = pair_call(
        idx, amino_strand, couple_embedding, separation_embedding, couple_shift_scaling, couple_shift_factors
    )
    entry = horizontal_entry_factors.reshape(width, 4 * width)
    bias, entry, beside, *near = lax.optimization_barrier((bias, entry, beside, *near))
    bias_blocks = [bias] + [swap(bias, SUB * k) for k in range(1, far)]
    near = jnp.concatenate(near, 0)
    across = swap(near, 1)
    projected = project_call(
        idx, [alignment_embedding, beside, near, across], horizontal_scaling_factor, entry, far, rows
    )
    sent = row_call(idx, bias_blocks, projected, alignment_validity, amino_validity, horizontal_exit_factors)
    pieces = [sent[0]] + [swap(sent[k], SUB * k) for k in range(1, far)]
    updated, left, right = column_call(
        idx,
        pieces,
        alignment_validity,
        vertical_scaling_factor,
        vertical_entry_factors.reshape(width, 4 * width),
        vertical_exit_factors,
        alignment_feedforward_scaling,
        alignment_widen_factors,
        alignment_narrow_factors,
        product_scaling_factor,
        product_twin_factors,
    )
    channels = left.shape[1]
    right = right.reshape(rows, channels * depth)
    factors = product_exit_factors.reshape(channels, -1)
    mixed = mix_call(left, factors, rows)
    parts = [right] + [swap(right, SUB * k) for k in range(1, far)]
    parts = lax.optimization_barrier((mixed, *parts))
    mixed, parts = parts[0], parts[1:]
    column = jnp.concatenate(parts, 0)
    near = [column] + [swap(column, k) for k in range(2, SUB, 2)]
    across = [swap(a, 1) for a in near]
    updated_pairs = finish_call(
        idx,
        near,
        across,
        mixed,
        pair_one,
        alignment_validity,
        couple_feedforward_scaling,
        couple_widen_factors,
        couple_narrow_factors,
        SUB,
        far,
    )
    return updated.transpose(1, 0, 2), updated_pairs


def solution(mesh):
    split = P("dap", None, None)
    return jax.shard_map(
        functools.partial(on_device, mesh.shape["dap"]),
        mesh=mesh,
        in_specs=(split, split) + (P(),) * 21,
        out_specs=(P(None, "dap", None), split),
        check_vma=False,
    )
```

```python
import functools

import jax
import jax.numpy as jnp
from jax import lax
from jax.experimental import pallas as pl
from jax.experimental.pallas import tpu as pltpu
from jax.sharding import PartitionSpec as P

HEADS = 8
SUB = 8
EPS = 1e-05
OUTER_EPS = 0.001
MASKED = -1000000000.0
LOG2E = 1.4426950408889634
F32 = jnp.float32
BF16 = jnp.bfloat16


def vmem_limit(length):
    return (16 if length is not None and length <= 320 else 56) * 1024 * 1024


def dot(a, b):
    return jnp.dot(a, b, preferred_element_type=F32)


def dot_nt(a, b):
    return lax.dot_general(a, b, (((1,), (1,)), ((), ())), preferred_element_type=F32)


def dot_tn(a, b):
    return lax.dot_general(a, b, (((0,), (0,)), ((), ())), preferred_element_type=F32)


def layer_norm(x, gain):
    centred = x - jnp.mean(x, -1, keepdims=True)
    spread = jnp.mean(centred * centred, -1, keepdims=True)
    return centred * lax.rsqrt(spread + EPS) * gain


def iota(shape, dim):
    return lax.broadcasted_iota(jnp.int32, shape, dim)


def div_const(x, d, limit):
    m = 65536 // d + 1
    assert all((v * m) >> 16 == v // d for v in range(limit)) and limit * m < 2**31
    return (x * m) >> 16


def one_hot(match):
    return jnp.where(match, 1.0, 0.0).astype(BF16)


def chunks(total, step, body):
    if total == step:
        body(0)
    else:
        lax.fori_loop(0, total // step, lambda c, x: (body(pl.multiple_of(c * step, step)), x)[1], 0)


def pair_kernel(
    idx, chain, pair, chain_row, table, gain, factors, pair_one, bias, shifted, chain_wide, *, rows, length, bins
):
    step = pl.program_id(0)
    reach = (bins - 2) // 2

    @pl.when(step == 0)
    def _():
        k = iota((2 * length, bins), 0)
        wanted = jnp.clip(length - k + reach, 0, 2 * reach)
        pick = jnp.where(wanted == iota((2 * length, bins), 1), 1.0, 0.0)
        shifted[...] = jnp.dot(pick, table[...], precision=lax.Precision.HIGHEST, preferred_element_type=F32)
        eye = iota((length, length), 0) == iota((length, length), 1)
        column = jnp.sum(jnp.where(eye, chain_row[...].astype(F32).reshape(1, length), 0.0), axis=1, keepdims=True)
        chain_wide[...] = jnp.broadcast_to(column, chain_wide.shape)

    other = table[bins - 1 : bins, :]
    block = pair.shape[0]
    for r in range(block):
        i = idx[0] * rows + step * block + r
        near = shifted[pl.ds(length - i, length), :]
        same = chain_wide[...] == chain[i].astype(F32)
        x = pair[r].astype(F32) + jnp.where(same, near, other)
        pair_one[r] = x
        normed = layer_norm(x, gain[...]).astype(BF16)
        bias[r] = dot_nt(factors[...], normed).astype(BF16)


def pair_call(idx, chain, pair, table, gain, factors):
    rows, length, depth = pair.shape
    block = 5 if rows % 5 == 0 else 1
    bins = table.shape[0]
    smem = pl.BlockSpec(memory_space=pltpu.SMEM)
    whole = lambda *shape: pl.BlockSpec(shape, lambda s: (0,) * len(shape))
    return pl.pallas_call(
        functools.partial(pair_kernel, rows=rows, length=length, bins=bins),
        grid=(rows // block,),
        in_specs=[
            smem,
            smem,
            pl.BlockSpec((block, length, depth), lambda s: (s, 0, 0)),
            whole(length),
            whole(bins, depth),
            whole(1, depth),
            whole(HEADS, depth),
        ],
        out_specs=[
            pl.BlockSpec((block, length, depth), lambda s: (s, 0, 0)),
            pl.BlockSpec((block, HEADS, length), lambda s: (s, 0, 0)),
        ],
        out_shape=[
            jax.ShapeDtypeStruct((rows, length, depth), F32),
            jax.ShapeDtypeStruct((rows, HEADS, length), BF16),
        ],
        scratch_shapes=[pltpu.VMEM((2 * length, depth), F32), pltpu.VMEM((length, depth), F32)],
        compiler_params=pltpu.CompilerParams(vmem_limit_bytes=vmem_limit(None)),
        cost_estimate=pl.CostEstimate(flops=4 * 10**9, bytes_accessed=4000000, transcendentals=10**5),
        name="pair_bias",
    )(idx, chain, pair, chain, table, gain[None, :], factors.T)


def project_kernel(idx, *refs, sub, far, rows, length, width):
    row_refs, refs = refs[:4], refs[4:]
    gain, entry, keys, values, query, gate, own_rows, own_normed = refs
    me = idx[0]
    z, p = me // sub, me % sub
    own = far * rows
    scale = (width // HEADS) ** -0.5 * LOG2E

    r = iota((own, length), 0)
    block = div_const(r, rows, own)
    residue = ((z ^ block) * sub + p) * rows + r - block * rows
    pick = one_hot(residue == iota((own, length), 1))

    step = min(length, 320)
    for k in range(sub):
        source = row_refs[k] if k < 2 else row_refs[2 + k % 2]
        place = 0 if k < 2 else k // 2 - 1

        def project(start, k=k, source=source, place=place):
            x = source[place, pl.ds(start, step), :]
            normed = layer_norm(x.astype(F32), gain[...]).astype(BF16)
            both = dot(normed, entry[:, width : 3 * width])
            keys[k, pl.ds(start, step), :] = both[:, :width].astype(BF16)
            values[k, pl.ds(start, step), :] = both[:, width:].astype(BF16)
            part = pick if length == step else one_hot(residue[:, :step] == iota((own, step), 1) + start)
            q_rows, a_rows = dot(part, normed), dot(part, x)
            here = pl.ds(k * own, own)
            if length == step:
                own_normed[here, :] = q_rows
                own_rows[here, :] = a_rows
            else:
                fresh = start == 0
                own_normed[here, :] = q_rows + jnp.where(fresh, 0.0, own_normed[here, :])
                own_rows[here, :] = a_rows + jnp.where(fresh, 0.0, own_rows[here, :])

        chunks(length, step, project)

    total = sub * own
    part = min(total, 320)

    def queries(start):
        here = pl.ds(start, part)
        normed = own_normed[here, :].astype(BF16)
        query[here, :] = dot(normed, entry[:, :width]) * scale
        gate[here, :] = jax.nn.sigmoid(dot(normed, entry[:, 3 * width :]))

    chunks(total, part, queries)


def project_call(idx, msa_rows, gain, entry, far, rows):
    sub = SUB
    _, length, width = msa_rows[0].shape
    own = far * rows
    vmem = pl.BlockSpec(memory_space=pltpu.VMEM)
    wide = jax.ShapeDtypeStruct((sub, length, width), BF16)
    narrow = jax.ShapeDtypeStruct((sub * own, width), F32)
    return pl.pallas_call(
        functools.partial(project_kernel, sub=sub, far=far, rows=rows, length=length, width=width),
        in_specs=[pl.BlockSpec(memory_space=pltpu.SMEM)] + [vmem] * 6,
        out_specs=[vmem] * 5,
        out_shape=[wide, wide, narrow, narrow, narrow],
        scratch_shapes=[pltpu.VMEM((sub * own, width), F32)],
        compiler_params=pltpu.CompilerParams(vmem_limit_bytes=vmem_limit(length)),
        cost_estimate=pl.CostEstimate(flops=3 * 10**9, bytes_accessed=4000000, transcendentals=10**5),
        name="row_project",
    )(idx, *msa_rows, gain[None, :], entry)


def row_kernel(idx, *refs, sub, far, rows, length, width):
    bias_refs, refs = refs[:far], refs[far:]
    keys, values, query, gate, own_rows, validity, amino, exit_ = refs[:8]
    outs, refs = refs[8 : 8 + far], refs[8 + far :]
    bias, gated = refs
    me = idx[0]
    z, p = me // sub, me % sub
    own = far * rows
    total = sub * own
    for b in range(far):
        bias[b * rows : (b + 1) * rows] = bias_refs[b][...].astype(F32) * LOG2E

    head_of = iota((HEADS, width), 1) // (width // HEADS)
    head_mask = jnp.where(head_of == iota((HEADS, width), 0), 1.0, 0.0)
    take = 40 if own % 40 == 0 else rows

    def attend(n, k, start):
        s = z * sub + (p ^ k)
        valid = validity[pl.ds(s, 1), :] * amino[...].reshape(1, length)
        masked = jnp.where(valid > 0, 0.0, MASKED)
        here = pl.ds(pl.multiple_of(n * take, take), take) if not isinstance(n, int) else pl.ds(n * take, take)
        q = (query[here, :][:, None, :] * head_mask[None]).reshape(take * HEADS, width).astype(BF16)
        scores = dot_nt(q, keys[k]) + bias[pl.ds(start, take)].reshape(take * HEADS, length) + masked
        expo = jnp.exp2(scores - jnp.max(scores, -1, keepdims=True))
        total_ = jnp.sum(expo, -1, keepdims=True)
        mixed = dot(expo.astype(BF16), values[k]) / total_
        merged = jnp.sum(mixed.reshape(take, HEADS, width) * head_mask[None], axis=1)
        gated[here, :] = merged * gate[here, :]

    parts = own // take
    if parts == 1:
        for k in range(sub):
            attend(k, k, 0)
    else:
        lax.fori_loop(0, sub * parts, lambda n, x: (attend(n, n // parts, (n % parts) * take), x)[1], 0)

    piece = rows * sub
    for b in range(far):
        q = iota((piece, total), 0) + b * piece
        residue_, row = div_const(q, sub, total), q & (sub - 1)
        swap = one_hot((row ^ p) * own + residue_ == iota((piece, total), 1))
        gated_rows = dot(swap, gated[...].astype(BF16)).astype(BF16)
        x = dot(swap, own_rows[...].astype(BF16)) + dot(gated_rows, exit_[...])
        outs[b][...] = x.astype(BF16).reshape(rows, sub, width)


def row_call(idx, bias_blocks, projected, validity, amino, exit_):
    keys, values, query, gate, own_rows = projected
    sub, far = keys.shape[0], len(bias_blocks)
    _, length, width = keys.shape
    rows = bias_blocks[0].shape[0]
    own = far * rows
    vmem = pl.BlockSpec(memory_space=pltpu.VMEM)
    return pl.pallas_call(
        functools.partial(row_kernel, sub=sub, far=far, rows=rows, length=length, width=width),
        in_specs=[pl.BlockSpec(memory_space=pltpu.SMEM)] + [vmem] * (far + 8),
        out_specs=[vmem] * far,
        out_shape=[jax.ShapeDtypeStruct((rows, sub, width), BF16)] * far,
        scratch_shapes=[
            pltpu.VMEM((own, HEADS, length), F32),
            pltpu.VMEM((sub * own, width), F32),
        ],
        compiler_params=pltpu.CompilerParams(vmem_limit_bytes=vmem_limit(length)),
        cost_estimate=pl.CostEstimate(flops=4 * 10**9, bytes_accessed=4000000, transcendentals=10**5),
        name="row_attention",
    )(idx, *bias_blocks, keys, values, query, gate, own_rows, validity, amino, exit_)


def column_kernel(idx, *refs, sub, far, rows, block, depth, width):
    piece_refs, refs = refs[:far], refs[far:]
    entry, twin, *sources = refs[:9]
    updated, left, right, start_rows, gated, *held = refs[9:-1]
    sems = refs[-1]
    copies = [pltpu.make_async_copy(src, dst, sems.at[n]) for n, (src, dst) in enumerate(zip(sources, held))]
    steps = rows // block

    def begin():
        for copy in copies:
            copy.start()

    def arrived(*which):
        def wait():
            for n in which:
                copies[n].wait()

        if steps == 1:
            wait()
        else:
            pl.when(pl.program_id(0) == 0)(wait)
        return [held[n][...] for n in which]

    if steps == 1:
        begin()
    else:
        pl.when(pl.program_id(0) == 0)(begin)
    me = idx[0]
    z = me // sub
    first = me * rows + (0 if steps == 1 else pl.program_id(0) * block)
    scale = (width // HEADS) ** -0.5 * LOG2E
    total = block * depth
    for b in range(far):
        here = pl.ds(pl.multiple_of((z ^ b) * sub, sub), sub)
        start_rows[:, here, :] = piece_refs[b][...].astype(F32)
    x = start_rows[...].reshape(total, width)
    (col_gain,) = arrived(0)
    normed = layer_norm(x, col_gain).astype(BF16)
    proj = dot(normed, entry[...])
    query = proj[:, :width] * scale
    keys = proj[:, width : 2 * width].astype(BF16)
    values = proj[:, 2 * width : 3 * width].astype(BF16)
    gate = jax.nn.sigmoid(proj[:, 3 * width :])

    (validity,) = arrived(1)
    length = validity.shape[1]
    lanes = 128
    pick = one_hot(iota((length, lanes), 0) == first + iota((length, lanes), 1))
    valid = dot(validity.astype(F32).astype(BF16), pick)
    head_of = iota((HEADS, width), 1) // (width // HEADS)
    head_mask = jnp.where(head_of == iota((HEADS, width), 0), 1.0, 0.0)
    for i in range(block):
        here = slice(i * depth, (i + 1) * depth)
        q = (query[here][:, None, :] * head_mask[None]).reshape(depth * HEADS, width).astype(BF16)
        masked = jnp.where(valid[:, i : i + 1] > 0, 0.0, MASKED)
        scores = dot_nt(keys[here], q) + masked
        expo = jnp.exp2(scores - jnp.max(scores, 0, keepdims=True))
        weights = (expo / jnp.sum(expo, 0, keepdims=True)).astype(BF16)
        mixed = dot_tn(weights, values[here])
        merged = jnp.sum(mixed.reshape(depth, HEADS, width) * head_mask[None], axis=1)
        gated[here, :] = merged * gate[here]
    exit_, ff_gain, widen, narrow, product_gain = arrived(2, 3, 4, 5, 6)
    x = x + dot(gated[...].astype(BF16), exit_)
    hidden = jnp.maximum(dot(layer_norm(x, ff_gain).astype(BF16), widen), 0.0).astype(BF16)
    x = x + dot(hidden, narrow)
    updated[...] = x.astype(BF16).reshape(block, depth, width)
    outer = layer_norm(x, product_gain).astype(BF16)
    both = dot(outer, twin[...])
    channels = twin.shape[1] // 2
    spread = iota((depth, channels * depth), 1)
    channel = spread // depth
    repeat = one_hot(
        iota((2 * channels, channels * depth), 0) - channels == iota((2 * channels, channels * depth), 1) // depth
    )
    mine = jnp.where(spread - channel * depth == iota((depth, channels * depth), 0), 1.0, 0.0)
    for i in range(block):
        here = slice(i * depth, (i + 1) * depth)
        part = (both[here] * valid[:, i : i + 1]).astype(BF16)
        left[here, :] = part[:, :channels]
        right[0, i : i + 1, :] = jnp.sum(dot(part, repeat) * mine, axis=0, keepdims=True).astype(BF16)


def column_call(idx, pieces, validity, col_gain, entry, exit_, ff_gain, widen, narrow, product_gain, twin):
    far = len(pieces)
    rows, sub, width = pieces[0].shape
    depth, length = validity.shape
    block = rows
    while block * depth > 320 and block % 2 == 0:
        block //= 2
    channels = twin.shape[1] // 2
    steps = rows // block
    here = [entry, twin]
    sources = [
        col_gain[None, :],
        validity,
        exit_,
        ff_gain[None, :],
        widen,
        narrow,
        product_gain[None, :],
    ]
    if steps == 1:
        grid, spec = {}, lambda shape, index: pl.BlockSpec(memory_space=pltpu.VMEM)
    else:
        grid, spec = {"grid": (steps,)}, pl.BlockSpec
    return pl.pallas_call(
        functools.partial(column_kernel, sub=sub, far=far, rows=rows, block=block, depth=depth, width=width),
        **grid,
        in_specs=[pl.BlockSpec(memory_space=pltpu.SMEM)]
        + [spec((block, sub, width), lambda s: (s, 0, 0))] * far
        + [spec(a.shape, lambda s: (0, 0)) for a in here]
        + [pl.BlockSpec(memory_space=pltpu.HBM)] * len(sources),
        out_specs=[
            spec((block, depth, width), lambda s: (s, 0, 0)),
            spec((block * depth, channels), lambda s: (s, 0)),
            spec((1, block, channels * depth), lambda s: (s, 0, 0)),
        ],
        out_shape=[
            jax.ShapeDtypeStruct((rows, depth, width), BF16),
            jax.ShapeDtypeStruct((rows * depth, channels), BF16),
            jax.ShapeDtypeStruct((steps, block, channels * depth), BF16),
        ],
        scratch_shapes=[pltpu.VMEM((block, depth, width), F32), pltpu.VMEM((block * depth, width), F32)]
        + [pltpu.VMEM(a.shape, a.dtype) for a in sources]
        + [pltpu.SemaphoreType.DMA((len(sources),))],
        compiler_params=pltpu.CompilerParams(vmem_limit_bytes=vmem_limit(length)),
        cost_estimate=pl.CostEstimate(flops=5 * 10**9, bytes_accessed=4000000, transcendentals=10**5),
        name="column_attention",
    )(idx, *pieces, *here, *sources)


def mix_kernel(left, factors, out, *, rows, depth):
    lanes = out.shape[1] // rows
    for e in range(0, out.shape[0] // depth, 2):
        y = dot(left[...], factors[:, e * lanes : (e + 2) * lanes]).astype(BF16)
        for i in range(rows):
            for f in range(2):
                block = y[i * depth : (i + 1) * depth, f * lanes : (f + 1) * lanes]
                out[(e + f) * depth : (e + f + 1) * depth, i * lanes : (i + 1) * lanes] = block


def mix_call(left, factors, rows, length):
    total, channels = left.shape
    depth = total // rows
    lanes = factors.shape[1] // channels
    block = 8
    return pl.pallas_call(
        functools.partial(mix_kernel, rows=rows, depth=depth),
        grid=(channels // block,),
        in_specs=[
            pl.BlockSpec((total, channels), lambda s: (0, 0)),
            pl.BlockSpec((channels, block * lanes), lambda s: (0, s)),
        ],
        out_specs=pl.BlockSpec((block * depth, rows * lanes), lambda s: (s, 0)),
        out_shape=jax.ShapeDtypeStruct((channels * depth, rows * lanes), BF16),
        compiler_params=pltpu.CompilerParams(vmem_limit_bytes=vmem_limit(length)),
        cost_estimate=pl.CostEstimate(flops=2 * 10**9, bytes_accessed=4000000, transcendentals=10**5),
        name="left_mix",
    )(left, factors)


def finish_kernel(
    idx, *refs, sub, far, rows, length, block
):
    near_refs, across_refs, refs = refs[: sub // 2], refs[sub // 2 : sub], refs[sub:]
    mixed, pair_one, validity, gain, widen, narrow, out, right, turned = refs
    me = idx[0]
    z, p = me // sub, me % sub
    step = 0 if block == rows else pl.program_id(0)
    half = far * rows * sub // 2
    lanes = pair_one.shape[2]
    part = min(length, 320)

    def first():
        r = iota((part, half), 1)
        b = div_const(r, rows, half)
        i = r - b * rows
        across_sub = 2 * div_const(b, far, half // rows)
        across_far = b - far * (across_sub >> 1)
        home = ((z ^ across_far) * sub + (p ^ across_sub)) * rows + i
        away = ((z ^ across_far) * sub + (p ^ 1 ^ across_sub)) * rows + i

        near = jnp.concatenate([ref[...].astype(F32) for ref in near_refs], 0).astype(BF16)
        across = jnp.concatenate([ref[...].astype(F32) for ref in across_refs], 0).astype(BF16)

        def arrange(start):
            j = iota((part, half), 0) + start
            here = pl.ds(start, part)
            right[here, :] = (dot(one_hot(j == home), near) + dot(one_hot(j == away), across)).astype(BF16)

        chunks(length, part, arrange)
        turned[...] = validity[...].astype(F32).T.astype(BF16)

    if block == rows:
        first()
    else:
        pl.when(step == 0)(first)
    i0 = me * rows + step * block
    target = i0 + iota((length, block * lanes), 1) // lanes
    mine = one_hot(iota((length, block * lanes), 0) == target)
    mine = dot(validity[...].astype(F32).astype(BF16), mine).astype(BF16)

    def finish(start):
        here = pl.ds(start, part)
        counts = dot(turned[here, :], mine) + OUTER_EPS
        update = dot(right[here, :], mixed[...]) / counts
        for r in range(block):
            x = pair_one[r, here, :] + update[:, r * lanes : (r + 1) * lanes]
            normed = layer_norm(x, gain[...]).astype(BF16)
            hidden = jnp.maximum(dot(normed, widen[...]), 0.0).astype(BF16)
            out[r, here, :] = (x + dot(hidden, narrow[...])).astype(BF16)

    chunks(length, part, finish)


def finish_call(idx, near, across, mixed, pair_one, validity, gain, widen, narrow, sub, far):
    rows, length, lanes = pair_one.shape
    depth = validity.shape[0]
    block = rows if length <= 320 else 2 if rows % 2 == 0 else 1
    product = mixed.shape[0]
    gain = gain[None, :]
    if block == rows:
        grid, vmem = {}, lambda a: pl.BlockSpec(memory_space=pltpu.VMEM)
        mixed_spec = pair_spec = vmem(mixed)
    else:
        grid, vmem = {"grid": (rows // block,)}, lambda a: pl.BlockSpec(a.shape, lambda s: (0,) * a.ndim)
        mixed_spec = pl.BlockSpec((product, block * lanes), lambda s: (0, s))
        pair_spec = pl.BlockSpec((block, length, lanes), lambda s: (s, 0, 0))
    return pl.pallas_call(
        functools.partial(finish_kernel, sub=sub, far=far, rows=rows, length=length, block=block),
        **grid,
        in_specs=[
            pl.BlockSpec(memory_space=pltpu.SMEM),
            *[vmem(a) for a in near + across],
            mixed_spec,
            pair_spec,
            vmem(validity),
            vmem(gain),
            vmem(widen),
            vmem(narrow),
        ],
        out_specs=pair_spec,
        out_shape=jax.ShapeDtypeStruct((rows, length, lanes), BF16),
        scratch_shapes=[pltpu.VMEM((length, product), BF16), pltpu.VMEM((length, depth), BF16)],
        compiler_params=pltpu.CompilerParams(vmem_limit_bytes=vmem_limit(length)),
        cost_estimate=pl.CostEstimate(flops=5 * 10**9, bytes_accessed=4000000, transcendentals=10**5),
        name="pair_update",
    )(idx, *near, *across, mixed, pair_one, validity, gain, widen, narrow)


def on_device(
    devices,
    alignment_embedding,
    couple_embedding,
    amino_strand,
    amino_validity,
    alignment_validity,
    separation_embedding,
    couple_shift_scaling,
    couple_shift_factors,
    horizontal_scaling_factor,
    horizontal_entry_factors,
    horizontal_exit_factors,
    vertical_scaling_factor,
    vertical_entry_factors,
    vertical_exit_factors,
    alignment_feedforward_scaling,
    alignment_widen_factors,
    alignment_narrow_factors,
    product_scaling_factor,
    product_twin_factors,
    product_exit_factors,
    couple_feedforward_scaling,
    couple_widen_factors,
    couple_narrow_factors,
):
    far = devices // SUB
    idx = lax.axis_index("dap").astype(jnp.int32).reshape(1)

    def swap(x, distance):
        return lax.ppermute(x, "dap", [(d, d ^ distance) for d in range(devices)])

    width = alignment_embedding.shape[2]
    rows = couple_embedding.shape[0]
    depth = alignment_validity.shape[0]

    beside = swap(alignment_embedding, 1)
    near = [swap(alignment_embedding, k) for k in range(2, SUB, 2)]
    pair_one, bias = pair_call(
        idx, amino_strand, couple_embedding, separation_embedding, couple_shift_scaling, couple_shift_factors
    )
    entry = horizontal_entry_factors.reshape(width, 4 * width)
    bias_blocks = [swap(bias, SUB)]
    later, entry, beside, *first = lax.optimization_barrier((bias, entry, beside, *near[:-1]))
    bias_blocks += [swap(later, SUB * k) for k in range(2, far)]
    bias_blocks = [bias] + bias_blocks
    near = first + near[-1:]
    near = jnp.concatenate(near, 0)
    across = swap(near, 1)
    projected = project_call(
        idx, [alignment_embedding, beside, near, across], horizontal_scaling_factor, entry, far, rows
    )
    sent = row_call(idx, bias_blocks, projected, alignment_validity, amino_validity, horizontal_exit_factors)
    pieces = [sent[0]] + [swap(sent[k], SUB * k) for k in range(1, far)]
    updated, left, right = column_call(
        idx,
        pieces,
        alignment_validity,
        vertical_scaling_factor,
        vertical_entry_factors.reshape(width, 4 * width),
        vertical_exit_factors,
        alignment_feedforward_scaling,
        alignment_widen_factors,
        alignment_narrow_factors,
        product_scaling_factor,
        product_twin_factors,
    )
    channels = left.shape[1]
    right = right.reshape(rows, channels * depth)
    factors = product_exit_factors.reshape(channels, -1)
    mixed = mix_call(left, factors, rows, alignment_validity.shape[1])
    parts = [right] + [swap(right, SUB * k) for k in range(1, far)]
    parts = lax.optimization_barrier((mixed, *parts))
    mixed, parts = parts[0], parts[1:]
    column = jnp.concatenate(parts, 0)
    near = [column] + [swap(column, k) for k in range(2, SUB, 2)]
    across = [swap(a, 1) for a in near]
    updated_pairs = finish_call(
        idx,
        near,
        across,
        mixed,
        pair_one,
        alignment_validity,
        couple_feedforward_scaling,
        couple_widen_factors,
        couple_narrow_factors,
        SUB,
        far,
    )
    return updated.transpose(1, 0, 2), updated_pairs


def solution(mesh):
    split = P("dap", None, None)
    return jax.shard_map(
        functools.partial(on_device, mesh.shape["dap"]),
        mesh=mesh,
        in_specs=(split, split) + (P(),) * 21,
        out_specs=(P(None, "dap", None), split),
        check_vma=False,
    )
```

```python
import functools

import jax
import jax.numpy as jnp
from jax import lax
from jax.experimental import pallas as pl
from jax.experimental.pallas import tpu as pltpu
from jax.sharding import PartitionSpec as P

HEADS = 8
SUB = 8
EPS = 1e-05
OUTER_EPS = 0.001
MASKED = -1000000000.0
LOG2E = 1.4426950408889634
F32 = jnp.float32
BF16 = jnp.bfloat16


def vmem_limit(length):
    return (16 if length is not None and length <= 320 else 56) * 1024 * 1024


def dot(a, b):
    return jnp.dot(a, b, preferred_element_type=F32)


def dot_nt(a, b):
    return lax.dot_general(a, b, (((1,), (1,)), ((), ())), preferred_element_type=F32)


def dot_tn(a, b):
    return lax.dot_general(a, b, (((0,), (0,)), ((), ())), preferred_element_type=F32)


def layer_norm(x, gain):
    centred = x - jnp.mean(x, -1, keepdims=True)
    spread = jnp.mean(centred * centred, -1, keepdims=True)
    return centred * lax.rsqrt(spread + EPS) * gain


def iota(shape, dim):
    return lax.broadcasted_iota(jnp.int32, shape, dim)


def div_const(x, d, limit):
    m = 65536 // d + 1
    assert all((v * m) >> 16 == v // d for v in range(limit)) and limit * m < 2**31
    return (x * m) >> 16


def one_hot(match):
    return jnp.where(match, 1.0, 0.0).astype(BF16)


def chunks(total, step, body):
    if total == step:
        body(0)
    else:
        lax.fori_loop(0, total // step, lambda c, x: (body(pl.multiple_of(c * step, step)), x)[1], 0)


def pair_kernel(
    idx, chain, pair, chain_row, table, gain, factors, pair_one, bias, shifted, chain_wide, *, rows, length, bins
):
    step = pl.program_id(0)
    reach = (bins - 2) // 2

    @pl.when(step == 0)
    def _():
        k = iota((2 * length, bins), 0)
        wanted = jnp.clip(length - k + reach, 0, 2 * reach)
        pick = jnp.where(wanted == iota((2 * length, bins), 1), 1.0, 0.0)
        shifted[...] = jnp.dot(pick, table[...], precision=lax.Precision.HIGHEST, preferred_element_type=F32)
        eye = iota((length, length), 0) == iota((length, length), 1)
        column = jnp.sum(jnp.where(eye, chain_row[...].astype(F32).reshape(1, length), 0.0), axis=1, keepdims=True)
        chain_wide[...] = jnp.broadcast_to(column, chain_wide.shape)

    other = table[bins - 1 : bins, :]
    block = pair.shape[0]
    for r in range(block):
        i = idx[0] * rows + step * block + r
        near = shifted[pl.ds(length - i, length), :]
        same = chain_wide[...] == chain[i].astype(F32)
        x = pair[r].astype(F32) + jnp.where(same, near, other)
        pair_one[r] = x
        normed = layer_norm(x, gain[...]).astype(BF16)
        bias[r] = dot_nt(factors[...], normed).astype(BF16)


def pair_call(idx, chain, pair, table, gain, factors):
    rows, length, depth = pair.shape
    block = 5 if rows % 5 == 0 else 1
    bins = table.shape[0]
    smem = pl.BlockSpec(memory_space=pltpu.SMEM)
    whole = lambda *shape: pl.BlockSpec(shape, lambda s: (0,) * len(shape))
    return pl.pallas_call(
        functools.partial(pair_kernel, rows=rows, length=length, bins=bins),
        grid=(rows // block,),
        in_specs=[
            smem,
            smem,
            pl.BlockSpec((block, length, depth), lambda s: (s, 0, 0)),
            whole(length),
            whole(bins, depth),
            whole(1, depth),
            whole(HEADS, depth),
        ],
        out_specs=[
            pl.BlockSpec((block, length, depth), lambda s: (s, 0, 0)),
            pl.BlockSpec((block, HEADS, length), lambda s: (s, 0, 0)),
        ],
        out_shape=[
            jax.ShapeDtypeStruct((rows, length, depth), F32),
            jax.ShapeDtypeStruct((rows, HEADS, length), BF16),
        ],
        scratch_shapes=[pltpu.VMEM((2 * length, depth), F32), pltpu.VMEM((length, depth), F32)],
        compiler_params=pltpu.CompilerParams(vmem_limit_bytes=vmem_limit(None)),
        cost_estimate=pl.CostEstimate(flops=4 * 10**9, bytes_accessed=4000000, transcendentals=10**5),
        name="pair_bias",
    )(idx, chain, pair, chain, table, gain[None, :], factors.T)


def project_kernel(idx, *refs, sub, far, rows, length, width):
    row_refs, refs = refs[:2], refs[2:]
    gain, entry, keys, values, query, gate, own_rows, own_normed = refs
    me = idx[0]
    z, p = me // sub, me % sub
    own = far * rows
    scale = (width // HEADS) ** -0.5 * LOG2E

    r = iota((own, length), 0)
    block = div_const(r, rows, own)
    residue = ((z ^ block) * sub + p) * rows + r - block * rows
    pick = one_hot(residue == iota((own, length), 1))

    step = min(length, 320)
    for k in range(sub):
        source, place = row_refs[k % 2], k // 2

        def project(start, k=k, source=source, place=place):
            x = source[place, pl.ds(start, step), :]
            normed = layer_norm(x.astype(F32), gain[...]).astype(BF16)
            both = dot(normed, entry[:, width : 3 * width])
            keys[k, pl.ds(start, step), :] = both[:, :width].astype(BF16)
            values[k, pl.ds(start, step), :] = both[:, width:].astype(BF16)
            part = pick if length == step else one_hot(residue[:, :step] == iota((own, step), 1) + start)
            q_rows, a_rows = dot(part, normed), dot(part, x)
            here = pl.ds(k * own, own)
            if length == step:
                own_normed[here, :] = q_rows
                own_rows[here, :] = a_rows
            else:
                fresh = start == 0
                own_normed[here, :] = q_rows + jnp.where(fresh, 0.0, own_normed[here, :])
                own_rows[here, :] = a_rows + jnp.where(fresh, 0.0, own_rows[here, :])

        chunks(length, step, project)

    total = sub * own
    part = min(total, 320)

    def queries(start):
        here = pl.ds(start, part)
        normed = own_normed[here, :].astype(BF16)
        query[here, :] = dot(normed, entry[:, :width]) * scale
        gate[here, :] = jax.nn.sigmoid(dot(normed, entry[:, 3 * width :]))

    chunks(total, part, queries)


def project_call(idx, msa_rows, gain, entry, far, rows):
    sub = SUB
    _, length, width = msa_rows[0].shape
    own = far * rows
    vmem = pl.BlockSpec(memory_space=pltpu.VMEM)
    wide = jax.ShapeDtypeStruct((sub, length, width), BF16)
    narrow = jax.ShapeDtypeStruct((sub * own, width), F32)
    return pl.pallas_call(
        functools.partial(project_kernel, sub=sub, far=far, rows=rows, length=length, width=width),
        in_specs=[pl.BlockSpec(memory_space=pltpu.SMEM)] + [vmem] * 4,
        out_specs=[vmem] * 5,
        out_shape=[wide, wide, narrow, narrow, narrow],
        scratch_shapes=[pltpu.VMEM((sub * own, width), F32)],
        compiler_params=pltpu.CompilerParams(vmem_limit_bytes=vmem_limit(length)),
        cost_estimate=pl.CostEstimate(flops=3 * 10**9, bytes_accessed=4000000, transcendentals=10**5),
        name="row_project",
    )(idx, *msa_rows, gain[None, :], entry)


def row_kernel(idx, *refs, order, sub, far, rows, length, width):
    bias_refs, refs = refs[:2], refs[2:]
    keys, values, query, gate, own_rows, validity, amino, exit_ = refs[:8]
    outs, refs = refs[8 : 8 + far], refs[8 + far :]
    by_residue, bias, gated = refs
    me = idx[0]
    z, p = me // sub, me % sub
    own = far * rows
    total = sub * own
    half = far // 2
    for n, b in enumerate(order):
        block = bias_refs[n // half][n % half * rows : (n % half + 1) * rows]
        by_residue[b * rows : (b + 1) * rows] = block.astype(F32) * LOG2E
    for h in range(HEADS):
        bias[h] = by_residue[:, h, :]

    channel = width // HEADS
    head_of = iota((1, width), 1) // channel
    head_mask = [jnp.where(head_of == h, 1.0, 0.0) for h in range(HEADS)]
    take = 40 if own % 40 == 0 else rows

    def attend(n, k, start):
        s = z * sub + (p ^ k)
        valid = validity[pl.ds(s, 1), :] * amino[...].reshape(1, length)
        masked = jnp.where(valid > 0, 0.0, MASKED)
        here = pl.ds(pl.multiple_of(n * take, take), take) if not isinstance(n, int) else pl.ds(n * take, take)
        q = query[here, :]
        q = jnp.concatenate([q * mask for mask in head_mask], 0).astype(BF16)
        scores = dot_nt(q, keys[k]) + bias[:, pl.ds(start, take), :].reshape(HEADS * take, length) + masked
        expo = jnp.exp2(scores - jnp.max(scores, -1, keepdims=True))
        share = 1.0 / jnp.sum(expo, -1, keepdims=True)
        mixed = dot(expo.astype(BF16), values[k]) * share
        merged = mixed[:take] * head_mask[0]
        for h in range(1, HEADS):
            merged += mixed[h * take : (h + 1) * take] * head_mask[h]
        gated[here, :] = merged * gate[here, :]

    parts = own // take
    if parts == 1:
        for k in range(sub):
            attend(k, k, 0)
    else:
        lax.fori_loop(0, sub * parts, lambda n, x: (attend(n, n // parts, (n % parts) * take), x)[1], 0)

    piece = rows * sub
    for b in range(far):
        q = iota((piece, total), 0) + b * piece
        residue_, row = div_const(q, sub, total), q & (sub - 1)
        swap = one_hot((row ^ p) * own + residue_ == iota((piece, total), 1))
        gated_rows = dot(swap, gated[...].astype(BF16)).astype(BF16)
        x = dot(swap, own_rows[...].astype(BF16)) + dot(gated_rows, exit_[...])
        outs[b][...] = x.astype(BF16).reshape(rows, sub, width)


def row_call(idx, bias_halves, order, projected, validity, amino, exit_):
    keys, values, query, gate, own_rows = projected
    sub, far = keys.shape[0], len(order)
    _, length, width = keys.shape
    rows = 2 * bias_halves[0].shape[0] // far
    own = far * rows
    vmem = pl.BlockSpec(memory_space=pltpu.VMEM)
    return pl.pallas_call(
        functools.partial(row_kernel, order=order, sub=sub, far=far, rows=rows, length=length, width=width),
        in_specs=[pl.BlockSpec(memory_space=pltpu.SMEM)] + [vmem] * 10,
        out_specs=[vmem] * far,
        out_shape=[jax.ShapeDtypeStruct((rows, sub, width), BF16)] * far,
        scratch_shapes=[
            pltpu.VMEM((own, HEADS, length), F32),
            pltpu.VMEM((HEADS, own, length), F32),
            pltpu.VMEM((sub * own, width), F32),
        ],
        compiler_params=pltpu.CompilerParams(vmem_limit_bytes=vmem_limit(length)),
        cost_estimate=pl.CostEstimate(flops=4 * 10**9, bytes_accessed=4000000, transcendentals=10**5),
        name="row_attention",
    )(idx, *bias_halves, keys, values, query, gate, own_rows, validity, amino, exit_)


def column_kernel(idx, *refs, sub, far, rows, block, depth, width):
    piece_refs, refs = refs[:far], refs[far:]
    entry, twin, *sources = refs[:9]
    updated, left, right, start_rows, gated, *held = refs[9:-1]
    sems = refs[-1]
    copies = [pltpu.make_async_copy(src, dst, sems.at[n]) for n, (src, dst) in enumerate(zip(sources, held))]
    steps = rows // block

    def begin():
        for copy in copies:
            copy.start()

    def arrived(*which):
        def wait():
            for n in which:
                copies[n].wait()

        if steps == 1:
            wait()
        else:
            pl.when(pl.program_id(0) == 0)(wait)
        return [held[n][...] for n in which]

    if steps == 1:
        begin()
    else:
        pl.when(pl.program_id(0) == 0)(begin)
    me = idx[0]
    z = me // sub
    first = me * rows + (0 if steps == 1 else pl.program_id(0) * block)
    scale = (width // HEADS) ** -0.5 * LOG2E
    total = block * depth
    for b in range(far):
        here = pl.ds(pl.multiple_of((z ^ b) * sub, sub), sub)
        start_rows[:, here, :] = piece_refs[b][...].astype(F32)
    x = start_rows[...].reshape(total, width)
    (col_gain,) = arrived(0)
    normed = layer_norm(x, col_gain).astype(BF16)
    proj = dot(normed, entry[...])
    query = proj[:, :width] * scale
    keys = proj[:, width : 2 * width].astype(BF16)
    values = proj[:, 2 * width : 3 * width].astype(BF16)
    gate = jax.nn.sigmoid(proj[:, 3 * width :])

    (validity,) = arrived(1)
    length = validity.shape[1]
    lanes = 128
    pick = one_hot(iota((length, lanes), 0) == first + iota((length, lanes), 1))
    valid = dot(validity.astype(F32).astype(BF16), pick)
    head_of = iota((1, width), 1) // (width // HEADS)
    head_mask = [jnp.where(head_of == h, 1.0, 0.0) for h in range(HEADS)]
    for i in range(block):
        here = slice(i * depth, (i + 1) * depth)
        q = jnp.concatenate([query[here] * mask for mask in head_mask], 0).astype(BF16)
        masked = jnp.where(valid[:, i : i + 1] > 0, 0.0, MASKED)
        scores = dot_nt(keys[here], q) + masked
        expo = jnp.exp2(scores - jnp.max(scores, 0, keepdims=True))
        weights = (expo * (1.0 / jnp.sum(expo, 0, keepdims=True))).astype(BF16)
        mixed = dot_tn(weights, values[here])
        merged = mixed[:depth] * head_mask[0]
        for h in range(1, HEADS):
            merged += mixed[h * depth : (h + 1) * depth] * head_mask[h]
        gated[here, :] = merged * gate[here]
    exit_, ff_gain, widen, narrow, product_gain = arrived(2, 3, 4, 5, 6)
    x = x + dot(gated[...].astype(BF16), exit_)
    hidden = jnp.maximum(dot(layer_norm(x, ff_gain).astype(BF16), widen).astype(BF16), 0.0)
    x = x + dot(hidden, narrow)
    updated[...] = x.astype(BF16).reshape(block, depth, width)
    outer = layer_norm(x, product_gain).astype(BF16)
    both = dot(outer, twin[...])
    channels = twin.shape[1] // 2
    spread = iota((depth, channels * depth), 1)
    channel = spread // depth
    repeat = one_hot(
        iota((2 * channels, channels * depth), 0) - channels == iota((2 * channels, channels * depth), 1) // depth
    )
    mine = jnp.where(spread - channel * depth == iota((depth, channels * depth), 0), 1.0, 0.0)
    for i in range(block):
        here = slice(i * depth, (i + 1) * depth)
        part = (both[here] * valid[:, i : i + 1]).astype(BF16)
        left[here, :] = part[:, :channels]
        right[0, i : i + 1, :] = jnp.sum(dot(part, repeat) * mine, axis=0, keepdims=True).astype(BF16)


def column_call(idx, pieces, validity, col_gain, entry, exit_, ff_gain, widen, narrow, product_gain, twin):
    far = len(pieces)
    rows, sub, width = pieces[0].shape
    depth, length = validity.shape
    block = rows
    while block * depth > 320 and block % 2 == 0:
        block //= 2
    channels = twin.shape[1] // 2
    steps = rows // block
    here = [entry, twin]
    sources = [
        col_gain[None, :],
        validity,
        exit_,
        ff_gain[None, :],
        widen,
        narrow,
        product_gain[None, :],
    ]
    if steps == 1:
        grid, spec = {}, lambda shape, index: pl.BlockSpec(memory_space=pltpu.VMEM)
    else:
        grid, spec = {"grid": (steps,)}, pl.BlockSpec
    return pl.pallas_call(
        functools.partial(column_kernel, sub=sub, far=far, rows=rows, block=block, depth=depth, width=width),
        **grid,
        in_specs=[pl.BlockSpec(memory_space=pltpu.SMEM)]
        + [spec((block, sub, width), lambda s: (s, 0, 0))] * far
        + [spec(a.shape, lambda s: (0, 0)) for a in here]
        + [pl.BlockSpec(memory_space=pltpu.HBM)] * len(sources),
        out_specs=[
            spec((block, depth, width), lambda s: (s, 0, 0)),
            spec((block * depth, channels), lambda s: (s, 0)),
            spec((1, block, channels * depth), lambda s: (s, 0, 0)),
        ],
        out_shape=[
            jax.ShapeDtypeStruct((rows, depth, width), BF16),
            jax.ShapeDtypeStruct((rows * depth, channels), BF16),
            jax.ShapeDtypeStruct((steps, block, channels * depth), BF16),
        ],
        scratch_shapes=[pltpu.VMEM((block, depth, width), F32), pltpu.VMEM((block * depth, width), F32)]
        + [pltpu.VMEM(a.shape, a.dtype) for a in sources]
        + [pltpu.SemaphoreType.DMA((len(sources),))],
        compiler_params=pltpu.CompilerParams(vmem_limit_bytes=vmem_limit(length)),
        cost_estimate=pl.CostEstimate(flops=5 * 10**9, bytes_accessed=4000000, transcendentals=10**5),
        name="column_attention",
    )(idx, *pieces, *here, *sources)


def mix_kernel(left, factors, out, *, rows, depth):
    lanes = out.shape[1] // rows
    for e in range(0, out.shape[0] // depth, 2):
        y = dot(left[...], factors[:, e * lanes : (e + 2) * lanes]).astype(BF16)
        for i in range(rows):
            for f in range(2):
                block = y[i * depth : (i + 1) * depth, f * lanes : (f + 1) * lanes]
                out[(e + f) * depth : (e + f + 1) * depth, i * lanes : (i + 1) * lanes] = block


def mix_call(left, factors, rows, length):
    total, channels = left.shape
    depth = total // rows
    lanes = factors.shape[1] // channels
    block = 8
    return pl.pallas_call(
        functools.partial(mix_kernel, rows=rows, depth=depth),
        grid=(channels // block,),
        in_specs=[
            pl.BlockSpec((total, channels), lambda s: (0, 0)),
            pl.BlockSpec((channels, block * lanes), lambda s: (0, s)),
        ],
        out_specs=pl.BlockSpec((block * depth, rows * lanes), lambda s: (s, 0)),
        out_shape=jax.ShapeDtypeStruct((channels * depth, rows * lanes), BF16),
        compiler_params=pltpu.CompilerParams(vmem_limit_bytes=vmem_limit(length)),
        cost_estimate=pl.CostEstimate(flops=2 * 10**9, bytes_accessed=4000000, transcendentals=10**5),
        name="left_mix",
    )(left, factors)


def finish_kernel(
    idx, *refs, sub, far, rows, length, block
):
    near_refs, across_refs, refs = refs[: sub // 2], refs[sub // 2 : sub], refs[sub:]
    mixed, pair_one, validity, gain, widen, narrow, out, right, turned = refs
    me = idx[0]
    z, p = me // sub, me % sub
    step = 0 if block == rows else pl.program_id(0)
    half = far * rows * sub // 2
    lanes = pair_one.shape[2]
    part = min(length, 320)

    def first():
        r = iota((part, half), 1)
        b = div_const(r, rows, half)
        i = r - b * rows
        across_sub = 2 * div_const(b, far, half // rows)
        across_far = b - far * (across_sub >> 1)
        home = ((z ^ across_far) * sub + (p ^ across_sub)) * rows + i
        away = ((z ^ across_far) * sub + (p ^ 1 ^ across_sub)) * rows + i

        near = jnp.concatenate([ref[...].astype(F32) for ref in near_refs], 0).astype(BF16)
        across = jnp.concatenate([ref[...].astype(F32) for ref in across_refs], 0).astype(BF16)

        def arrange(start):
            j = iota((part, half), 0) + start
            here = pl.ds(start, part)
            right[here, :] = (dot(one_hot(j == home), near) + dot(one_hot(j == away), across)).astype(BF16)

        chunks(length, part, arrange)
        turned[...] = validity[...].astype(F32).T.astype(BF16)

    if block == rows:
        first()
    else:
        pl.when(step == 0)(first)
    i0 = me * rows + step * block
    target = i0 + iota((length, block * lanes), 1) // lanes
    mine = one_hot(iota((length, block * lanes), 0) == target)
    mine = dot(validity[...].astype(F32).astype(BF16), mine).astype(BF16)

    def finish(start):
        here = pl.ds(start, part)
        counts = dot(turned[here, :], mine) + OUTER_EPS
        update = dot(right[here, :], mixed[...]) / counts
        for r in range(block):
            x = pair_one[r, here, :] + update[:, r * lanes : (r + 1) * lanes]
            normed = layer_norm(x, gain[...]).astype(BF16)
            hidden = jnp.maximum(dot(normed, widen[...]).astype(BF16), 0.0)
            out[r, here, :] = (x + dot(hidden, narrow[...])).astype(BF16)

    chunks(length, part, finish)


def finish_call(idx, near, across, mixed, pair_one, validity, gain, widen, narrow, sub, far):
    rows, length, lanes = pair_one.shape
    depth = validity.shape[0]
    block = rows if length <= 320 else 2 if rows % 2 == 0 else 1
    product = mixed.shape[0]
    gain = gain[None, :]
    if block == rows:
        grid, vmem = {}, lambda a: pl.BlockSpec(memory_space=pltpu.VMEM)
        mixed_spec = pair_spec = vmem(mixed)
    else:
        grid, vmem = {"grid": (rows // block,)}, lambda a: pl.BlockSpec(a.shape, lambda s: (0,) * a.ndim)
        mixed_spec = pl.BlockSpec((product, block * lanes), lambda s: (0, s))
        pair_spec = pl.BlockSpec((block, length, lanes), lambda s: (s, 0, 0))
    return pl.pallas_call(
        functools.partial(finish_kernel, sub=sub, far=far, rows=rows, length=length, block=block),
        **grid,
        in_specs=[
            pl.BlockSpec(memory_space=pltpu.SMEM),
            *[vmem(a) for a in near + across],
            mixed_spec,
            pair_spec,
            vmem(validity),
            vmem(gain),
            vmem(widen),
            vmem(narrow),
        ],
        out_specs=pair_spec,
        out_shape=jax.ShapeDtypeStruct((rows, length, lanes), BF16),
        scratch_shapes=[pltpu.VMEM((length, product), BF16), pltpu.VMEM((length, depth), BF16)],
        compiler_params=pltpu.CompilerParams(vmem_limit_bytes=vmem_limit(length)),
        cost_estimate=pl.CostEstimate(flops=5 * 10**9, bytes_accessed=4000000, transcendentals=10**5),
        name="pair_update",
    )(idx, *near, *across, mixed, pair_one, validity, gain, widen, narrow)


def on_device(
    devices,
    alignment_embedding,
    couple_embedding,
    amino_strand,
    amino_validity,
    alignment_validity,
    separation_embedding,
    couple_shift_scaling,
    couple_shift_factors,
    horizontal_scaling_factor,
    horizontal_entry_factors,
    horizontal_exit_factors,
    vertical_scaling_factor,
    vertical_entry_factors,
    vertical_exit_factors,
    alignment_feedforward_scaling,
    alignment_widen_factors,
    alignment_narrow_factors,
    product_scaling_factor,
    product_twin_factors,
    product_exit_factors,
    couple_feedforward_scaling,
    couple_widen_factors,
    couple_narrow_factors,
):
    far = devices // SUB
    idx = lax.axis_index("dap").astype(jnp.int32).reshape(1)

    def swap(x, distance):
        return lax.ppermute(x, "dap", [(d, d ^ distance) for d in range(devices)])

    width = alignment_embedding.shape[2]
    rows = couple_embedding.shape[0]
    depth = alignment_validity.shape[0]

    near = [swap(alignment_embedding, k) for k in range(2, SUB, 2)]
    pair_one, bias = pair_call(
        idx, amino_strand, couple_embedding, separation_embedding, couple_shift_scaling, couple_shift_factors
    )
    entry = horizontal_entry_factors.reshape(width, 4 * width)
    order, distance = [0], far // 2
    mine, theirs = bias, swap(bias, SUB * distance)
    order += [b ^ distance for b in order]
    while distance > 1:
        distance //= 2
        mine = jnp.concatenate([mine, theirs], 0)
        theirs = swap(mine, SUB * distance)
        order += [b ^ distance for b in order]
    near = jnp.concatenate([alignment_embedding, *near], 0)
    entry, mine, near = lax.optimization_barrier((entry, mine, near))
    across = swap(near, 1)
    projected = project_call(idx, [near, across], horizontal_scaling_factor, entry, far, rows)
    sent = row_call(
        idx, [mine, theirs], order, projected, alignment_validity, amino_validity, horizontal_exit_factors
    )
    pieces = [sent[0]] + [swap(sent[k], SUB * k) for k in range(1, far)]
    updated, left, right = column_call(
        idx,
        pieces,
        alignment_validity,
        vertical_scaling_factor,
        vertical_entry_factors.reshape(width, 4 * width),
        vertical_exit_factors,
        alignment_feedforward_scaling,
        alignment_widen_factors,
        alignment_narrow_factors,
        product_scaling_factor,
        product_twin_factors,
    )
    channels = left.shape[1]
    right = right.reshape(rows, channels * depth)
    factors = product_exit_factors.reshape(channels, -1)
    mixed = mix_call(left, factors, rows, alignment_validity.shape[1])
    parts = [right] + [swap(right, SUB * k) for k in range(1, far)]
    parts = lax.optimization_barrier((mixed, *parts))
    mixed, parts = parts[0], parts[1:]
    column = jnp.concatenate(parts, 0)
    near = [column] + [swap(column, k) for k in range(2, SUB, 2)]
    across = [swap(a, 1) for a in near]
    updated_pairs = finish_call(
        idx,
        near,
        across,
        mixed,
        pair_one,
        alignment_validity,
        couple_feedforward_scaling,
        couple_widen_factors,
        couple_narrow_factors,
        SUB,
        far,
    )
    return updated.transpose(1, 0, 2), updated_pairs


def solution(mesh):
    split = P("dap", None, None)
    return jax.shard_map(
        functools.partial(on_device, mesh.shape["dap"]),
        mesh=mesh,
        in_specs=(split, split) + (P(),) * 21,
        out_specs=(P(None, "dap", None), split),
        check_vma=False,
    )
```

```python
import functools

import jax
import jax.numpy as jnp
from jax import lax
from jax.experimental import pallas as pl
from jax.experimental.pallas import tpu as pltpu
from jax.sharding import PartitionSpec as P

HEADS = 8
SUB = 8
EPS = 1e-05
OUTER_EPS = 0.001
MASKED = -1000000000.0
LOG2E = 1.4426950408889634
F32 = jnp.float32
BF16 = jnp.bfloat16


def vmem_limit(length):
    return (16 if length is not None and length <= 320 else 56) * 1024 * 1024


def dot(a, b):
    return jnp.dot(a, b, preferred_element_type=F32)


def dot_nt(a, b):
    return lax.dot_general(a, b, (((1,), (1,)), ((), ())), preferred_element_type=F32)


def dot_tn(a, b):
    return lax.dot_general(a, b, (((0,), (0,)), ((), ())), preferred_element_type=F32)


def layer_norm(x, gain):
    centred = x - jnp.mean(x, -1, keepdims=True)
    spread = jnp.mean(centred * centred, -1, keepdims=True)
    return centred * lax.rsqrt(spread + EPS) * gain


def iota(shape, dim):
    return lax.broadcasted_iota(jnp.int32, shape, dim)


def div_const(x, d, limit):
    m = 65536 // d + 1
    assert all((v * m) >> 16 == v // d for v in range(limit)) and limit * m < 2**31
    return (x * m) >> 16


def one_hot(match):
    return jnp.where(match, 1.0, 0.0).astype(BF16)


def chunks(total, step, body):
    if total == step:
        body(0)
    else:
        lax.fori_loop(0, total // step, lambda c, x: (body(pl.multiple_of(c * step, step)), x)[1], 0)


def pair_kernel(
    idx, chain, pair, chain_row, table, gain, factors, pair_one, bias, shifted, chain_wide, *, rows, length, bins
):
    step = pl.program_id(0)
    reach = (bins - 2) // 2

    @pl.when(step == 0)
    def _():
        k = iota((2 * length, bins), 0)
        wanted = jnp.clip(length - k + reach, 0, 2 * reach)
        pick = one_hot(wanted == iota((2 * length, bins), 1))
        rest, total = table[...], 0.0
        for _ in range(3):
            part = rest.astype(BF16)
            total += dot(pick, part)
            rest = rest - part.astype(F32)
        shifted[...] = total
        eye = iota((length, length), 0) == iota((length, length), 1)
        column = jnp.sum(jnp.where(eye, chain_row[...].astype(F32).reshape(1, length), 0.0), axis=1, keepdims=True)
        chain_wide[...] = jnp.broadcast_to(column, chain_wide.shape)

    other = table[bins - 1 : bins, :]
    block = pair.shape[0]
    for r in range(block):
        i = idx[0] * rows + step * block + r
        near = shifted[pl.ds(length - i, length), :]
        same = chain_wide[...] == chain[i].astype(F32)
        x = pair[r].astype(F32) + jnp.where(same, near, other)
        pair_one[r] = x
        normed = layer_norm(x, gain[...]).astype(BF16)
        bias[r] = dot_nt(factors[...], normed).astype(BF16)


def pair_call(idx, chain, pair, table, gain, factors):
    rows, length, depth = pair.shape
    block = 5 if rows % 5 == 0 else 1
    bins = table.shape[0]
    smem = pl.BlockSpec(memory_space=pltpu.SMEM)
    whole = lambda *shape: pl.BlockSpec(shape, lambda s: (0,) * len(shape))
    return pl.pallas_call(
        functools.partial(pair_kernel, rows=rows, length=length, bins=bins),
        grid=(rows // block,),
        in_specs=[
            smem,
            smem,
            pl.BlockSpec((block, length, depth), lambda s: (s, 0, 0)),
            whole(length),
            whole(bins, depth),
            whole(1, depth),
            whole(HEADS, depth),
        ],
        out_specs=[
            pl.BlockSpec((block, length, depth), lambda s: (s, 0, 0)),
            pl.BlockSpec((block, HEADS, length), lambda s: (s, 0, 0)),
        ],
        out_shape=[
            jax.ShapeDtypeStruct((rows, length, depth), F32),
            jax.ShapeDtypeStruct((rows, HEADS, length), BF16),
        ],
        scratch_shapes=[pltpu.VMEM((2 * length, depth), F32), pltpu.VMEM((length, depth), F32)],
        compiler_params=pltpu.CompilerParams(vmem_limit_bytes=vmem_limit(None)),
        cost_estimate=pl.CostEstimate(flops=4 * 10**9, bytes_accessed=4000000, transcendentals=10**5),
        name="pair_bias",
    )(idx, chain, pair, chain, table, gain[None, :], factors.T)


def project_kernel(idx, *refs, sub, far, rows, length, width):
    row_refs, refs = refs[:2], refs[2:]
    gain, entry, keys, values, query, gate, own_rows, own_normed = refs
    me = idx[0]
    z, p = me // sub, me % sub
    own = far * rows
    scale = (width // HEADS) ** -0.5 * LOG2E

    r = iota((own, length), 0)
    block = div_const(r, rows, own)
    residue = ((z ^ block) * sub + p) * rows + r - block * rows
    pick = one_hot(residue == iota((own, length), 1))

    step = min(length, 320)
    for k in range(sub):
        source, place = row_refs[k % 2], k // 2

        def project(start, k=k, source=source, place=place):
            x = source[place, pl.ds(start, step), :]
            normed = layer_norm(x.astype(F32), gain[...]).astype(BF16)
            both = dot(normed, entry[:, width : 3 * width])
            keys[k, pl.ds(start, step), :] = both[:, :width].astype(BF16)
            values[k, pl.ds(start, step), :] = both[:, width:].astype(BF16)
            part = pick if length == step else one_hot(residue[:, :step] == iota((own, step), 1) + start)
            q_rows, a_rows = dot(part, normed), dot(part, x)
            here = pl.ds(k * own, own)
            if length == step:
                own_normed[here, :] = q_rows
                own_rows[here, :] = a_rows
            else:
                fresh = start == 0
                own_normed[here, :] = q_rows + jnp.where(fresh, 0.0, own_normed[here, :])
                own_rows[here, :] = a_rows + jnp.where(fresh, 0.0, own_rows[here, :])

        chunks(length, step, project)

    total = sub * own
    part = min(total, 320)

    def queries(start):
        here = pl.ds(start, part)
        normed = own_normed[here, :].astype(BF16)
        query[here, :] = dot(normed, entry[:, :width]) * scale
        gate[here, :] = jax.nn.sigmoid(dot(normed, entry[:, 3 * width :]))

    chunks(total, part, queries)


def project_call(idx, msa_rows, gain, entry, far, rows):
    sub = SUB
    _, length, width = msa_rows[0].shape
    own = far * rows
    vmem = pl.BlockSpec(memory_space=pltpu.VMEM)
    wide = jax.ShapeDtypeStruct((sub, length, width), BF16)
    narrow = jax.ShapeDtypeStruct((sub * own, width), F32)
    return pl.pallas_call(
        functools.partial(project_kernel, sub=sub, far=far, rows=rows, length=length, width=width),
        in_specs=[pl.BlockSpec(memory_space=pltpu.SMEM)] + [vmem] * 4,
        out_specs=[vmem] * 5,
        out_shape=[wide, wide, narrow, narrow, narrow],
        scratch_shapes=[pltpu.VMEM((sub * own, width), F32)],
        compiler_params=pltpu.CompilerParams(vmem_limit_bytes=vmem_limit(length)),
        cost_estimate=pl.CostEstimate(flops=3 * 10**9, bytes_accessed=4000000, transcendentals=10**5),
        name="row_project",
    )(idx, *msa_rows, gain[None, :], entry)


def row_kernel(idx, *refs, order, sub, far, rows, length, width):
    bias_refs, refs = refs[:2], refs[2:]
    keys, values, query, gate, own_rows, validity, amino, exit_ = refs[:8]
    outs, refs = refs[8 : 8 + far], refs[8 + far :]
    by_residue, bias, gated = refs
    me = idx[0]
    z, p = me // sub, me % sub
    own = far * rows
    total = sub * own
    half = far // 2
    for n, b in enumerate(order):
        block = bias_refs[n // half][n % half * rows : (n % half + 1) * rows]
        by_residue[b * rows : (b + 1) * rows] = block.astype(F32) * LOG2E
    for h in range(HEADS):
        bias[h] = by_residue[:, h, :]

    channel = width // HEADS
    head_of = iota((1, width), 1) // channel
    head_mask = [jnp.where(head_of == h, 1.0, 0.0) for h in range(HEADS)]
    take = 40 if own % 40 == 0 else rows

    def attend(n, k, start):
        s = z * sub + (p ^ k)
        valid = validity[pl.ds(s, 1), :] * amino[...].reshape(1, length)
        masked = jnp.where(valid > 0, 0.0, MASKED)
        here = pl.ds(pl.multiple_of(n * take, take), take) if not isinstance(n, int) else pl.ds(n * take, take)
        q = query[here, :]
        q = jnp.concatenate([q * mask for mask in head_mask], 0).astype(BF16)
        scores = dot_nt(q, keys[k]) + bias[:, pl.ds(start, take), :].reshape(HEADS * take, length) + masked
        expo = jnp.exp2(scores - jnp.max(scores, -1, keepdims=True))
        share = 1.0 / jnp.sum(expo, -1, keepdims=True)
        mixed = dot(expo.astype(BF16), values[k]) * share
        merged = mixed[:take] * head_mask[0]
        for h in range(1, HEADS):
            merged += mixed[h * take : (h + 1) * take] * head_mask[h]
        gated[here, :] = merged * gate[here, :]

    parts = own // take
    if parts == 1:
        for k in range(sub):
            attend(k, k, 0)
    else:
        lax.fori_loop(0, sub * parts, lambda n, x: (attend(n, n // parts, (n % parts) * take), x)[1], 0)

    piece = rows * sub
    for b in range(far):
        q = iota((piece, total), 0) + b * piece
        residue_, row = div_const(q, sub, total), q & (sub - 1)
        swap = one_hot((row ^ p) * own + residue_ == iota((piece, total), 1))
        gated_rows = dot(swap, gated[...].astype(BF16)).astype(BF16)
        x = dot(swap, own_rows[...].astype(BF16)) + dot(gated_rows, exit_[...])
        outs[b][...] = x.astype(BF16).reshape(rows, sub, width)


def row_call(idx, bias_halves, order, projected, validity, amino, exit_):
    keys, values, query, gate, own_rows = projected
    sub, far = keys.shape[0], len(order)
    _, length, width = keys.shape
    rows = 2 * bias_halves[0].shape[0] // far
    own = far * rows
    vmem = pl.BlockSpec(memory_space=pltpu.VMEM)
    return pl.pallas_call(
        functools.partial(row_kernel, order=order, sub=sub, far=far, rows=rows, length=length, width=width),
        in_specs=[pl.BlockSpec(memory_space=pltpu.SMEM)] + [vmem] * 10,
        out_specs=[vmem] * far,
        out_shape=[jax.ShapeDtypeStruct((rows, sub, width), BF16)] * far,
        scratch_shapes=[
            pltpu.VMEM((own, HEADS, length), F32),
            pltpu.VMEM((HEADS, own, length), F32),
            pltpu.VMEM((sub * own, width), F32),
        ],
        compiler_params=pltpu.CompilerParams(vmem_limit_bytes=vmem_limit(length)),
        cost_estimate=pl.CostEstimate(flops=4 * 10**9, bytes_accessed=4000000, transcendentals=10**5),
        name="row_attention",
    )(idx, *bias_halves, keys, values, query, gate, own_rows, validity, amino, exit_)


def column_kernel(idx, *refs, sub, far, rows, block, depth, width):
    piece_refs, refs = refs[:far], refs[far:]
    entry, twin, *sources = refs[:9]
    updated, left, right, start_rows, gated, *held = refs[9:-1]
    sems = refs[-1]
    copies = [pltpu.make_async_copy(src, dst, sems.at[n]) for n, (src, dst) in enumerate(zip(sources, held))]
    steps = rows // block

    def begin():
        for copy in copies:
            copy.start()

    def arrived(*which):
        def wait():
            for n in which:
                copies[n].wait()

        if steps == 1:
            wait()
        else:
            pl.when(pl.program_id(0) == 0)(wait)
        return [held[n][...] for n in which]

    if steps == 1:
        begin()
    else:
        pl.when(pl.program_id(0) == 0)(begin)
    me = idx[0]
    z = me // sub
    first = me * rows + (0 if steps == 1 else pl.program_id(0) * block)
    scale = (width // HEADS) ** -0.5 * LOG2E
    total = block * depth
    for b in range(far):
        here = pl.ds(pl.multiple_of((z ^ b) * sub, sub), sub)
        start_rows[:, here, :] = piece_refs[b][...].astype(F32)
    x = start_rows[...].reshape(total, width)
    (col_gain,) = arrived(0)
    normed = layer_norm(x, col_gain).astype(BF16)
    proj = dot(normed, entry[...])
    query = proj[:, :width] * scale
    keys = proj[:, width : 2 * width].astype(BF16)
    values = proj[:, 2 * width : 3 * width].astype(BF16)
    gate = jax.nn.sigmoid(proj[:, 3 * width :])

    (validity,) = arrived(1)
    length = validity.shape[1]
    lanes = 128
    pick = one_hot(iota((length, lanes), 0) == first + iota((length, lanes), 1))
    valid = dot(validity.astype(F32).astype(BF16), pick)
    head_of = iota((1, width), 1) // (width // HEADS)
    head_mask = [jnp.where(head_of == h, 1.0, 0.0) for h in range(HEADS)]
    for i in range(block):
        here = slice(i * depth, (i + 1) * depth)
        q = jnp.concatenate([query[here] * mask for mask in head_mask], 0).astype(BF16)
        masked = jnp.where(valid[:, i : i + 1] > 0, 0.0, MASKED)
        scores = dot_nt(keys[here], q) + masked
        expo = jnp.exp2(scores - jnp.max(scores, 0, keepdims=True))
        weights = (expo * (1.0 / jnp.sum(expo, 0, keepdims=True))).astype(BF16)
        mixed = dot_tn(weights, values[here])
        merged = mixed[:depth] * head_mask[0]
        for h in range(1, HEADS):
            merged += mixed[h * depth : (h + 1) * depth] * head_mask[h]
        gated[here, :] = merged * gate[here]
    exit_, ff_gain, widen, narrow, product_gain = arrived(2, 3, 4, 5, 6)
    x = x + dot(gated[...].astype(BF16), exit_)
    hidden = jnp.maximum(dot(layer_norm(x, ff_gain).astype(BF16), widen).astype(BF16), 0.0)
    x = x + dot(hidden, narrow)
    updated[...] = x.astype(BF16).reshape(block, depth, width)
    outer = layer_norm(x, product_gain).astype(BF16)
    both = dot(outer, twin[...])
    channels = twin.shape[1] // 2
    spread = iota((depth, channels * depth), 1)
    channel = spread // depth
    repeat = one_hot(
        iota((2 * channels, channels * depth), 0) - channels == iota((2 * channels, channels * depth), 1) // depth
    )
    mine = jnp.where(spread - channel * depth == iota((depth, channels * depth), 0), 1.0, 0.0)
    for i in range(block):
        here = slice(i * depth, (i + 1) * depth)
        part = (both[here] * valid[:, i : i + 1]).astype(BF16)
        left[here, :] = part[:, :channels]
        right[0, i : i + 1, :] = jnp.sum(dot(part, repeat) * mine, axis=0, keepdims=True).astype(BF16)


def column_call(idx, pieces, validity, col_gain, entry, exit_, ff_gain, widen, narrow, product_gain, twin):
    far = len(pieces)
    rows, sub, width = pieces[0].shape
    depth, length = validity.shape
    block = rows
    while block * depth > 320 and block % 2 == 0:
        block //= 2
    channels = twin.shape[1] // 2
    steps = rows // block
    here = [entry, twin]
    sources = [
        col_gain[None, :],
        validity,
        exit_,
        ff_gain[None, :],
        widen,
        narrow,
        product_gain[None, :],
    ]
    if steps == 1:
        grid, spec = {}, lambda shape, index: pl.BlockSpec(memory_space=pltpu.VMEM)
    else:
        grid, spec = {"grid": (steps,)}, pl.BlockSpec
    return pl.pallas_call(
        functools.partial(column_kernel, sub=sub, far=far, rows=rows, block=block, depth=depth, width=width),
        **grid,
        in_specs=[pl.BlockSpec(memory_space=pltpu.SMEM)]
        + [spec((block, sub, width), lambda s: (s, 0, 0))] * far
        + [spec(a.shape, lambda s: (0, 0)) for a in here]
        + [pl.BlockSpec(memory_space=pltpu.HBM)] * len(sources),
        out_specs=[
            spec((block, depth, width), lambda s: (s, 0, 0)),
            spec((block * depth, channels), lambda s: (s, 0)),
            spec((1, block, channels * depth), lambda s: (s, 0, 0)),
        ],
        out_shape=[
            jax.ShapeDtypeStruct((rows, depth, width), BF16),
            jax.ShapeDtypeStruct((rows * depth, channels), BF16),
            jax.ShapeDtypeStruct((steps, block, channels * depth), BF16),
        ],
        scratch_shapes=[pltpu.VMEM((block, depth, width), F32), pltpu.VMEM((block * depth, width), F32)]
        + [pltpu.VMEM(a.shape, a.dtype) for a in sources]
        + [pltpu.SemaphoreType.DMA((len(sources),))],
        compiler_params=pltpu.CompilerParams(vmem_limit_bytes=vmem_limit(length)),
        cost_estimate=pl.CostEstimate(flops=5 * 10**9, bytes_accessed=4000000, transcendentals=10**5),
        name="column_attention",
    )(idx, *pieces, *here, *sources)


def mix_kernel(idx, left, factors, validity, out, inverse, *, rows, depth, steps):
    lanes = out.shape[1] // rows
    for e in range(0, out.shape[0] // depth, 2):
        y = dot(left[...], factors[:, e * lanes : (e + 2) * lanes]).astype(BF16)
        for i in range(rows):
            for f in range(2):
                block = y[i * depth : (i + 1) * depth, f * lanes : (f + 1) * lanes]
                out[(e + f) * depth : (e + f + 1) * depth, i * lanes : (i + 1) * lanes] = block

    def count():
        length = validity.shape[1]
        valid = validity[...].astype(F32)
        target = idx[0] * rows + iota((length, rows * lanes), 1) // lanes
        mine = dot(valid.astype(BF16), one_hot(iota((length, rows * lanes), 0) == target))
        mine, turned = mine.astype(BF16), valid.T.astype(BF16)
        part = min(length, 320)
        for start in range(0, length, part):
            inverse[start : start + part, :] = 1.0 / (dot(turned[start : start + part], mine) + OUTER_EPS)

    if steps == 1:
        count()
    else:
        pl.when(pl.program_id(0) == 0)(count)


def mix_call(idx, left, factors, validity, rows):
    total, channels = left.shape
    depth, length = validity.shape
    lanes = factors.shape[1] // channels
    steps = 1 if length <= 320 else 4
    block = channels // steps
    if steps == 1:
        grid, spec = {}, lambda shape, index: pl.BlockSpec(memory_space=pltpu.VMEM)
    else:
        grid, spec = {"grid": (steps,)}, pl.BlockSpec
    return pl.pallas_call(
        functools.partial(mix_kernel, rows=rows, depth=depth, steps=steps),
        **grid,
        in_specs=[
            pl.BlockSpec(memory_space=pltpu.SMEM),
            spec((total, channels), lambda s: (0, 0)),
            spec((channels, block * lanes), lambda s: (0, s)),
            spec((depth, length), lambda s: (0, 0)),
        ],
        out_specs=[
            spec((block * depth, rows * lanes), lambda s: (s, 0)),
            spec((length, rows * lanes), lambda s: (0, 0)),
        ],
        out_shape=[
            jax.ShapeDtypeStruct((channels * depth, rows * lanes), BF16),
            jax.ShapeDtypeStruct((length, rows * lanes), F32),
        ],
        compiler_params=pltpu.CompilerParams(vmem_limit_bytes=vmem_limit(length)),
        cost_estimate=pl.CostEstimate(flops=2 * 10**9, bytes_accessed=4000000, transcendentals=10**5),
        name="left_mix",
    )(idx, left, factors, validity)


def finish_kernel(idx, *refs, pieces, sub, far, rows, length, block):
    near_refs, across_refs, refs = refs[:pieces], refs[pieces : 2 * pieces], refs[2 * pieces :]
    mixed, inverse, pair_one, gain, widen, narrow, out, right, held, sems = refs
    me = idx[0]
    z, p = me // sub, me % sub
    half = far * rows * sub // 2
    lanes = pair_one.shape[2]
    part = min(length, 320)
    alone = block == rows

    def first():
        r = iota((part, half), 1)
        b = div_const(r, rows, half)
        i = r - b * rows
        across_sub = 2 * div_const(b, far, half // rows)
        across_far = b - far * (across_sub >> 1)
        home = ((z ^ across_far) * sub + (p ^ across_sub)) * rows + i
        away = ((z ^ across_far) * sub + (p ^ 1 ^ across_sub)) * rows + i
        near = jnp.concatenate([ref[...].astype(F32) for ref in near_refs], 0).astype(BF16)
        across = jnp.concatenate([ref[...].astype(F32) for ref in across_refs], 0).astype(BF16)

        def arrange(start):
            j = iota((part, half), 0) + start
            here = pl.ds(start, part)
            right[here, :] = (dot(one_hot(j == home), near) + dot(one_hot(j == away), across)).astype(BF16)

        chunks(length, part, arrange)

    if alone:
        first()
    else:
        pl.when(pl.program_id(0) == 0)(first)

    together = 2 if block % 2 == 0 else 1
    copies = []

    def finish(start):
        here = pl.ds(start, part)
        update = dot(right[here, :], mixed[...])
        for n, r in enumerate(range(0, block, together)):
            x = []
            for q in range(r, r + together):
                columns = slice(q * lanes, (q + 1) * lanes)
                x.append(pair_one[q, here, :] + update[:, columns] * inverse[here, columns])
            x = jnp.concatenate(x, 0)
            normed = layer_norm(x, gain[...]).astype(BF16)
            hidden = jnp.maximum(dot(normed, widen[...]).astype(BF16), 0.0)
            x = (x + dot(hidden, narrow[...])).astype(BF16)
            for q in range(together):
                (held if alone else out)[r + q, here, :] = x[q * part : (q + 1) * part]
            if alone:
                done = pl.ds(r, together)
                copies.append(pltpu.make_async_copy(held.at[done], out.at[done], sems.at[n]))
                copies[-1].start()

    chunks(length, part, finish)
    for copy in copies:
        copy.wait()


def finish_call(idx, near, across, mixed, inverse, pair_one, gain, widen, narrow, sub, far):
    rows, length, lanes = pair_one.shape
    block = rows if length <= 320 else 2 if rows % 2 == 0 else 1
    product = mixed.shape[0]
    gain = gain[None, :]
    if block == rows:
        grid, spec = {}, lambda shape, index: pl.BlockSpec(memory_space=pltpu.VMEM)
        out_spec = pl.BlockSpec(memory_space=pl.ANY)
    else:
        grid, spec = {"grid": (rows // block,)}, pl.BlockSpec
        out_spec = spec((block, length, lanes), lambda s: (s, 0, 0))
    whole = lambda a: spec(a.shape, lambda s: (0,) * a.ndim)
    return pl.pallas_call(
        functools.partial(
            finish_kernel, pieces=len(near), sub=sub, far=far, rows=rows, length=length, block=block
        ),
        **grid,
        in_specs=[
            pl.BlockSpec(memory_space=pltpu.SMEM),
            *[whole(a) for a in near + across],
            spec((product, block * lanes), lambda s: (0, s)),
            spec((length, block * lanes), lambda s: (0, s)),
            spec((block, length, lanes), lambda s: (s, 0, 0)),
            whole(gain),
            whole(widen),
            whole(narrow),
        ],
        out_specs=out_spec,
        out_shape=jax.ShapeDtypeStruct((rows, length, lanes), BF16),
        scratch_shapes=[
            pltpu.VMEM((length, product), BF16),
            pltpu.VMEM((rows, length, lanes) if block == rows else (1, 16, 128), BF16),
            pltpu.SemaphoreType.DMA((rows,)),
        ],
        compiler_params=pltpu.CompilerParams(vmem_limit_bytes=vmem_limit(length)),
        cost_estimate=pl.CostEstimate(flops=4 * 10**9, bytes_accessed=4000000, transcendentals=10**5),
        name="pair_update",
    )(idx, *near, *across, mixed, inverse, pair_one, gain, widen, narrow)


def on_device(
    devices,
    alignment_embedding,
    couple_embedding,
    amino_strand,
    amino_validity,
    alignment_validity,
    separation_embedding,
    couple_shift_scaling,
    couple_shift_factors,
    horizontal_scaling_factor,
    horizontal_entry_factors,
    horizontal_exit_factors,
    vertical_scaling_factor,
    vertical_entry_factors,
    vertical_exit_factors,
    alignment_feedforward_scaling,
    alignment_widen_factors,
    alignment_narrow_factors,
    product_scaling_factor,
    product_twin_factors,
    product_exit_factors,
    couple_feedforward_scaling,
    couple_widen_factors,
    couple_narrow_factors,
):
    far = devices // SUB
    idx = lax.axis_index("dap").astype(jnp.int32).reshape(1)

    def swap(x, distance):
        return lax.ppermute(x, "dap", [(d, d ^ distance) for d in range(devices)])

    width = alignment_embedding.shape[2]
    rows = couple_embedding.shape[0]
    depth = alignment_validity.shape[0]

    near = [swap(alignment_embedding, k) for k in range(2, SUB, 2)]
    pair_one, bias = pair_call(
        idx, amino_strand, couple_embedding, separation_embedding, couple_shift_scaling, couple_shift_factors
    )
    entry = horizontal_entry_factors.reshape(width, 4 * width)
    order, distance = [0], far // 2
    mine, theirs = bias, swap(bias, SUB * distance)
    order += [b ^ distance for b in order]
    while distance > 1:
        distance //= 2
        mine = jnp.concatenate([mine, theirs], 0)
        theirs = swap(mine, SUB * distance)
        order += [b ^ distance for b in order]
    near = jnp.concatenate([alignment_embedding, *near], 0)
    entry, mine, near = lax.optimization_barrier((entry, mine, near))
    across = swap(near, 1)
    projected = project_call(idx, [near, across], horizontal_scaling_factor, entry, far, rows)
    sent = row_call(
        idx, [mine, theirs], order, projected, alignment_validity, amino_validity, horizontal_exit_factors
    )
    pieces = [swap(sent[k], SUB * k) for k in [*range(2, far), 1]]
    pieces = lax.optimization_barrier(pieces)
    pieces = [sent[0]] + [part for _, part in sorted(zip([*range(2, far), 1], pieces), key=lambda pair: pair[0])]
    updated, left, right = column_call(
        idx,
        pieces,
        alignment_validity,
        vertical_scaling_factor,
        vertical_entry_factors.reshape(width, 4 * width),
        vertical_exit_factors,
        alignment_feedforward_scaling,
        alignment_widen_factors,
        alignment_narrow_factors,
        product_scaling_factor,
        product_twin_factors,
    )
    channels = left.shape[1]
    right = right.reshape(rows, channels * depth)
    factors = product_exit_factors.reshape(channels, -1)
    mixed, inverse = mix_call(idx, left, factors, alignment_validity, rows)
    parts = [swap(right, SUB * k) for k in [1, *range(far - 1, 1, -1)]]
    mixed, right, *parts = lax.optimization_barrier((mixed, right, *parts))
    parts = [right] + [part for _, part in sorted(zip([1, *range(far - 1, 1, -1)], parts), key=lambda pair: pair[0])]
    column = jnp.concatenate(parts, 0)
    near = [swap(column, k) for k in [6, 2, 4]]
    near = lax.optimization_barrier(near)
    near = [part for _, part in sorted(zip([6, 2, 4], near), key=lambda pair: pair[0])]
    near = [column, jnp.concatenate(near, 0)]
    across = [swap(a, 1) for a in near]
    updated_pairs = finish_call(
        idx,
        near,
        across,
        mixed,
        inverse,
        pair_one,
        couple_feedforward_scaling,
        couple_widen_factors,
        couple_narrow_factors,
        SUB,
        far,
    )
    return updated.transpose(1, 0, 2), updated_pairs


def solution(mesh):
    split = P("dap", None, None)
    return jax.shard_map(
        functools.partial(on_device, mesh.shape["dap"]),
        mesh=mesh,
        in_specs=(split, split) + (P(),) * 21,
        out_specs=(P(None, "dap", None), split),
        check_vma=False,
    )
```

```python
import functools

import jax
import jax.numpy as jnp
from jax import lax
from jax.experimental import pallas as pl
from jax.experimental.pallas import tpu as pltpu
from jax.sharding import PartitionSpec as P

HEADS = 8
SUB = 8
EPS = 1e-05
OUTER_EPS = 0.001
MASKED = -1000000000.0
LOG2E = 1.4426950408889634
F32 = jnp.float32
BF16 = jnp.bfloat16


def vmem_limit(length):
    return (16 if length is not None and length <= 320 else 56) * 1024 * 1024


def dot(a, b):
    return jnp.dot(a, b, preferred_element_type=F32)


def dot_nt(a, b):
    return lax.dot_general(a, b, (((1,), (1,)), ((), ())), preferred_element_type=F32)


def dot_tn(a, b):
    return lax.dot_general(a, b, (((0,), (0,)), ((), ())), preferred_element_type=F32)


def layer_norm(x, gain):
    centred = x - jnp.mean(x, -1, keepdims=True)
    spread = jnp.mean(centred * centred, -1, keepdims=True)
    return centred * lax.rsqrt(spread + EPS) * gain


def iota(shape, dim):
    return lax.broadcasted_iota(jnp.int32, shape, dim)


def div_const(x, d, limit):
    m = 65536 // d + 1
    assert all((v * m) >> 16 == v // d for v in range(limit)) and limit * m < 2**31
    return (x * m) >> 16


def one_hot(match):
    return jnp.where(match, 1.0, 0.0).astype(BF16)


def chunks(total, step, body):
    if total == step:
        body(0)
    else:
        lax.fori_loop(0, total // step, lambda c, x: (body(pl.multiple_of(c * step, step)), x)[1], 0)


def pair_kernel(
    idx, chain, pair, chain_row, table, gain, factors, pair_one, bias, shifted, chain_wide, *, rows, length, bins
):
    step = pl.program_id(0)
    reach = (bins - 2) // 2

    @pl.when(step == 0)
    def _():
        k = iota((2 * length, bins), 0)
        wanted = jnp.clip(length - k + reach, 0, 2 * reach)
        pick = one_hot(wanted == iota((2 * length, bins), 1))
        rest, total = table[...], 0.0
        for _ in range(3):
            part = rest.astype(BF16)
            total += dot(pick, part)
            rest = rest - part.astype(F32)
        shifted[...] = total
        eye = iota((length, length), 0) == iota((length, length), 1)
        column = jnp.sum(jnp.where(eye, chain_row[...].astype(F32).reshape(1, length), 0.0), axis=1, keepdims=True)
        chain_wide[...] = jnp.broadcast_to(column, chain_wide.shape)

    other = table[bins - 1 : bins, :]
    block = pair.shape[0]
    for r in range(block):
        i = idx[0] * rows + step * block + r
        near = shifted[pl.ds(length - i, length), :]
        same = chain_wide[...] == chain[i].astype(F32)
        x = pair[r].astype(F32) + jnp.where(same, near, other)
        pair_one[r] = x
        normed = layer_norm(x, gain[...]).astype(BF16)
        bias[r] = dot_nt(factors[...], normed).astype(BF16)


def pair_call(idx, chain, pair, table, gain, factors):
    rows, length, depth = pair.shape
    block = 5 if rows % 5 == 0 else 1
    bins = table.shape[0]
    smem = pl.BlockSpec(memory_space=pltpu.SMEM)
    whole = lambda *shape: pl.BlockSpec(shape, lambda s: (0,) * len(shape))
    return pl.pallas_call(
        functools.partial(pair_kernel, rows=rows, length=length, bins=bins),
        grid=(rows // block,),
        in_specs=[
            smem,
            smem,
            pl.BlockSpec((block, length, depth), lambda s: (s, 0, 0)),
            whole(length),
            whole(bins, depth),
            whole(1, depth),
            whole(HEADS, depth),
        ],
        out_specs=[
            pl.BlockSpec((block, length, depth), lambda s: (s, 0, 0)),
            pl.BlockSpec((block, HEADS, length), lambda s: (s, 0, 0)),
        ],
        out_shape=[
            jax.ShapeDtypeStruct((rows, length, depth), F32),
            jax.ShapeDtypeStruct((rows, HEADS, length), BF16),
        ],
        scratch_shapes=[pltpu.VMEM((2 * length, depth), F32), pltpu.VMEM((length, depth), F32)],
        compiler_params=pltpu.CompilerParams(vmem_limit_bytes=vmem_limit(None)),
        cost_estimate=pl.CostEstimate(flops=4 * 10**9, bytes_accessed=4000000, transcendentals=10**5),
        name="pair_bias",
    )(idx, chain, pair, chain, table, gain[None, :], factors.T)


def project_kernel(idx, *refs, sub, far, rows, length, width):
    row_refs, refs = refs[:2], refs[2:]
    gain, entry, keys, values, query, gate, own_rows, own_normed = refs
    me = idx[0]
    z, p = me // sub, me % sub
    own = far * rows
    scale = (width // HEADS) ** -0.5 * LOG2E

    r = iota((own, length), 0)
    block = div_const(r, rows, own)
    residue = ((z ^ block) * sub + p) * rows + r - block * rows
    pick = one_hot(residue == iota((own, length), 1))

    step = min(length, 320)
    for k in range(sub):
        source, place = row_refs[k % 2], k // 2

        def project(start, k=k, source=source, place=place):
            x = source[place, pl.ds(start, step), :]
            normed = layer_norm(x.astype(F32), gain[...]).astype(BF16)
            both = dot(normed, entry[:, width : 3 * width])
            keys[k, pl.ds(start, step), :] = both[:, :width].astype(BF16)
            values[k, pl.ds(start, step), :] = both[:, width:].astype(BF16)
            part = pick if length == step else one_hot(residue[:, :step] == iota((own, step), 1) + start)
            q_rows, a_rows = dot(part, normed), dot(part, x)
            here = pl.ds(k * own, own)
            if length == step:
                own_normed[here, :] = q_rows
                own_rows[here, :] = a_rows
            else:
                fresh = start == 0
                own_normed[here, :] = q_rows + jnp.where(fresh, 0.0, own_normed[here, :])
                own_rows[here, :] = a_rows + jnp.where(fresh, 0.0, own_rows[here, :])

        chunks(length, step, project)

    total = sub * own
    part = min(total, 320)

    def queries(start):
        here = pl.ds(start, part)
        normed = own_normed[here, :].astype(BF16)
        query[here, :] = dot(normed, entry[:, :width]) * scale
        gate[here, :] = jax.nn.sigmoid(dot(normed, entry[:, 3 * width :]))

    chunks(total, part, queries)


def project_call(idx, msa_rows, gain, entry, far, rows):
    sub = SUB
    _, length, width = msa_rows[0].shape
    own = far * rows
    vmem = pl.BlockSpec(memory_space=pltpu.VMEM)
    wide = jax.ShapeDtypeStruct((sub, length, width), BF16)
    narrow = jax.ShapeDtypeStruct((sub * own, width), F32)
    return pl.pallas_call(
        functools.partial(project_kernel, sub=sub, far=far, rows=rows, length=length, width=width),
        in_specs=[pl.BlockSpec(memory_space=pltpu.SMEM)] + [vmem] * 4,
        out_specs=[vmem] * 5,
        out_shape=[wide, wide, narrow, narrow, narrow],
        scratch_shapes=[pltpu.VMEM((sub * own, width), F32)],
        compiler_params=pltpu.CompilerParams(vmem_limit_bytes=vmem_limit(length)),
        cost_estimate=pl.CostEstimate(flops=3 * 10**9, bytes_accessed=4000000, transcendentals=10**5),
        name="row_project",
    )(idx, *msa_rows, gain[None, :], entry)


def row_kernel(idx, *refs, order, sub, far, rows, length, width):
    bias_refs, refs = refs[:2], refs[2:]
    keys, values, query, gate, own_rows, validity, amino, exit_ = refs[:8]
    outs, refs = refs[8 : 8 + far], refs[8 + far :]
    by_residue, bias, gated = refs
    me = idx[0]
    z, p = me // sub, me % sub
    own = far * rows
    total = sub * own
    half = far // 2
    for n, b in enumerate(order):
        block = bias_refs[n // half][n % half * rows : (n % half + 1) * rows]
        by_residue[b * rows : (b + 1) * rows] = block.astype(F32) * LOG2E
    for h in range(HEADS):
        bias[h] = by_residue[:, h, :]

    channel = width // HEADS
    head_of = iota((1, width), 1) // channel
    head_mask = [jnp.where(head_of == h, 1.0, 0.0) for h in range(HEADS)]
    take = 40 if own % 40 == 0 else rows

    def attend(n, k, start):
        s = z * sub + (p ^ k)
        valid = validity[pl.ds(s, 1), :] * amino[...].reshape(1, length)
        masked = jnp.where(valid > 0, 0.0, MASKED)
        here = pl.ds(pl.multiple_of(n * take, take), take) if not isinstance(n, int) else pl.ds(n * take, take)
        q = query[here, :]
        q = jnp.concatenate([q * mask for mask in head_mask], 0).astype(BF16)
        scores = dot_nt(q, keys[k]) + bias[:, pl.ds(start, take), :].reshape(HEADS * take, length) + masked
        expo = jnp.exp2(scores - jnp.max(scores, -1, keepdims=True))
        share = 1.0 / jnp.sum(expo, -1, keepdims=True)
        mixed = dot(expo.astype(BF16), values[k]) * share
        merged = mixed[:take] * head_mask[0]
        for h in range(1, HEADS):
            merged += mixed[h * take : (h + 1) * take] * head_mask[h]
        gated[here, :] = merged * gate[here, :]

    parts = own // take
    if parts == 1:
        for k in range(sub):
            attend(k, k, 0)
    else:
        lax.fori_loop(0, sub * parts, lambda n, x: (attend(n, n // parts, (n % parts) * take), x)[1], 0)

    piece = rows * sub
    for b in range(far):
        q = iota((piece, total), 0) + b * piece
        residue_, row = div_const(q, sub, total), q & (sub - 1)
        swap = one_hot((row ^ p) * own + residue_ == iota((piece, total), 1))
        gated_rows = dot(swap, gated[...].astype(BF16)).astype(BF16)
        x = dot(swap, own_rows[...].astype(BF16)) + dot(gated_rows, exit_[...])
        outs[b][...] = x.astype(BF16).reshape(rows, sub, width)


def row_call(idx, bias_halves, order, projected, validity, amino, exit_):
    keys, values, query, gate, own_rows = projected
    sub, far = keys.shape[0], len(order)
    _, length, width = keys.shape
    rows = 2 * bias_halves[0].shape[0] // far
    own = far * rows
    vmem = pl.BlockSpec(memory_space=pltpu.VMEM)
    return pl.pallas_call(
        functools.partial(row_kernel, order=order, sub=sub, far=far, rows=rows, length=length, width=width),
        in_specs=[pl.BlockSpec(memory_space=pltpu.SMEM)] + [vmem] * 10,
        out_specs=[vmem] * far,
        out_shape=[jax.ShapeDtypeStruct((rows, sub, width), BF16)] * far,
        scratch_shapes=[
            pltpu.VMEM((own, HEADS, length), F32),
            pltpu.VMEM((HEADS, own, length), F32),
            pltpu.VMEM((sub * own, width), F32),
        ],
        compiler_params=pltpu.CompilerParams(vmem_limit_bytes=vmem_limit(length)),
        cost_estimate=pl.CostEstimate(flops=4 * 10**9, bytes_accessed=4000000, transcendentals=10**5),
        name="row_attention",
    )(idx, *bias_halves, keys, values, query, gate, own_rows, validity, amino, exit_)


def column_kernel(idx, *refs, sub, far, rows, block, depth, width):
    piece_refs, refs = refs[:far], refs[far:]
    entry, twin, *sources = refs[:9]
    updated, left, right, start_rows, gated, *held = refs[9:-1]
    sems = refs[-1]
    copies = [pltpu.make_async_copy(src, dst, sems.at[n]) for n, (src, dst) in enumerate(zip(sources, held))]
    steps = rows // block

    def begin():
        for copy in copies:
            copy.start()

    def arrived(*which):
        def wait():
            for n in which:
                copies[n].wait()

        if steps == 1:
            wait()
        else:
            pl.when(pl.program_id(0) == 0)(wait)
        return [held[n][...] for n in which]

    if steps == 1:
        begin()
    else:
        pl.when(pl.program_id(0) == 0)(begin)
    me = idx[0]
    z = me // sub
    first = me * rows + (0 if steps == 1 else pl.program_id(0) * block)
    scale = (width // HEADS) ** -0.5 * LOG2E
    total = block * depth
    for b in range(far):
        here = pl.ds(pl.multiple_of((z ^ b) * sub, sub), sub)
        start_rows[:, here, :] = piece_refs[b][...].astype(F32)
    x = start_rows[...].reshape(total, width)
    (col_gain,) = arrived(0)
    normed = layer_norm(x, col_gain).astype(BF16)
    proj = dot(normed, entry[...])
    query = proj[:, :width] * scale
    keys = proj[:, width : 2 * width].astype(BF16)
    values = proj[:, 2 * width : 3 * width].astype(BF16)
    gate = jax.nn.sigmoid(proj[:, 3 * width :])

    (validity,) = arrived(1)
    length = validity.shape[1]
    lanes = 128
    pick = one_hot(iota((length, lanes), 0) == first + iota((length, lanes), 1))
    valid = dot(validity.astype(F32).astype(BF16), pick)
    head_of = iota((1, width), 1) // (width // HEADS)
    head_mask = [jnp.where(head_of == h, 1.0, 0.0) for h in range(HEADS)]
    for i in range(block):
        here = slice(i * depth, (i + 1) * depth)
        q = jnp.concatenate([query[here] * mask for mask in head_mask], 0).astype(BF16)
        masked = jnp.where(valid[:, i : i + 1] > 0, 0.0, MASKED)
        scores = dot_nt(keys[here], q) + masked
        expo = jnp.exp2(scores - jnp.max(scores, 0, keepdims=True))
        weights = (expo * (1.0 / jnp.sum(expo, 0, keepdims=True))).astype(BF16)
        mixed = dot_tn(weights, values[here])
        merged = mixed[:depth] * head_mask[0]
        for h in range(1, HEADS):
            merged += mixed[h * depth : (h + 1) * depth] * head_mask[h]
        gated[here, :] = merged * gate[here]
    exit_, ff_gain, widen, narrow, product_gain = arrived(2, 3, 4, 5, 6)
    x = x + dot(gated[...].astype(BF16), exit_)
    hidden = jnp.maximum(dot(layer_norm(x, ff_gain).astype(BF16), widen).astype(BF16), 0.0)
    x = x + dot(hidden, narrow)
    updated[...] = x.astype(BF16).reshape(block, depth, width)
    outer = layer_norm(x, product_gain).astype(BF16)
    both = dot(outer, twin[...])
    channels = twin.shape[1] // 2
    spread = iota((depth, channels * depth), 1)
    channel = spread // depth
    repeat = one_hot(
        iota((2 * channels, channels * depth), 0) - channels == iota((2 * channels, channels * depth), 1) // depth
    )
    mine = jnp.where(spread - channel * depth == iota((depth, channels * depth), 0), 1.0, 0.0)
    for i in range(block):
        here = slice(i * depth, (i + 1) * depth)
        part = (both[here] * valid[:, i : i + 1]).astype(BF16)
        left[here, :] = part[:, :channels]
        right[0, i : i + 1, :] = jnp.sum(dot(part, repeat) * mine, axis=0, keepdims=True).astype(BF16)


def column_call(idx, pieces, validity, col_gain, entry, exit_, ff_gain, widen, narrow, product_gain, twin):
    far = len(pieces)
    rows, sub, width = pieces[0].shape
    depth, length = validity.shape
    block = rows
    while block * depth > 320 and block % 2 == 0:
        block //= 2
    channels = twin.shape[1] // 2
    steps = rows // block
    here = [entry, twin]
    sources = [
        col_gain[None, :],
        validity,
        exit_,
        ff_gain[None, :],
        widen,
        narrow,
        product_gain[None, :],
    ]
    if steps == 1:
        grid, spec = {}, lambda shape, index: pl.BlockSpec(memory_space=pltpu.VMEM)
    else:
        grid, spec = {"grid": (steps,)}, pl.BlockSpec
    return pl.pallas_call(
        functools.partial(column_kernel, sub=sub, far=far, rows=rows, block=block, depth=depth, width=width),
        **grid,
        in_specs=[pl.BlockSpec(memory_space=pltpu.SMEM)]
        + [spec((block, sub, width), lambda s: (s, 0, 0))] * far
        + [spec(a.shape, lambda s: (0, 0)) for a in here]
        + [pl.BlockSpec(memory_space=pltpu.HBM)] * len(sources),
        out_specs=[
            spec((block, depth, width), lambda s: (s, 0, 0)),
            spec((block * depth, channels), lambda s: (s, 0)),
            spec((1, block, channels * depth), lambda s: (s, 0, 0)),
        ],
        out_shape=[
            jax.ShapeDtypeStruct((rows, depth, width), BF16),
            jax.ShapeDtypeStruct((rows * depth, channels), BF16),
            jax.ShapeDtypeStruct((steps, block, channels * depth), BF16),
        ],
        scratch_shapes=[pltpu.VMEM((block, depth, width), F32), pltpu.VMEM((block * depth, width), F32)]
        + [pltpu.VMEM(a.shape, a.dtype) for a in sources]
        + [pltpu.SemaphoreType.DMA((len(sources),))],
        compiler_params=pltpu.CompilerParams(vmem_limit_bytes=vmem_limit(length)),
        cost_estimate=pl.CostEstimate(flops=5 * 10**9, bytes_accessed=4000000, transcendentals=10**5),
        name="column_attention",
    )(idx, *pieces, *here, *sources)


def mix_kernel(idx, left, factors, validity, out, inverse, *, rows, depth, steps):
    lanes = out.shape[1] // rows
    for e in range(0, out.shape[0] // depth, 2):
        y = dot(left[...], factors[:, e * lanes : (e + 2) * lanes]).astype(BF16)
        for i in range(rows):
            for f in range(2):
                block = y[i * depth : (i + 1) * depth, f * lanes : (f + 1) * lanes]
                out[(e + f) * depth : (e + f + 1) * depth, i * lanes : (i + 1) * lanes] = block

    def count():
        length = validity.shape[1]
        valid = validity[...].astype(F32)
        target = idx[0] * rows + iota((length, rows * lanes), 1) // lanes
        mine = dot(valid.astype(BF16), one_hot(iota((length, rows * lanes), 0) == target))
        mine, turned = mine.astype(BF16), valid.T.astype(BF16)
        part = min(length, 320)
        for start in range(0, length, part):
            inverse[start : start + part, :] = 1.0 / (dot(turned[start : start + part], mine) + OUTER_EPS)

    if steps == 1:
        count()
    else:
        pl.when(pl.program_id(0) == 0)(count)


def mix_call(idx, left, factors, validity, rows):
    total, channels = left.shape
    depth, length = validity.shape
    lanes = factors.shape[1] // channels
    steps = 1 if length <= 320 else 4
    block = channels // steps
    if steps == 1:
        grid, spec = {}, lambda shape, index: pl.BlockSpec(memory_space=pltpu.VMEM)
    else:
        grid, spec = {"grid": (steps,)}, pl.BlockSpec
    return pl.pallas_call(
        functools.partial(mix_kernel, rows=rows, depth=depth, steps=steps),
        **grid,
        in_specs=[
            pl.BlockSpec(memory_space=pltpu.SMEM),
            spec((total, channels), lambda s: (0, 0)),
            spec((channels, block * lanes), lambda s: (0, s)),
            spec((depth, length), lambda s: (0, 0)),
        ],
        out_specs=[
            spec((block * depth, rows * lanes), lambda s: (s, 0)),
            spec((length, rows * lanes), lambda s: (0, 0)),
        ],
        out_shape=[
            jax.ShapeDtypeStruct((channels * depth, rows * lanes), BF16),
            jax.ShapeDtypeStruct((length, rows * lanes), F32),
        ],
        compiler_params=pltpu.CompilerParams(vmem_limit_bytes=vmem_limit(length)),
        cost_estimate=pl.CostEstimate(flops=2 * 10**9, bytes_accessed=4000000, transcendentals=10**5),
        name="left_mix",
    )(idx, left, factors, validity)


def finish_kernel(idx, *refs, pieces, sub, far, rows, length, block):
    near_refs, across_refs, refs = refs[:pieces], refs[pieces : 2 * pieces], refs[2 * pieces :]
    mixed, inverse, pair_one, gain, widen, narrow, out, right, held, sems = refs
    me = idx[0]
    z, p = me // sub, me % sub
    half = far * rows * sub // 2
    lanes = pair_one.shape[2]
    part = min(length, 320)
    alone = block == rows

    def first():
        r = iota((part, half), 1)
        b = div_const(r, rows, half)
        i = r - b * rows
        across_sub = 2 * div_const(b, far, half // rows)
        across_far = b - far * (across_sub >> 1)
        core = jnp.where(across_sub > 0, 1, 0) ^ jnp.where(across_far > 0, 1, 0)
        home = ((z ^ across_far) * sub + (p ^ across_sub ^ core)) * rows + i
        away = ((z ^ across_far) * sub + (p ^ 1 ^ across_sub ^ core)) * rows + i
        near = jnp.concatenate([ref[...].astype(F32) for ref in near_refs], 0).astype(BF16)
        across = jnp.concatenate([ref[...].astype(F32) for ref in across_refs], 0).astype(BF16)

        def arrange(start):
            j = iota((part, half), 0) + start
            here = pl.ds(start, part)
            right[here, :] = (dot(one_hot(j == home), near) + dot(one_hot(j == away), across)).astype(BF16)

        chunks(length, part, arrange)

    if alone:
        first()
    else:
        pl.when(pl.program_id(0) == 0)(first)

    together = 2 if block % 2 == 0 else 1
    copies = []

    def finish(start):
        here = pl.ds(start, part)
        update = dot(right[here, :], mixed[...])
        for n, r in enumerate(range(0, block, together)):
            x = []
            for q in range(r, r + together):
                columns = slice(q * lanes, (q + 1) * lanes)
                x.append(pair_one[q, here, :] + update[:, columns] * inverse[here, columns])
            x = jnp.concatenate(x, 0)
            normed = layer_norm(x, gain[...]).astype(BF16)
            hidden = jnp.maximum(dot(normed, widen[...]).astype(BF16), 0.0)
            x = (x + dot(hidden, narrow[...])).astype(BF16)
            for q in range(together):
                (held if alone else out)[r + q, here, :] = x[q * part : (q + 1) * part]
            if alone:
                done = pl.ds(r, together)
                copies.append(pltpu.make_async_copy(held.at[done], out.at[done], sems.at[n]))
                copies[-1].start()

    chunks(length, part, finish)
    for copy in copies:
        copy.wait()


def finish_call(idx, near, across, mixed, inverse, pair_one, gain, widen, narrow, sub, far):
    rows, length, lanes = pair_one.shape
    block = rows if length <= 320 else 2 if rows % 2 == 0 else 1
    product = mixed.shape[0]
    gain = gain[None, :]
    if block == rows:
        grid, spec = {}, lambda shape, index: pl.BlockSpec(memory_space=pltpu.VMEM)
        out_spec = pl.BlockSpec(memory_space=pl.ANY)
    else:
        grid, spec = {"grid": (rows // block,)}, pl.BlockSpec
        out_spec = spec((block, length, lanes), lambda s: (s, 0, 0))
    whole = lambda a: spec(a.shape, lambda s: (0,) * a.ndim)
    return pl.pallas_call(
        functools.partial(
            finish_kernel, pieces=len(near), sub=sub, far=far, rows=rows, length=length, block=block
        ),
        **grid,
        in_specs=[
            pl.BlockSpec(memory_space=pltpu.SMEM),
            *[whole(a) for a in near + across],
            spec((product, block * lanes), lambda s: (0, s)),
            spec((length, block * lanes), lambda s: (0, s)),
            spec((block, length, lanes), lambda s: (s, 0, 0)),
            whole(gain),
            whole(widen),
            whole(narrow),
        ],
        out_specs=out_spec,
        out_shape=jax.ShapeDtypeStruct((rows, length, lanes), BF16),
        scratch_shapes=[
            pltpu.VMEM((length, product), BF16),
            pltpu.VMEM((rows, length, lanes) if block == rows else (1, 16, 128), BF16),
            pltpu.SemaphoreType.DMA((rows,)),
        ],
        compiler_params=pltpu.CompilerParams(vmem_limit_bytes=vmem_limit(length)),
        cost_estimate=pl.CostEstimate(flops=4 * 10**9, bytes_accessed=4000000, transcendentals=10**5),
        name="pair_update",
    )(idx, *near, *across, mixed, inverse, pair_one, gain, widen, narrow)


def on_device(
    devices,
    alignment_embedding,
    couple_embedding,
    amino_strand,
    amino_validity,
    alignment_validity,
    separation_embedding,
    couple_shift_scaling,
    couple_shift_factors,
    horizontal_scaling_factor,
    horizontal_entry_factors,
    horizontal_exit_factors,
    vertical_scaling_factor,
    vertical_entry_factors,
    vertical_exit_factors,
    alignment_feedforward_scaling,
    alignment_widen_factors,
    alignment_narrow_factors,
    product_scaling_factor,
    product_twin_factors,
    product_exit_factors,
    couple_feedforward_scaling,
    couple_widen_factors,
    couple_narrow_factors,
):
    far = devices // SUB
    idx = lax.axis_index("dap").astype(jnp.int32).reshape(1)

    def swap(x, distance):
        return lax.ppermute(x, "dap", [(d, d ^ distance) for d in range(devices)])

    width = alignment_embedding.shape[2]
    rows = couple_embedding.shape[0]
    depth = alignment_validity.shape[0]

    near = [swap(alignment_embedding, k) for k in range(2, SUB, 2)]
    pair_one, bias = pair_call(
        idx, amino_strand, couple_embedding, separation_embedding, couple_shift_scaling, couple_shift_factors
    )
    entry = horizontal_entry_factors.reshape(width, 4 * width)
    order, distance = [0], far // 2
    mine, theirs = bias, swap(bias, SUB * distance)
    order += [b ^ distance for b in order]
    while distance > 1:
        distance //= 2
        mine = jnp.concatenate([mine, theirs], 0)
        theirs = swap(mine, SUB * distance)
        order += [b ^ distance for b in order]
    near = jnp.concatenate([alignment_embedding, *near], 0)
    entry, mine, near = lax.optimization_barrier((entry, mine, near))
    across = swap(near, 1)
    projected = project_call(idx, [near, across], horizontal_scaling_factor, entry, far, rows)
    sent = row_call(
        idx, [mine, theirs], order, projected, alignment_validity, amino_validity, horizontal_exit_factors
    )
    pieces = [swap(sent[k], SUB * k) for k in [*range(2, far), 1]]
    pieces = lax.optimization_barrier(pieces)
    pieces = [sent[0]] + [part for _, part in sorted(zip([*range(2, far), 1], pieces), key=lambda pair: pair[0])]
    updated, left, right = column_call(
        idx,
        pieces,
        alignment_validity,
        vertical_scaling_factor,
        vertical_entry_factors.reshape(width, 4 * width),
        vertical_exit_factors,
        alignment_feedforward_scaling,
        alignment_widen_factors,
        alignment_narrow_factors,
        product_scaling_factor,
        product_twin_factors,
    )
    channels = left.shape[1]
    right = right.reshape(rows, channels * depth)
    factors = product_exit_factors.reshape(channels, -1)
    mixed, inverse = mix_call(idx, left, factors, alignment_validity, rows)
    parts = [swap(right, SUB * k ^ 1) for k in [*range(2, far), 1]]
    mixed, right, *parts = lax.optimization_barrier((mixed, right, *parts))
    parts = [right] + [part for _, part in sorted(zip([*range(2, far), 1], parts), key=lambda pair: pair[0])]
    column = jnp.concatenate(parts, 0)
    near = [swap(column, k ^ 1) for k in [6, 2, 4]]
    near = lax.optimization_barrier(near)
    near = [part for _, part in sorted(zip([6, 2, 4], near), key=lambda pair: pair[0])]
    near = [column, jnp.concatenate(near, 0)]
    across = [swap(a, 1) for a in near]
    updated_pairs = finish_call(
        idx,
        near,
        across,
        mixed,
        inverse,
        pair_one,
        couple_feedforward_scaling,
        couple_widen_factors,
        couple_narrow_factors,
        SUB,
        far,
    )
    return updated.transpose(1, 0, 2), updated_pairs


def solution(mesh):
    split = P("dap", None, None)
    return jax.shard_map(
        functools.partial(on_device, mesh.shape["dap"]),
        mesh=mesh,
        in_specs=(split, split) + (P(),) * 21,
        out_specs=(P(None, "dap", None), split),
        check_vma=False,
    )
```

```python
import functools

import jax
import jax.numpy as jnp
from jax import lax
from jax.experimental import pallas as pl
from jax.experimental.pallas import tpu as pltpu
from jax.sharding import PartitionSpec as P

HEADS = 8
SUB = 8
EPS = 1e-05
OUTER_EPS = 0.001
MASKED = -1000000000.0
LOG2E = 1.4426950408889634
F32 = jnp.float32
BF16 = jnp.bfloat16


def vmem_limit(length):
    return (16 if length is not None and length <= 320 else 56) * 1024 * 1024


def dot(a, b):
    return jnp.dot(a, b, preferred_element_type=F32)


def dot_nt(a, b):
    return lax.dot_general(a, b, (((1,), (1,)), ((), ())), preferred_element_type=F32)


def dot_tn(a, b):
    return lax.dot_general(a, b, (((0,), (0,)), ((), ())), preferred_element_type=F32)


def layer_norm(x, gain):
    centred = x - jnp.mean(x, -1, keepdims=True)
    spread = jnp.mean(centred * centred, -1, keepdims=True)
    return centred * lax.rsqrt(spread + EPS) * gain


def iota(shape, dim):
    return lax.broadcasted_iota(jnp.int32, shape, dim)


def div_const(x, d, limit):
    m = 65536 // d + 1
    assert all((v * m) >> 16 == v // d for v in range(limit)) and limit * m < 2**31
    return (x * m) >> 16


def one_hot(match):
    return jnp.where(match, 1.0, 0.0).astype(BF16)


def chunks(total, step, body):
    if total == step:
        body(0)
    else:
        lax.fori_loop(0, total // step, lambda c, x: (body(pl.multiple_of(c * step, step)), x)[1], 0)


def pair_kernel(
    idx, chain, pair, chain_row, table, gain, factors, pair_one, bias, shifted, chain_wide, *, rows, length, bins
):
    step = pl.program_id(0)
    reach = (bins - 2) // 2

    @pl.when(step == 0)
    def _():
        k = iota((2 * length, bins), 0)
        wanted = jnp.clip(length - k + reach, 0, 2 * reach)
        pick = one_hot(wanted == iota((2 * length, bins), 1))
        rest, total = table[...], 0.0
        for _ in range(3):
            part = rest.astype(BF16)
            total += dot(pick, part)
            rest = rest - part.astype(F32)
        shifted[...] = total
        eye = iota((length, length), 0) == iota((length, length), 1)
        column = jnp.sum(jnp.where(eye, chain_row[...].astype(F32).reshape(1, length), 0.0), axis=1, keepdims=True)
        chain_wide[...] = jnp.broadcast_to(column, chain_wide.shape)

    other = table[bins - 1 : bins, :]
    block = pair.shape[0]
    together = block
    for start in range(0, block, together):
        sums = []
        for r in range(start, start + together):
            i = idx[0] * rows + step * block + r
            near = shifted[pl.ds(length - i, length), :]
            same = chain_wide[...] == chain[i].astype(F32)
            x = pair[r].astype(F32) + jnp.where(same, near, other)
            pair_one[r] = x
            sums.append(x)
        normed = layer_norm(jnp.concatenate(sums, 0), gain[...]).astype(BF16)
        both = dot_nt(factors[...], normed).astype(BF16)
        for r in range(together):
            bias[start + r] = both[:, r * length : (r + 1) * length]


def pair_call(idx, chain, pair, table, gain, factors):
    rows, length, depth = pair.shape
    block = 5 if rows % 5 == 0 else 1
    bins = table.shape[0]
    smem = pl.BlockSpec(memory_space=pltpu.SMEM)
    whole = lambda *shape: pl.BlockSpec(shape, lambda s: (0,) * len(shape))
    return pl.pallas_call(
        functools.partial(pair_kernel, rows=rows, length=length, bins=bins),
        grid=(rows // block,),
        in_specs=[
            smem,
            smem,
            pl.BlockSpec((block, length, depth), lambda s: (s, 0, 0)),
            whole(length),
            whole(bins, depth),
            whole(1, depth),
            whole(HEADS, depth),
        ],
        out_specs=[
            pl.BlockSpec((block, length, depth), lambda s: (s, 0, 0)),
            pl.BlockSpec((block, HEADS, length), lambda s: (s, 0, 0)),
        ],
        out_shape=[
            jax.ShapeDtypeStruct((rows, length, depth), F32),
            jax.ShapeDtypeStruct((rows, HEADS, length), BF16),
        ],
        scratch_shapes=[pltpu.VMEM((2 * length, depth), F32), pltpu.VMEM((length, depth), F32)],
        compiler_params=pltpu.CompilerParams(vmem_limit_bytes=vmem_limit(None)),
        cost_estimate=pl.CostEstimate(flops=4 * 10**9, bytes_accessed=4000000, transcendentals=10**5),
        name="pair_bias",
    )(idx, chain, pair, chain, table, gain[None, :], factors.T)


def project_kernel(idx, *refs, sub, far, rows, length, width):
    row_refs, refs = refs[:2], refs[2:]
    gain, entry, keys, values, query, gate, own_rows, own_normed = refs
    me = idx[0]
    z, p = me // sub, me % sub
    own = far * rows
    scale = (width // HEADS) ** -0.5 * LOG2E

    r = iota((own, length), 0)
    block = div_const(r, rows, own)
    residue = ((z ^ block) * sub + p) * rows + r - block * rows
    pick = one_hot(residue == iota((own, length), 1))

    step = min(length, 320)
    for k in range(sub):
        source, place = row_refs[k % 2], k // 2

        def project(start, k=k, source=source, place=place):
            x = source[place, pl.ds(start, step), :]
            normed = layer_norm(x.astype(F32), gain[...]).astype(BF16)
            both = dot(normed, entry[:, width : 3 * width])
            keys[k, pl.ds(start, step), :] = both[:, :width].astype(BF16)
            values[k, pl.ds(start, step), :] = both[:, width:].astype(BF16)
            part = pick if length == step else one_hot(residue[:, :step] == iota((own, step), 1) + start)
            q_rows, a_rows = dot(part, normed), dot(part, x)
            here = pl.ds(k * own, own)
            if length == step:
                own_normed[here, :] = q_rows
                own_rows[here, :] = a_rows
            else:
                fresh = start == 0
                own_normed[here, :] = q_rows + jnp.where(fresh, 0.0, own_normed[here, :])
                own_rows[here, :] = a_rows + jnp.where(fresh, 0.0, own_rows[here, :])

        chunks(length, step, project)

    total = sub * own
    part = min(total, 320)

    def queries(start):
        here = pl.ds(start, part)
        normed = own_normed[here, :].astype(BF16)
        query[here, :] = dot(normed, entry[:, :width]) * scale
        gate[here, :] = jax.nn.sigmoid(dot(normed, entry[:, 3 * width :]))

    chunks(total, part, queries)


def project_call(idx, msa_rows, gain, entry, far, rows):
    sub = SUB
    _, length, width = msa_rows[0].shape
    own = far * rows
    vmem = pl.BlockSpec(memory_space=pltpu.VMEM)
    wide = jax.ShapeDtypeStruct((sub, length, width), BF16)
    narrow = jax.ShapeDtypeStruct((sub * own, width), F32)
    return pl.pallas_call(
        functools.partial(project_kernel, sub=sub, far=far, rows=rows, length=length, width=width),
        in_specs=[pl.BlockSpec(memory_space=pltpu.SMEM)] + [vmem] * 4,
        out_specs=[vmem] * 5,
        out_shape=[wide, wide, narrow, narrow, narrow],
        scratch_shapes=[pltpu.VMEM((sub * own, width), F32)],
        compiler_params=pltpu.CompilerParams(vmem_limit_bytes=vmem_limit(length)),
        cost_estimate=pl.CostEstimate(flops=3 * 10**9, bytes_accessed=4000000, transcendentals=10**5),
        name="row_project",
    )(idx, *msa_rows, gain[None, :], entry)


def row_kernel(idx, *refs, order, sub, far, rows, length, width):
    bias_refs, refs = refs[:2], refs[2:]
    keys, values, query, gate, own_rows, validity, amino, exit_ = refs[:8]
    outs, refs = refs[8 : 8 + far], refs[8 + far :]
    by_residue, bias, gated = refs
    me = idx[0]
    z, p = me // sub, me % sub
    own = far * rows
    total = sub * own
    half = far // 2
    for n, b in enumerate(order):
        block = bias_refs[n // half][n % half * rows : (n % half + 1) * rows]
        by_residue[b * rows : (b + 1) * rows] = block.astype(F32) * LOG2E
    for h in range(HEADS):
        bias[h] = by_residue[:, h, :]

    channel = width // HEADS
    head_of = iota((1, width), 1) // channel
    head_mask = [jnp.where(head_of == h, 1.0, 0.0) for h in range(HEADS)]
    take = 40 if own % 40 == 0 else rows

    def attend(n, k, start):
        s = z * sub + (p ^ k)
        valid = validity[pl.ds(s, 1), :] * amino[...].reshape(1, length)
        masked = jnp.where(valid > 0, 0.0, MASKED)
        here = pl.ds(pl.multiple_of(n * take, take), take) if not isinstance(n, int) else pl.ds(n * take, take)
        q = query[here, :]
        q = jnp.concatenate([q * mask for mask in head_mask], 0).astype(BF16)
        scores = dot_nt(q, keys[k]) + bias[:, pl.ds(start, take), :].reshape(HEADS * take, length) + masked
        expo = jnp.exp2(scores - jnp.max(scores, -1, keepdims=True))
        share = 1.0 / jnp.sum(expo, -1, keepdims=True)
        mixed = dot(expo.astype(BF16), values[k]) * share
        merged = mixed[:take] * head_mask[0]
        for h in range(1, HEADS):
            merged += mixed[h * take : (h + 1) * take] * head_mask[h]
        gated[here, :] = merged * gate[here, :]

    parts = own // take
    if parts == 1:
        for k in range(sub):
            attend(k, k, 0)
    else:
        lax.fori_loop(0, sub * parts, lambda n, x: (attend(n, n // parts, (n % parts) * take), x)[1], 0)

    piece = rows * sub
    for b in range(far):
        q = iota((piece, total), 0) + b * piece
        residue_, row = div_const(q, sub, total), q & (sub - 1)
        swap = one_hot((row ^ p) * own + residue_ == iota((piece, total), 1))
        gated_rows = dot(swap, gated[...].astype(BF16)).astype(BF16)
        x = dot(swap, own_rows[...].astype(BF16)) + dot(gated_rows, exit_[...])
        outs[b][...] = x.astype(BF16).reshape(rows, sub, width)


def row_call(idx, bias_halves, order, projected, validity, amino, exit_):
    keys, values, query, gate, own_rows = projected
    sub, far = keys.shape[0], len(order)
    _, length, width = keys.shape
    rows = 2 * bias_halves[0].shape[0] // far
    own = far * rows
    vmem = pl.BlockSpec(memory_space=pltpu.VMEM)
    return pl.pallas_call(
        functools.partial(row_kernel, order=order, sub=sub, far=far, rows=rows, length=length, width=width),
        in_specs=[pl.BlockSpec(memory_space=pltpu.SMEM)] + [vmem] * 10,
        out_specs=[vmem] * far,
        out_shape=[jax.ShapeDtypeStruct((rows, sub, width), BF16)] * far,
        scratch_shapes=[
            pltpu.VMEM((own, HEADS, length), F32),
            pltpu.VMEM((HEADS, own, length), F32),
            pltpu.VMEM((sub * own, width), F32),
        ],
        compiler_params=pltpu.CompilerParams(vmem_limit_bytes=vmem_limit(length)),
        cost_estimate=pl.CostEstimate(flops=4 * 10**9, bytes_accessed=4000000, transcendentals=10**5),
        name="row_attention",
    )(idx, *bias_halves, keys, values, query, gate, own_rows, validity, amino, exit_)


def column_kernel(idx, *refs, sub, far, rows, block, depth, width):
    piece_refs, refs = refs[:far], refs[far:]
    entry, twin, *sources = refs[:9]
    updated, left, right, start_rows, gated, *held = refs[9:-1]
    sems = refs[-1]
    copies = [pltpu.make_async_copy(src, dst, sems.at[n]) for n, (src, dst) in enumerate(zip(sources, held))]
    steps = rows // block

    def begin():
        for copy in copies:
            copy.start()

    def arrived(*which):
        def wait():
            for n in which:
                copies[n].wait()

        if steps == 1:
            wait()
        else:
            pl.when(pl.program_id(0) == 0)(wait)
        return [held[n][...] for n in which]

    if steps == 1:
        begin()
    else:
        pl.when(pl.program_id(0) == 0)(begin)
    me = idx[0]
    z = me // sub
    first = me * rows + (0 if steps == 1 else pl.program_id(0) * block)
    scale = (width // HEADS) ** -0.5 * LOG2E
    total = block * depth
    for b in range(far):
        here = pl.ds(pl.multiple_of((z ^ b) * sub, sub), sub)
        start_rows[:, here, :] = piece_refs[b][...].astype(F32)
    x = start_rows[...].reshape(total, width)
    (col_gain,) = arrived(0)
    normed = layer_norm(x, col_gain).astype(BF16)
    proj = dot(normed, entry[...])
    query = proj[:, :width] * scale
    keys = proj[:, width : 2 * width].astype(BF16)
    values = proj[:, 2 * width : 3 * width].astype(BF16)
    gate = jax.nn.sigmoid(proj[:, 3 * width :])

    (validity,) = arrived(1)
    length = validity.shape[1]
    lanes = 128
    pick = one_hot(iota((length, lanes), 0) == first + iota((length, lanes), 1))
    valid = dot(validity.astype(F32).astype(BF16), pick)
    head_of = iota((1, width), 1) // (width // HEADS)
    head_mask = [jnp.where(head_of == h, 1.0, 0.0) for h in range(HEADS)]
    for i in range(block):
        here = slice(i * depth, (i + 1) * depth)
        q = jnp.concatenate([query[here] * mask for mask in head_mask], 0).astype(BF16)
        masked = jnp.where(valid[:, i : i + 1] > 0, 0.0, MASKED)
        scores = dot_nt(keys[here], q) + masked
        expo = jnp.exp2(scores - jnp.max(scores, 0, keepdims=True))
        weights = (expo * (1.0 / jnp.sum(expo, 0, keepdims=True))).astype(BF16)
        mixed = dot_tn(weights, values[here])
        merged = mixed[:depth] * head_mask[0]
        for h in range(1, HEADS):
            merged += mixed[h * depth : (h + 1) * depth] * head_mask[h]
        gated[here, :] = merged * gate[here]
    exit_, ff_gain, widen, narrow, product_gain = arrived(2, 3, 4, 5, 6)
    x = x + dot(gated[...].astype(BF16), exit_)
    hidden = jnp.maximum(dot(layer_norm(x, ff_gain).astype(BF16), widen).astype(BF16), 0.0)
    x = x + dot(hidden, narrow)
    updated[...] = x.astype(BF16).reshape(block, depth, width)
    outer = layer_norm(x, product_gain).astype(BF16)
    both = dot(outer, twin[...])
    channels = twin.shape[1] // 2
    spread = iota((depth, channels * depth), 1)
    channel = spread // depth
    repeat = one_hot(
        iota((2 * channels, channels * depth), 0) - channels == iota((2 * channels, channels * depth), 1) // depth
    )
    mine = jnp.where(spread - channel * depth == iota((depth, channels * depth), 0), 1.0, 0.0)
    for i in range(block):
        here = slice(i * depth, (i + 1) * depth)
        part = (both[here] * valid[:, i : i + 1]).astype(BF16)
        left[here, :] = part[:, :channels]
        right[0, i : i + 1, :] = jnp.sum(dot(part, repeat) * mine, axis=0, keepdims=True).astype(BF16)


def column_call(idx, pieces, validity, col_gain, entry, exit_, ff_gain, widen, narrow, product_gain, twin):
    far = len(pieces)
    rows, sub, width = pieces[0].shape
    depth, length = validity.shape
    block = rows
    while block * depth > 320 and block % 2 == 0:
        block //= 2
    channels = twin.shape[1] // 2
    steps = rows // block
    here = [entry, twin]
    sources = [
        col_gain[None, :],
        validity,
        exit_,
        ff_gain[None, :],
        widen,
        narrow,
        product_gain[None, :],
    ]
    if steps == 1:
        grid, spec = {}, lambda shape, index: pl.BlockSpec(memory_space=pltpu.VMEM)
    else:
        grid, spec = {"grid": (steps,)}, pl.BlockSpec
    return pl.pallas_call(
        functools.partial(column_kernel, sub=sub, far=far, rows=rows, block=block, depth=depth, width=width),
        **grid,
        in_specs=[pl.BlockSpec(memory_space=pltpu.SMEM)]
        + [spec((block, sub, width), lambda s: (s, 0, 0))] * far
        + [spec(a.shape, lambda s: (0, 0)) for a in here]
        + [pl.BlockSpec(memory_space=pltpu.HBM)] * len(sources),
        out_specs=[
            spec((block, depth, width), lambda s: (s, 0, 0)),
            spec((block * depth, channels), lambda s: (s, 0)),
            spec((1, block, channels * depth), lambda s: (s, 0, 0)),
        ],
        out_shape=[
            jax.ShapeDtypeStruct((rows, depth, width), BF16),
            jax.ShapeDtypeStruct((rows * depth, channels), BF16),
            jax.ShapeDtypeStruct((steps, block, channels * depth), BF16),
        ],
        scratch_shapes=[pltpu.VMEM((block, depth, width), F32), pltpu.VMEM((block * depth, width), F32)]
        + [pltpu.VMEM(a.shape, a.dtype) for a in sources]
        + [pltpu.SemaphoreType.DMA((len(sources),))],
        compiler_params=pltpu.CompilerParams(vmem_limit_bytes=vmem_limit(length)),
        cost_estimate=pl.CostEstimate(flops=5 * 10**9, bytes_accessed=4000000, transcendentals=10**5),
        name="column_attention",
    )(idx, *pieces, *here, *sources)


def mix_kernel(idx, left, factors, validity, out, inverse, *, rows, depth, steps):
    lanes = out.shape[1] // rows
    for e in range(0, out.shape[0] // depth, 2):
        y = dot(left[...], factors[:, e * lanes : (e + 2) * lanes]).astype(BF16)
        for i in range(rows):
            for f in range(2):
                block = y[i * depth : (i + 1) * depth, f * lanes : (f + 1) * lanes]
                out[(e + f) * depth : (e + f + 1) * depth, i * lanes : (i + 1) * lanes] = block

    def count():
        length = validity.shape[1]
        valid = validity[...].astype(F32)
        target = idx[0] * rows + iota((length, rows * lanes), 1) // lanes
        mine = dot(valid.astype(BF16), one_hot(iota((length, rows * lanes), 0) == target))
        mine, turned = mine.astype(BF16), valid.T.astype(BF16)
        part = min(length, 320)
        for start in range(0, length, part):
            inverse[start : start + part, :] = 1.0 / (dot(turned[start : start + part], mine) + OUTER_EPS)

    if steps == 1:
        count()
    else:
        pl.when(pl.program_id(0) == 0)(count)


def mix_call(idx, left, factors, validity, rows):
    total, channels = left.shape
    depth, length = validity.shape
    lanes = factors.shape[1] // channels
    steps = 1 if length <= 320 else 4
    block = channels // steps
    if steps == 1:
        grid, spec = {}, lambda shape, index: pl.BlockSpec(memory_space=pltpu.VMEM)
    else:
        grid, spec = {"grid": (steps,)}, pl.BlockSpec
    return pl.pallas_call(
        functools.partial(mix_kernel, rows=rows, depth=depth, steps=steps),
        **grid,
        in_specs=[
            pl.BlockSpec(memory_space=pltpu.SMEM),
            spec((total, channels), lambda s: (0, 0)),
            spec((channels, block * lanes), lambda s: (0, s)),
            spec((depth, length), lambda s: (0, 0)),
        ],
        out_specs=[
            spec((block * depth, rows * lanes), lambda s: (s, 0)),
            spec((length, rows * lanes), lambda s: (0, 0)),
        ],
        out_shape=[
            jax.ShapeDtypeStruct((channels * depth, rows * lanes), BF16),
            jax.ShapeDtypeStruct((length, rows * lanes), F32),
        ],
        compiler_params=pltpu.CompilerParams(vmem_limit_bytes=vmem_limit(length)),
        cost_estimate=pl.CostEstimate(flops=2 * 10**9, bytes_accessed=4000000, transcendentals=10**5),
        name="left_mix",
    )(idx, left, factors, validity)


def finish_kernel(idx, *refs, pieces, sub, far, rows, length, block):
    near_refs, across_refs, refs = refs[:pieces], refs[pieces : 2 * pieces], refs[2 * pieces :]
    mixed, inverse, pair_one, gain, widen, narrow, out, right, held, sems = refs
    me = idx[0]
    z, p = me // sub, me % sub
    half = far * rows * sub // 2
    lanes = pair_one.shape[2]
    part = min(length, 320)
    alone = block == rows

    def first():
        r = iota((part, half), 1)
        b = div_const(r, rows, half)
        i = r - b * rows
        across_sub = 2 * div_const(b, far, half // rows)
        across_far = b - far * (across_sub >> 1)
        core = jnp.where(across_sub > 0, 1, 0) ^ jnp.where(across_far > 0, 1, 0)
        home = ((z ^ across_far) * sub + (p ^ across_sub ^ core)) * rows + i
        away = ((z ^ across_far) * sub + (p ^ 1 ^ across_sub ^ core)) * rows + i
        near = jnp.concatenate([ref[...].astype(F32) for ref in near_refs], 0).astype(BF16)
        across = jnp.concatenate([ref[...].astype(F32) for ref in across_refs], 0).astype(BF16)

        def arrange(start):
            j = iota((part, half), 0) + start
            here = pl.ds(start, part)
            right[here, :] = (dot(one_hot(j == home), near) + dot(one_hot(j == away), across)).astype(BF16)

        chunks(length, part, arrange)

    if alone:
        first()
    else:
        pl.when(pl.program_id(0) == 0)(first)

    together = 2 if block % 2 == 0 else 1
    copies = []

    def finish(start):
        here = pl.ds(start, part)
        update = dot(right[here, :], mixed[...])
        for n, r in enumerate(range(0, block, together)):
            x = []
            for q in range(r, r + together):
                columns = slice(q * lanes, (q + 1) * lanes)
                x.append(pair_one[q, here, :] + update[:, columns] * inverse[here, columns])
            x = jnp.concatenate(x, 0)
            normed = layer_norm(x, gain[...]).astype(BF16)
            hidden = jnp.maximum(dot(normed, widen[...]).astype(BF16), 0.0)
            x = (x + dot(hidden, narrow[...])).astype(BF16)
            for q in range(together):
                (held if alone else out)[r + q, here, :] = x[q * part : (q + 1) * part]
            if alone:
                done = pl.ds(r, together)
                copies.append(pltpu.make_async_copy(held.at[done], out.at[done], sems.at[n]))
                copies[-1].start()

    chunks(length, part, finish)
    for copy in copies:
        copy.wait()


def finish_call(idx, near, across, mixed, inverse, pair_one, gain, widen, narrow, sub, far):
    rows, length, lanes = pair_one.shape
    block = rows if length <= 320 else 2 if rows % 2 == 0 else 1
    product = mixed.shape[0]
    gain = gain[None, :]
    if block == rows:
        grid, spec = {}, lambda shape, index: pl.BlockSpec(memory_space=pltpu.VMEM)
        out_spec = pl.BlockSpec(memory_space=pl.ANY)
    else:
        grid, spec = {"grid": (rows // block,)}, pl.BlockSpec
        out_spec = spec((block, length, lanes), lambda s: (s, 0, 0))
    whole = lambda a: spec(a.shape, lambda s: (0,) * a.ndim)
    return pl.pallas_call(
        functools.partial(
            finish_kernel, pieces=len(near), sub=sub, far=far, rows=rows, length=length, block=block
        ),
        **grid,
        in_specs=[
            pl.BlockSpec(memory_space=pltpu.SMEM),
            *[whole(a) for a in near + across],
            spec((product, block * lanes), lambda s: (0, s)),
            spec((length, block * lanes), lambda s: (0, s)),
            spec((block, length, lanes), lambda s: (s, 0, 0)),
            whole(gain),
            whole(widen),
            whole(narrow),
        ],
        out_specs=out_spec,
        out_shape=jax.ShapeDtypeStruct((rows, length, lanes), BF16),
        scratch_shapes=[
            pltpu.VMEM((length, product), BF16),
            pltpu.VMEM((rows, length, lanes) if block == rows else (1, 16, 128), BF16),
            pltpu.SemaphoreType.DMA((rows,)),
        ],
        compiler_params=pltpu.CompilerParams(vmem_limit_bytes=vmem_limit(length)),
        cost_estimate=pl.CostEstimate(flops=4 * 10**9, bytes_accessed=4000000, transcendentals=10**5),
        name="pair_update",
    )(idx, *near, *across, mixed, inverse, pair_one, gain, widen, narrow)


def on_device(
    devices,
    alignment_embedding,
    couple_embedding,
    amino_strand,
    amino_validity,
    alignment_validity,
    separation_embedding,
    couple_shift_scaling,
    couple_shift_factors,
    horizontal_scaling_factor,
    horizontal_entry_factors,
    horizontal_exit_factors,
    vertical_scaling_factor,
    vertical_entry_factors,
    vertical_exit_factors,
    alignment_feedforward_scaling,
    alignment_widen_factors,
    alignment_narrow_factors,
    product_scaling_factor,
    product_twin_factors,
    product_exit_factors,
    couple_feedforward_scaling,
    couple_widen_factors,
    couple_narrow_factors,
):
    far = devices // SUB
    idx = lax.axis_index("dap").astype(jnp.int32).reshape(1)

    def swap(x, distance):
        return lax.ppermute(x, "dap", [(d, d ^ distance) for d in range(devices)])

    width = alignment_embedding.shape[2]
    rows = couple_embedding.shape[0]
    depth = alignment_validity.shape[0]

    near = [swap(alignment_embedding, k) for k in range(2, SUB, 2)]
    pair_one, bias = pair_call(
        idx, amino_strand, couple_embedding, separation_embedding, couple_shift_scaling, couple_shift_factors
    )
    entry = horizontal_entry_factors.reshape(width, 4 * width)
    order, distance = [0], far // 2
    mine, theirs = bias, swap(bias, SUB * distance)
    order += [b ^ distance for b in order]
    while distance > 1:
        distance //= 2
        mine = jnp.concatenate([mine, theirs], 0)
        theirs = swap(mine, SUB * distance)
        order += [b ^ distance for b in order]
    near = jnp.concatenate([alignment_embedding, *near], 0)
    entry, mine, near = lax.optimization_barrier((entry, mine, near))
    across = swap(near, 1)
    projected = project_call(idx, [near, across], horizontal_scaling_factor, entry, far, rows)
    sent = row_call(
        idx, [mine, theirs], order, projected, alignment_validity, amino_validity, horizontal_exit_factors
    )
    pieces = [swap(sent[k], SUB * k) for k in [*range(2, far), 1]]
    pieces = lax.optimization_barrier(pieces)
    pieces = [sent[0]] + [part for _, part in sorted(zip([*range(2, far), 1], pieces), key=lambda pair: pair[0])]
    updated, left, right = column_call(
        idx,
        pieces,
        alignment_validity,
        vertical_scaling_factor,
        vertical_entry_factors.reshape(width, 4 * width),
        vertical_exit_factors,
        alignment_feedforward_scaling,
        alignment_widen_factors,
        alignment_narrow_factors,
        product_scaling_factor,
        product_twin_factors,
    )
    channels = left.shape[1]
    right = right.reshape(rows, channels * depth)
    factors = product_exit_factors.reshape(channels, -1)
    mixed, inverse = mix_call(idx, left, factors, alignment_validity, rows)
    parts = [swap(right, SUB * k ^ 1) for k in [*range(2, far), 1]]
    mixed, right, *parts = lax.optimization_barrier((mixed, right, *parts))
    parts = [right] + [part for _, part in sorted(zip([*range(2, far), 1], parts), key=lambda pair: pair[0])]
    column = jnp.concatenate(parts, 0)
    near = [swap(column, k ^ 1) for k in [6, 2, 4]]
    near = lax.optimization_barrier(near)
    near = [part for _, part in sorted(zip([6, 2, 4], near), key=lambda pair: pair[0])]
    near = [column, jnp.concatenate(near, 0)]
    across = [swap(a, 1) for a in near]
    updated_pairs = finish_call(
        idx,
        near,
        across,
        mixed,
        inverse,
        pair_one,
        couple_feedforward_scaling,
        couple_widen_factors,
        couple_narrow_factors,
        SUB,
        far,
    )
    return updated.transpose(1, 0, 2), updated_pairs


def solution(mesh):
    split = P("dap", None, None)
    return jax.shard_map(
        functools.partial(on_device, mesh.shape["dap"]),
        mesh=mesh,
        in_specs=(split, split) + (P(),) * 21,
        out_specs=(P(None, "dap", None), split),
        check_vma=False,
    )
```

```python
import functools

import jax
import jax.numpy as jnp
from jax import lax
from jax.experimental import pallas as pl
from jax.experimental.pallas import tpu as pltpu
from jax.sharding import PartitionSpec as P

HEADS = 8
SUB = 8
EPS = 1e-05
OUTER_EPS = 0.001
MASKED = -1000000000.0
LOG2E = 1.4426950408889634
F32 = jnp.float32
BF16 = jnp.bfloat16


def vmem_limit(length):
    return (16 if length is not None and length <= 320 else 56) * 1024 * 1024


def dot(a, b):
    return jnp.dot(a, b, preferred_element_type=F32)


def dot_nt(a, b):
    return lax.dot_general(a, b, (((1,), (1,)), ((), ())), preferred_element_type=F32)


def dot_tn(a, b):
    return lax.dot_general(a, b, (((0,), (0,)), ((), ())), preferred_element_type=F32)


def layer_norm(x, gain):
    centred = x - jnp.mean(x, -1, keepdims=True)
    spread = jnp.mean(centred * centred, -1, keepdims=True)
    return centred * lax.rsqrt(spread + EPS) * gain


def iota(shape, dim):
    return lax.broadcasted_iota(jnp.int32, shape, dim)


def div_const(x, d, limit):
    m = 65536 // d + 1
    assert all((v * m) >> 16 == v // d for v in range(limit)) and limit * m < 2**31
    return (x * m) >> 16


def one_hot(match):
    return jnp.where(match, 1.0, 0.0).astype(BF16)


def chunks(total, step, body):
    if total == step:
        body(0)
    else:
        lax.fori_loop(0, total // step, lambda c, x: (body(pl.multiple_of(c * step, step)), x)[1], 0)


def pair_kernel(
    idx, chain, pair, chain_row, table, gain, factors, pair_one, bias, shifted, chain_wide, *, rows, length, bins
):
    step = pl.program_id(0)
    reach = (bins - 2) // 2

    @pl.when(step == 0)
    def _():
        k = iota((2 * length, bins), 0)
        wanted = jnp.clip(length - k + reach, 0, 2 * reach)
        pick = one_hot(wanted == iota((2 * length, bins), 1))
        rest, total = table[...], 0.0
        for _ in range(3):
            part = rest.astype(BF16)
            total += dot(pick, part)
            rest = rest - part.astype(F32)
        shifted[...] = total
        eye = iota((length, length), 0) == iota((length, length), 1)
        column = jnp.sum(jnp.where(eye, chain_row[...].astype(F32).reshape(1, length), 0.0), axis=1, keepdims=True)
        chain_wide[...] = jnp.broadcast_to(column, chain_wide.shape)

    other = table[bins - 1 : bins, :]
    block = pair.shape[0]
    together = block
    for start in range(0, block, together):
        sums = []
        for r in range(start, start + together):
            i = idx[0] * rows + step * block + r
            near = shifted[pl.ds(length - i, length), :]
            same = chain_wide[...] == chain[i].astype(F32)
            x = pair[r].astype(F32) + jnp.where(same, near, other)
            pair_one[r] = x
            sums.append(x)
        normed = layer_norm(jnp.concatenate(sums, 0), gain[...]).astype(BF16)
        both = dot_nt(factors[...], normed).astype(BF16)
        for r in range(together):
            bias[start + r] = both[:, r * length : (r + 1) * length]


def pair_call(idx, chain, pair, table, gain, factors):
    rows, length, depth = pair.shape
    block = 5 if rows % 5 == 0 else 1
    bins = table.shape[0]
    smem = pl.BlockSpec(memory_space=pltpu.SMEM)
    whole = lambda *shape: pl.BlockSpec(shape, lambda s: (0,) * len(shape))
    return pl.pallas_call(
        functools.partial(pair_kernel, rows=rows, length=length, bins=bins),
        grid=(rows // block,),
        in_specs=[
            smem,
            smem,
            pl.BlockSpec((block, length, depth), lambda s: (s, 0, 0)),
            whole(length),
            whole(bins, depth),
            whole(1, depth),
            whole(HEADS, depth),
        ],
        out_specs=[
            pl.BlockSpec((block, length, depth), lambda s: (s, 0, 0)),
            pl.BlockSpec((block, HEADS, length), lambda s: (s, 0, 0)),
        ],
        out_shape=[
            jax.ShapeDtypeStruct((rows, length, depth), F32),
            jax.ShapeDtypeStruct((rows, HEADS, length), BF16),
        ],
        scratch_shapes=[pltpu.VMEM((2 * length, depth), F32), pltpu.VMEM((length, depth), F32)],
        compiler_params=pltpu.CompilerParams(vmem_limit_bytes=vmem_limit(None)),
        cost_estimate=pl.CostEstimate(flops=4 * 10**9, bytes_accessed=4000000, transcendentals=10**5),
        name="pair_bias",
    )(idx, chain, pair, chain, table, gain[None, :], factors.T)


def core_of(place, far):
    core, bit = 0, 0
    while far >> (bit + 1):
        core = core ^ ((place >> bit) & 1)
        bit += 1
    return core


def project_kernel(idx, *refs, sub, far, rows, length, width):
    row_refs, refs = refs[:2], refs[2:]
    gain, entry, keys, values, query, gate, own_rows, own_normed = refs
    me = idx[0]
    z, p = me // sub, me % sub
    own = far * rows
    scale = (width // HEADS) ** -0.5 * LOG2E

    r = iota((own, length), 0)
    block = div_const(r, rows, own)
    residue = ((z ^ block) * sub + (p ^ core_of(block, far))) * rows + r - block * rows
    pick = one_hot(residue == iota((own, length), 1))

    step = min(length, 320)
    for k in range(sub):
        source, place = row_refs[k % 2 ^ (k > 1)], k // 2

        def project(start, k=k, source=source, place=place):
            x = source[place, pl.ds(start, step), :]
            normed = layer_norm(x.astype(F32), gain[...]).astype(BF16)
            both = dot(normed, entry[:, width : 3 * width])
            keys[k, pl.ds(start, step), :] = both[:, :width].astype(BF16)
            values[k, pl.ds(start, step), :] = both[:, width:].astype(BF16)
            part = pick if length == step else one_hot(residue[:, :step] == iota((own, step), 1) + start)
            q_rows, a_rows = dot(part, normed), dot(part, x)
            here = pl.ds(k * own, own)
            if length == step:
                own_normed[here, :] = q_rows
                own_rows[here, :] = a_rows
            else:
                fresh = start == 0
                own_normed[here, :] = q_rows + jnp.where(fresh, 0.0, own_normed[here, :])
                own_rows[here, :] = a_rows + jnp.where(fresh, 0.0, own_rows[here, :])

        chunks(length, step, project)

    total = sub * own
    part = min(total, 320)

    def queries(start):
        here = pl.ds(start, part)
        normed = own_normed[here, :].astype(BF16)
        query[here, :] = dot(normed, entry[:, :width]) * scale
        gate[here, :] = jax.nn.sigmoid(dot(normed, entry[:, 3 * width :]))

    chunks(total, part, queries)


def project_call(idx, msa_rows, gain, entry, far, rows):
    sub = SUB
    _, length, width = msa_rows[0].shape
    own = far * rows
    vmem = pl.BlockSpec(memory_space=pltpu.VMEM)
    wide = jax.ShapeDtypeStruct((sub, length, width), BF16)
    narrow = jax.ShapeDtypeStruct((sub * own, width), F32)
    return pl.pallas_call(
        functools.partial(project_kernel, sub=sub, far=far, rows=rows, length=length, width=width),
        in_specs=[pl.BlockSpec(memory_space=pltpu.SMEM)] + [vmem] * 4,
        out_specs=[vmem] * 5,
        out_shape=[wide, wide, narrow, narrow, narrow],
        scratch_shapes=[pltpu.VMEM((sub * own, width), F32)],
        compiler_params=pltpu.CompilerParams(vmem_limit_bytes=vmem_limit(length)),
        cost_estimate=pl.CostEstimate(flops=3 * 10**9, bytes_accessed=4000000, transcendentals=10**5),
        name="row_project",
    )(idx, *msa_rows, gain[None, :], entry)


def row_kernel(idx, *refs, order, sub, far, rows, length, width):
    bias_refs, refs = refs[:2], refs[2:]
    keys, values, query, gate, own_rows, validity, amino, exit_ = refs[:8]
    outs, refs = refs[8 : 8 + far], refs[8 + far :]
    by_residue, bias, gated = refs
    me = idx[0]
    z, p = me // sub, me % sub
    own = far * rows
    total = sub * own
    half = far // 2
    for n, b in enumerate(order):
        block = bias_refs[n // half][n % half * rows : (n % half + 1) * rows]
        by_residue[b * rows : (b + 1) * rows] = block.astype(F32) * LOG2E
    for h in range(HEADS):
        bias[h] = by_residue[:, h, :]

    channel = width // HEADS
    head_of = iota((1, width), 1) // channel
    head_mask = [jnp.where(head_of == h, 1.0, 0.0) for h in range(HEADS)]
    take = 40 if own % 40 == 0 else rows

    def attend(n, k, start):
        s = z * sub + (p ^ k)
        valid = validity[pl.ds(s, 1), :] * amino[...].reshape(1, length)
        masked = jnp.where(valid > 0, 0.0, MASKED)
        here = pl.ds(pl.multiple_of(n * take, take), take) if not isinstance(n, int) else pl.ds(n * take, take)
        q = query[here, :]
        q = jnp.concatenate([q * mask for mask in head_mask], 0).astype(BF16)
        scores = dot_nt(q, keys[k]) + bias[:, pl.ds(start, take), :].reshape(HEADS * take, length) + masked
        expo = jnp.exp2(scores - jnp.max(scores, -1, keepdims=True))
        share = 1.0 / jnp.sum(expo, -1, keepdims=True)
        mixed = dot(expo.astype(BF16), values[k]) * share
        merged = mixed[:take] * head_mask[0]
        for h in range(1, HEADS):
            merged += mixed[h * take : (h + 1) * take] * head_mask[h]
        gated[here, :] = merged * gate[here, :]

    parts = own // take
    if parts == 1:
        for k in range(sub):
            attend(k, k, 0)
    else:
        lax.fori_loop(0, sub * parts, lambda n, x: (attend(n, n // parts, (n % parts) * take), x)[1], 0)

    piece = rows * sub
    for b in range(far):
        q = iota((piece, total), 0) + b * piece
        residue_, row = div_const(q, sub, total), q & (sub - 1)
        swap = one_hot((row ^ p) * own + residue_ == iota((piece, total), 1))
        gated_rows = dot(swap, gated[...].astype(BF16)).astype(BF16)
        x = dot(swap, own_rows[...].astype(BF16)) + dot(gated_rows, exit_[...])
        outs[b][...] = x.astype(BF16).reshape(rows, sub, width)


def row_call(idx, bias_halves, order, projected, validity, amino, exit_):
    keys, values, query, gate, own_rows = projected
    sub, far = keys.shape[0], len(order)
    _, length, width = keys.shape
    rows = 2 * bias_halves[0].shape[0] // far
    own = far * rows
    vmem = pl.BlockSpec(memory_space=pltpu.VMEM)
    return pl.pallas_call(
        functools.partial(row_kernel, order=order, sub=sub, far=far, rows=rows, length=length, width=width),
        in_specs=[pl.BlockSpec(memory_space=pltpu.SMEM)] + [vmem] * 10,
        out_specs=[vmem] * far,
        out_shape=[jax.ShapeDtypeStruct((rows, sub, width), BF16)] * far,
        scratch_shapes=[
            pltpu.VMEM((own, HEADS, length), F32),
            pltpu.VMEM((HEADS, own, length), F32),
            pltpu.VMEM((sub * own, width), F32),
        ],
        compiler_params=pltpu.CompilerParams(vmem_limit_bytes=vmem_limit(length)),
        cost_estimate=pl.CostEstimate(flops=4 * 10**9, bytes_accessed=4000000, transcendentals=10**5),
        name="row_attention",
    )(idx, *bias_halves, keys, values, query, gate, own_rows, validity, amino, exit_)


def column_kernel(idx, *refs, sub, far, rows, block, depth, width):
    piece_refs, refs = refs[:far], refs[far:]
    entry, twin, *sources = refs[:9]
    updated, left, right, start_rows, gated, *held = refs[9:-1]
    sems = refs[-1]
    copies = [pltpu.make_async_copy(src, dst, sems.at[n]) for n, (src, dst) in enumerate(zip(sources, held))]
    steps = rows // block

    def begin():
        for copy in copies:
            copy.start()

    def arrived(*which):
        def wait():
            for n in which:
                copies[n].wait()

        if steps == 1:
            wait()
        else:
            pl.when(pl.program_id(0) == 0)(wait)
        return [held[n][...] for n in which]

    if steps == 1:
        begin()
    else:
        pl.when(pl.program_id(0) == 0)(begin)
    me = idx[0]
    z = me // sub
    first = me * rows + (0 if steps == 1 else pl.program_id(0) * block)
    scale = (width // HEADS) ** -0.5 * LOG2E
    total = block * depth
    for b in range(far):
        here = pl.ds(pl.multiple_of((z ^ b) * sub, sub), sub)
        start_rows[:, here, :] = piece_refs[b][...].astype(F32)
    x = start_rows[...].reshape(total, width)
    (col_gain,) = arrived(0)
    normed = layer_norm(x, col_gain).astype(BF16)
    proj = dot(normed, entry[...])
    query = proj[:, :width] * scale
    keys = proj[:, width : 2 * width].astype(BF16)
    values = proj[:, 2 * width : 3 * width].astype(BF16)
    gate = jax.nn.sigmoid(proj[:, 3 * width :])

    (validity,) = arrived(1)
    length = validity.shape[1]
    lanes = 128
    pick = one_hot(iota((length, lanes), 0) == first + iota((length, lanes), 1))
    valid = dot(validity.astype(F32).astype(BF16), pick)
    head_of = iota((1, width), 1) // (width // HEADS)
    head_mask = [jnp.where(head_of == h, 1.0, 0.0) for h in range(HEADS)]
    for i in range(block):
        here = slice(i * depth, (i + 1) * depth)
        q = jnp.concatenate([query[here] * mask for mask in head_mask], 0).astype(BF16)
        masked = jnp.where(valid[:, i : i + 1] > 0, 0.0, MASKED)
        scores = dot_nt(keys[here], q) + masked
        expo = jnp.exp2(scores - jnp.max(scores, 0, keepdims=True))
        weights = (expo * (1.0 / jnp.sum(expo, 0, keepdims=True))).astype(BF16)
        mixed = dot_tn(weights, values[here])
        merged = mixed[:depth] * head_mask[0]
        for h in range(1, HEADS):
            merged += mixed[h * depth : (h + 1) * depth] * head_mask[h]
        gated[here, :] = merged * gate[here]
    exit_, ff_gain, widen, narrow, product_gain = arrived(2, 3, 4, 5, 6)
    x = x + dot(gated[...].astype(BF16), exit_)
    hidden = jnp.maximum(dot(layer_norm(x, ff_gain).astype(BF16), widen).astype(BF16), 0.0)
    x = x + dot(hidden, narrow)
    updated[...] = x.astype(BF16).reshape(block, depth, width)
    outer = layer_norm(x, product_gain).astype(BF16)
    both = dot(outer, twin[...])
    channels = twin.shape[1] // 2
    spread = iota((depth, channels * depth), 1)
    channel = spread // depth
    repeat = one_hot(
        iota((2 * channels, channels * depth), 0) - channels == iota((2 * channels, channels * depth), 1) // depth
    )
    mine = jnp.where(spread - channel * depth == iota((depth, channels * depth), 0), 1.0, 0.0)
    for i in range(block):
        here = slice(i * depth, (i + 1) * depth)
        part = (both[here] * valid[:, i : i + 1]).astype(BF16)
        left[here, :] = part[:, :channels]
        right[0, i : i + 1, :] = jnp.sum(dot(part, repeat) * mine, axis=0, keepdims=True).astype(BF16)


def column_call(idx, pieces, validity, col_gain, entry, exit_, ff_gain, widen, narrow, product_gain, twin):
    far = len(pieces)
    rows, sub, width = pieces[0].shape
    depth, length = validity.shape
    block = rows
    while block * depth > 320 and block % 2 == 0:
        block //= 2
    channels = twin.shape[1] // 2
    steps = rows // block
    here = [entry, twin]
    sources = [
        col_gain[None, :],
        validity,
        exit_,
        ff_gain[None, :],
        widen,
        narrow,
        product_gain[None, :],
    ]
    if steps == 1:
        grid, spec = {}, lambda shape, index: pl.BlockSpec(memory_space=pltpu.VMEM)
    else:
        grid, spec = {"grid": (steps,)}, pl.BlockSpec
    return pl.pallas_call(
        functools.partial(column_kernel, sub=sub, far=far, rows=rows, block=block, depth=depth, width=width),
        **grid,
        in_specs=[pl.BlockSpec(memory_space=pltpu.SMEM)]
        + [spec((block, sub, width), lambda s: (s, 0, 0))] * far
        + [spec(a.shape, lambda s: (0, 0)) for a in here]
        + [pl.BlockSpec(memory_space=pltpu.HBM)] * len(sources),
        out_specs=[
            spec((block, depth, width), lambda s: (s, 0, 0)),
            spec((block * depth, channels), lambda s: (s, 0)),
            spec((1, block, channels * depth), lambda s: (s, 0, 0)),
        ],
        out_shape=[
            jax.ShapeDtypeStruct((rows, depth, width), BF16),
            jax.ShapeDtypeStruct((rows * depth, channels), BF16),
            jax.ShapeDtypeStruct((steps, block, channels * depth), BF16),
        ],
        scratch_shapes=[pltpu.VMEM((block, depth, width), F32), pltpu.VMEM((block * depth, width), F32)]
        + [pltpu.VMEM(a.shape, a.dtype) for a in sources]
        + [pltpu.SemaphoreType.DMA((len(sources),))],
        compiler_params=pltpu.CompilerParams(vmem_limit_bytes=vmem_limit(length)),
        cost_estimate=pl.CostEstimate(flops=5 * 10**9, bytes_accessed=4000000, transcendentals=10**5),
        name="column_attention",
    )(idx, *pieces, *here, *sources)


def mix_kernel(idx, left, factors, validity, out, inverse, *, rows, depth, steps):
    lanes = out.shape[1] // rows
    for e in range(0, out.shape[0] // depth, 2):
        y = dot(left[...], factors[:, e * lanes : (e + 2) * lanes]).astype(BF16)
        for i in range(rows):
            for f in range(2):
                block = y[i * depth : (i + 1) * depth, f * lanes : (f + 1) * lanes]
                out[(e + f) * depth : (e + f + 1) * depth, i * lanes : (i + 1) * lanes] = block

    def count():
        length = validity.shape[1]
        valid = validity[...].astype(F32)
        target = idx[0] * rows + iota((length, rows * lanes), 1) // lanes
        mine = dot(valid.astype(BF16), one_hot(iota((length, rows * lanes), 0) == target))
        mine, turned = mine.astype(BF16), valid.T.astype(BF16)
        part = min(length, 320)
        for start in range(0, length, part):
            inverse[start : start + part, :] = 1.0 / (dot(turned[start : start + part], mine) + OUTER_EPS)

    if steps == 1:
        count()
    else:
        pl.when(pl.program_id(0) == 0)(count)


def mix_call(idx, left, factors, validity, rows):
    total, channels = left.shape
    depth, length = validity.shape
    lanes = factors.shape[1] // channels
    steps = 1 if length <= 320 else 4
    block = channels // steps
    if steps == 1:
        grid, spec = {}, lambda shape, index: pl.BlockSpec(memory_space=pltpu.VMEM)
    else:
        grid, spec = {"grid": (steps,)}, pl.BlockSpec
    return pl.pallas_call(
        functools.partial(mix_kernel, rows=rows, depth=depth, steps=steps),
        **grid,
        in_specs=[
            pl.BlockSpec(memory_space=pltpu.SMEM),
            spec((total, channels), lambda s: (0, 0)),
            spec((channels, block * lanes), lambda s: (0, s)),
            spec((depth, length), lambda s: (0, 0)),
        ],
        out_specs=[
            spec((block * depth, rows * lanes), lambda s: (s, 0)),
            spec((length, rows * lanes), lambda s: (0, 0)),
        ],
        out_shape=[
            jax.ShapeDtypeStruct((channels * depth, rows * lanes), BF16),
            jax.ShapeDtypeStruct((length, rows * lanes), F32),
        ],
        compiler_params=pltpu.CompilerParams(vmem_limit_bytes=vmem_limit(length)),
        cost_estimate=pl.CostEstimate(flops=2 * 10**9, bytes_accessed=4000000, transcendentals=10**5),
        name="left_mix",
    )(idx, left, factors, validity)


def finish_kernel(idx, *refs, pieces, sub, far, rows, length, block):
    near_refs, across_refs, refs = refs[:pieces], refs[pieces : 2 * pieces], refs[2 * pieces :]
    mixed, inverse, pair_one, gain, widen, narrow, out, right, held, sems = refs
    me = idx[0]
    z, p = me // sub, me % sub
    half = far * rows * sub // 2
    lanes = pair_one.shape[2]
    part = min(length, 320)
    alone = block == rows

    def first():
        r = iota((part, half), 1)
        b = div_const(r, rows, half)
        i = r - b * rows
        across_sub = 2 * div_const(b, far, half // rows)
        across_far = b - far * (across_sub >> 1)
        core = jnp.where(across_sub > 0, 1, 0) ^ jnp.where(across_far > 0, 1, 0)
        home = ((z ^ across_far) * sub + (p ^ across_sub ^ core)) * rows + i
        away = ((z ^ across_far) * sub + (p ^ 1 ^ across_sub ^ core)) * rows + i
        near = jnp.concatenate([ref[...].astype(F32) for ref in near_refs], 0).astype(BF16)
        across = jnp.concatenate([ref[...].astype(F32) for ref in across_refs], 0).astype(BF16)

        def arrange(start):
            j = iota((part, half), 0) + start
            here = pl.ds(start, part)
            right[here, :] = (dot(one_hot(j == home), near) + dot(one_hot(j == away), across)).astype(BF16)

        chunks(length, part, arrange)

    if alone:
        first()
    else:
        pl.when(pl.program_id(0) == 0)(first)

    together = 2 if block % 2 == 0 else 1
    copies = []

    def finish(start):
        here = pl.ds(start, part)
        update = dot(right[here, :], mixed[...])
        for n, r in enumerate(range(0, block, together)):
            x = []
            for q in range(r, r + together):
                columns = slice(q * lanes, (q + 1) * lanes)
                x.append(pair_one[q, here, :] + update[:, columns] * inverse[here, columns])
            x = jnp.concatenate(x, 0)
            normed = layer_norm(x, gain[...]).astype(BF16)
            hidden = jnp.maximum(dot(normed, widen[...]).astype(BF16), 0.0)
            x = (x + dot(hidden, narrow[...])).astype(BF16)
            for q in range(together):
                (held if alone else out)[r + q, here, :] = x[q * part : (q + 1) * part]
            if alone:
                done = pl.ds(r, together)
                copies.append(pltpu.make_async_copy(held.at[done], out.at[done], sems.at[n]))
                copies[-1].start()

    chunks(length, part, finish)
    for copy in copies:
        copy.wait()


def finish_call(idx, near, across, mixed, inverse, pair_one, gain, widen, narrow, sub, far):
    rows, length, lanes = pair_one.shape
    block = rows if length <= 320 else 2 if rows % 2 == 0 else 1
    product = mixed.shape[0]
    gain = gain[None, :]
    if block == rows:
        grid, spec = {}, lambda shape, index: pl.BlockSpec(memory_space=pltpu.VMEM)
        out_spec = pl.BlockSpec(memory_space=pl.ANY)
    else:
        grid, spec = {"grid": (rows // block,)}, pl.BlockSpec
        out_spec = spec((block, length, lanes), lambda s: (s, 0, 0))
    whole = lambda a: spec(a.shape, lambda s: (0,) * a.ndim)
    return pl.pallas_call(
        functools.partial(
            finish_kernel, pieces=len(near), sub=sub, far=far, rows=rows, length=length, block=block
        ),
        **grid,
        in_specs=[
            pl.BlockSpec(memory_space=pltpu.SMEM),
            *[whole(a) for a in near + across],
            spec((product, block * lanes), lambda s: (0, s)),
            spec((length, block * lanes), lambda s: (0, s)),
            spec((block, length, lanes), lambda s: (s, 0, 0)),
            whole(gain),
            whole(widen),
            whole(narrow),
        ],
        out_specs=out_spec,
        out_shape=jax.ShapeDtypeStruct((rows, length, lanes), BF16),
        scratch_shapes=[
            pltpu.VMEM((length, product), BF16),
            pltpu.VMEM((rows, length, lanes) if block == rows else (1, 16, 128), BF16),
            pltpu.SemaphoreType.DMA((rows,)),
        ],
        compiler_params=pltpu.CompilerParams(vmem_limit_bytes=vmem_limit(length)),
        cost_estimate=pl.CostEstimate(flops=4 * 10**9, bytes_accessed=4000000, transcendentals=10**5),
        name="pair_update",
    )(idx, *near, *across, mixed, inverse, pair_one, gain, widen, narrow)


def on_device(
    devices,
    alignment_embedding,
    couple_embedding,
    amino_strand,
    amino_validity,
    alignment_validity,
    separation_embedding,
    couple_shift_scaling,
    couple_shift_factors,
    horizontal_scaling_factor,
    horizontal_entry_factors,
    horizontal_exit_factors,
    vertical_scaling_factor,
    vertical_entry_factors,
    vertical_exit_factors,
    alignment_feedforward_scaling,
    alignment_widen_factors,
    alignment_narrow_factors,
    product_scaling_factor,
    product_twin_factors,
    product_exit_factors,
    couple_feedforward_scaling,
    couple_widen_factors,
    couple_narrow_factors,
):
    far = devices // SUB
    idx = lax.axis_index("dap").astype(jnp.int32).reshape(1)

    def swap(x, distance):
        return lax.ppermute(x, "dap", [(d, d ^ distance) for d in range(devices)])

    width = alignment_embedding.shape[2]
    rows = couple_embedding.shape[0]
    depth = alignment_validity.shape[0]

    near = [swap(alignment_embedding, k ^ 1) for k in range(2, SUB, 2)]
    pair_one, bias = pair_call(
        idx, amino_strand, couple_embedding, separation_embedding, couple_shift_scaling, couple_shift_factors
    )
    entry = horizontal_entry_factors.reshape(width, 4 * width)
    order, distance = [0], far // 2
    mine, theirs = bias, swap(bias, SUB * distance ^ 1)
    order += [b ^ distance for b in order]
    while distance > 1:
        distance //= 2
        mine = jnp.concatenate([mine, theirs], 0)
        theirs = swap(mine, SUB * distance ^ 1)
        order += [b ^ distance for b in order]
    near = jnp.concatenate([alignment_embedding, *near], 0)
    entry, mine, near = lax.optimization_barrier((entry, mine, near))
    across = swap(near, 1)
    projected = project_call(idx, [near, across], horizontal_scaling_factor, entry, far, rows)
    sent = row_call(
        idx, [mine, theirs], order, projected, alignment_validity, amino_validity, horizontal_exit_factors
    )
    pieces = [swap(sent[k], SUB * k ^ core_of(k, far)) for k in [*range(2, far), 1]]
    pieces = lax.optimization_barrier(pieces)
    pieces = [sent[0]] + [part for _, part in sorted(zip([*range(2, far), 1], pieces), key=lambda pair: pair[0])]
    updated, left, right = column_call(
        idx,
        pieces,
        alignment_validity,
        vertical_scaling_factor,
        vertical_entry_factors.reshape(width, 4 * width),
        vertical_exit_factors,
        alignment_feedforward_scaling,
        alignment_widen_factors,
        alignment_narrow_factors,
        product_scaling_factor,
        product_twin_factors,
    )
    channels = left.shape[1]
    right = right.reshape(rows, channels * depth)
    factors = product_exit_factors.reshape(channels, -1)
    mixed, inverse = mix_call(idx, left, factors, alignment_validity, rows)
    parts = [swap(right, SUB * k ^ 1) for k in [*range(2, far), 1]]
    mixed, right, *parts = lax.optimization_barrier((mixed, right, *parts))
    parts = [right] + [part for _, part in sorted(zip([*range(2, far), 1], parts), key=lambda pair: pair[0])]
    column = jnp.concatenate(parts, 0)
    near = [swap(column, k ^ 1) for k in [6, 2, 4]]
    beside = swap(column, 1)
    *near, beside = lax.optimization_barrier((*near, beside))
    near = [part for _, part in sorted(zip([6, 2, 4], near), key=lambda pair: pair[0])]
    near = [column, jnp.concatenate(near, 0)]
    across = [beside, swap(near[1], 1)]
    updated_pairs = finish_call(
        idx,
        near,
        across,
        mixed,
        inverse,
        pair_one,
        couple_feedforward_scaling,
        couple_widen_factors,
        couple_narrow_factors,
        SUB,
        far,
    )
    return updated.transpose(1, 0, 2), updated_pairs


def solution(mesh):
    split = P("dap", None, None)
    return jax.shard_map(
        functools.partial(on_device, mesh.shape["dap"]),
        mesh=mesh,
        in_specs=(split, split) + (P(),) * 21,
        out_specs=(P(None, "dap", None), split),
        check_vma=False,
    )
```

```python
import functools

import jax
import jax.numpy as jnp
from jax import lax
from jax.experimental import pallas as pl
from jax.experimental.pallas import tpu as pltpu
from jax.sharding import PartitionSpec as P

HEADS = 8
SUB = 8
EPS = 1e-05
OUTER_EPS = 0.001
MASKED = -1000000000.0
LOG2E = 1.4426950408889634
F32 = jnp.float32
BF16 = jnp.bfloat16


def vmem_limit(length):
    return (16 if length is not None and length <= 320 else 56) * 1024 * 1024


def dot(a, b):
    return jnp.dot(a, b, preferred_element_type=F32)


def dot_nt(a, b):
    return lax.dot_general(a, b, (((1,), (1,)), ((), ())), preferred_element_type=F32)


def dot_tn(a, b):
    return lax.dot_general(a, b, (((0,), (0,)), ((), ())), preferred_element_type=F32)


def layer_norm(x, gain):
    centred = x - jnp.mean(x, -1, keepdims=True)
    spread = jnp.mean(centred * centred, -1, keepdims=True)
    return centred * lax.rsqrt(spread + EPS) * gain


def iota(shape, dim):
    return lax.broadcasted_iota(jnp.int32, shape, dim)


def div_const(x, d, limit):
    m = 65536 // d + 1
    assert all((v * m) >> 16 == v // d for v in range(limit)) and limit * m < 2**31
    return (x * m) >> 16


def one_hot(match):
    return jnp.where(match, 1.0, 0.0).astype(BF16)


def chunks(total, step, body):
    if total == step:
        body(0)
    else:
        lax.fori_loop(0, total // step, lambda c, x: (body(pl.multiple_of(c * step, step)), x)[1], 0)


def pair_kernel(
    idx, chain, pair, chain_row, table, gain, factors, pair_one, bias, shifted, chain_wide, *, rows, length, bins
):
    step = pl.program_id(0)
    reach = (bins - 2) // 2

    @pl.when(step == 0)
    def _():
        k = iota((2 * length, bins), 0)
        wanted = jnp.clip(length - k + reach, 0, 2 * reach)
        pick = one_hot(wanted == iota((2 * length, bins), 1))
        rest, total = table[...], 0.0
        for _ in range(3):
            part = rest.astype(BF16)
            total += dot(pick, part)
            rest = rest - part.astype(F32)
        shifted[...] = total
        eye = iota((length, length), 0) == iota((length, length), 1)
        column = jnp.sum(jnp.where(eye, chain_row[...].astype(F32).reshape(1, length), 0.0), axis=1, keepdims=True)
        chain_wide[...] = jnp.broadcast_to(column, chain_wide.shape)

    other = table[bins - 1 : bins, :]
    block = pair.shape[0]
    together = block
    for start in range(0, block, together):
        sums = []
        for r in range(start, start + together):
            i = idx[0] * rows + step * block + r
            near = shifted[pl.ds(length - i, length), :]
            same = chain_wide[...] == chain[i].astype(F32)
            x = pair[r].astype(F32) + jnp.where(same, near, other)
            pair_one[r] = x
            sums.append(x)
        normed = layer_norm(jnp.concatenate(sums, 0), gain[...]).astype(BF16)
        both = dot_nt(factors[...], normed).astype(BF16)
        for r in range(together):
            bias[start + r] = both[:, r * length : (r + 1) * length]


def pair_call(idx, chain, pair, table, gain, factors):
    rows, length, depth = pair.shape
    block = 5 if rows % 5 == 0 else 1
    bins = table.shape[0]
    smem = pl.BlockSpec(memory_space=pltpu.SMEM)
    whole = lambda *shape: pl.BlockSpec(shape, lambda s: (0,) * len(shape))
    return pl.pallas_call(
        functools.partial(pair_kernel, rows=rows, length=length, bins=bins),
        grid=(rows // block,),
        in_specs=[
            smem,
            smem,
            pl.BlockSpec((block, length, depth), lambda s: (s, 0, 0)),
            whole(length),
            whole(bins, depth),
            whole(1, depth),
            whole(HEADS, depth),
        ],
        out_specs=[
            pl.BlockSpec((block, length, depth), lambda s: (s, 0, 0)),
            pl.BlockSpec((block, HEADS, length), lambda s: (s, 0, 0)),
        ],
        out_shape=[
            jax.ShapeDtypeStruct((rows, length, depth), F32),
            jax.ShapeDtypeStruct((rows, HEADS, length), BF16),
        ],
        scratch_shapes=[pltpu.VMEM((2 * length, depth), F32), pltpu.VMEM((length, depth), F32)],
        compiler_params=pltpu.CompilerParams(vmem_limit_bytes=vmem_limit(None)),
        cost_estimate=pl.CostEstimate(flops=4 * 10**9, bytes_accessed=4000000, transcendentals=10**5),
        name="pair_bias",
    )(idx, chain, pair, chain, table, gain[None, :], factors.T)


def core_of(place, far):
    core, bit = 0, 0
    while far >> (bit + 1):
        core = core ^ ((place >> bit) & 1)
        bit += 1
    return core


def project_kernel(idx, *refs, sub, far, rows, length, width):
    row_refs, refs = refs[:2], refs[2:]
    gain, entry, keys, values, query, gate, own_rows, own_normed = refs
    me = idx[0]
    z, p = me // sub, me % sub
    own = far * rows
    scale = (width // HEADS) ** -0.5 * LOG2E

    r = iota((own, length), 0)
    block = div_const(r, rows, own)
    residue = ((z ^ block) * sub + (p ^ core_of(block, far))) * rows + r - block * rows
    pick = one_hot(residue == iota((own, length), 1))

    step = min(length, 320)
    for k in range(sub):
        source, place = row_refs[k % 2 ^ (k > 1)], k // 2

        def project(start, k=k, source=source, place=place):
            x = source[place, pl.ds(start, step), :]
            normed = layer_norm(x.astype(F32), gain[...]).astype(BF16)
            both = dot(normed, entry[:, width : 3 * width])
            keys[k, pl.ds(start, step), :] = both[:, :width].astype(BF16)
            values[k, pl.ds(start, step), :] = both[:, width:].astype(BF16)
            part = pick if length == step else one_hot(residue[:, :step] == iota((own, step), 1) + start)
            q_rows, a_rows = dot(part, normed), dot(part, x)
            here = pl.ds(k * own, own)
            if length == step:
                own_normed[here, :] = q_rows
                own_rows[here, :] = a_rows
            else:
                fresh = start == 0
                own_normed[here, :] = q_rows + jnp.where(fresh, 0.0, own_normed[here, :])
                own_rows[here, :] = a_rows + jnp.where(fresh, 0.0, own_rows[here, :])

        chunks(length, step, project)

    total = sub * own
    part = min(total, 320)

    def queries(start):
        here = pl.ds(start, part)
        normed = own_normed[here, :].astype(BF16)
        query[here, :] = dot(normed, entry[:, :width]) * scale
        gate[here, :] = jax.nn.sigmoid(dot(normed, entry[:, 3 * width :]))

    chunks(total, part, queries)


def project_call(idx, msa_rows, gain, entry, far, rows):
    sub = SUB
    _, length, width = msa_rows[0].shape
    own = far * rows
    vmem = pl.BlockSpec(memory_space=pltpu.VMEM)
    wide = jax.ShapeDtypeStruct((sub, length, width), BF16)
    narrow = jax.ShapeDtypeStruct((sub * own, width), F32)
    return pl.pallas_call(
        functools.partial(project_kernel, sub=sub, far=far, rows=rows, length=length, width=width),
        in_specs=[pl.BlockSpec(memory_space=pltpu.SMEM)] + [vmem] * 4,
        out_specs=[vmem] * 5,
        out_shape=[wide, wide, narrow, narrow, narrow],
        scratch_shapes=[pltpu.VMEM((sub * own, width), F32)],
        compiler_params=pltpu.CompilerParams(vmem_limit_bytes=vmem_limit(length)),
        cost_estimate=pl.CostEstimate(flops=3 * 10**9, bytes_accessed=4000000, transcendentals=10**5),
        name="row_project",
    )(idx, *msa_rows, gain[None, :], entry)


def row_kernel(idx, *refs, order, sub, far, rows, length, width):
    bias_refs, refs = refs[:2], refs[2:]
    keys, values, query, gate, own_rows, validity, amino, exit_ = refs[:8]
    outs, refs = refs[8 : 8 + far], refs[8 + far :]
    by_residue, bias, gated = refs
    me = idx[0]
    z, p = me // sub, me % sub
    own = far * rows
    total = sub * own
    half = far // 2
    for n, b in enumerate(order):
        block = bias_refs[n // half][n % half * rows : (n % half + 1) * rows]
        by_residue[b * rows : (b + 1) * rows] = block.astype(F32) * LOG2E
    for h in range(HEADS):
        bias[h] = by_residue[:, h, :]

    channel = width // HEADS
    head_of = iota((1, width), 1) // channel
    head_mask = [jnp.where(head_of == h, 1.0, 0.0) for h in range(HEADS)]
    take = 40 if own % 40 == 0 else rows

    def attend(n, k, start):
        s = z * sub + (p ^ k)
        valid = validity[pl.ds(s, 1), :] * amino[...].reshape(1, length)
        masked = jnp.where(valid > 0, 0.0, MASKED)
        here = pl.ds(pl.multiple_of(n * take, take), take) if not isinstance(n, int) else pl.ds(n * take, take)
        q = query[here, :]
        q = jnp.concatenate([q * mask for mask in head_mask], 0).astype(BF16)
        scores = dot_nt(q, keys[k]) + bias[:, pl.ds(start, take), :].reshape(HEADS * take, length) + masked
        expo = jnp.exp2(scores - jnp.max(scores, -1, keepdims=True))
        share = 1.0 / jnp.sum(expo, -1, keepdims=True)
        mixed = dot(expo.astype(BF16), values[k]) * share
        merged = mixed[:take] * head_mask[0]
        for h in range(1, HEADS):
            merged += mixed[h * take : (h + 1) * take] * head_mask[h]
        gated[here, :] = merged * gate[here, :]

    parts = own // take
    if parts == 1:
        for k in range(sub):
            attend(k, k, 0)
    else:
        lax.fori_loop(0, sub * parts, lambda n, x: (attend(n, n // parts, (n % parts) * take), x)[1], 0)

    piece = rows * sub
    for b in range(far):
        q = iota((piece, total), 0) + b * piece
        residue_, row = div_const(q, sub, total), q & (sub - 1)
        swap = one_hot((row ^ p) * own + residue_ == iota((piece, total), 1))
        gated_rows = dot(swap, gated[...].astype(BF16)).astype(BF16)
        x = dot(swap, own_rows[...].astype(BF16)) + dot(gated_rows, exit_[...])
        outs[b][...] = x.astype(BF16).reshape(rows, sub, width)


def row_call(idx, bias_halves, order, projected, validity, amino, exit_):
    keys, values, query, gate, own_rows = projected
    sub, far = keys.shape[0], len(order)
    _, length, width = keys.shape
    rows = 2 * bias_halves[0].shape[0] // far
    own = far * rows
    vmem = pl.BlockSpec(memory_space=pltpu.VMEM)
    return pl.pallas_call(
        functools.partial(row_kernel, order=order, sub=sub, far=far, rows=rows, length=length, width=width),
        in_specs=[pl.BlockSpec(memory_space=pltpu.SMEM)] + [vmem] * 10,
        out_specs=[vmem] * far,
        out_shape=[jax.ShapeDtypeStruct((rows, sub, width), BF16)] * far,
        scratch_shapes=[
            pltpu.VMEM((own, HEADS, length), F32),
            pltpu.VMEM((HEADS, own, length), F32),
            pltpu.VMEM((sub * own, width), F32),
        ],
        compiler_params=pltpu.CompilerParams(vmem_limit_bytes=vmem_limit(length)),
        cost_estimate=pl.CostEstimate(flops=4 * 10**9, bytes_accessed=4000000, transcendentals=10**5),
        name="row_attention",
    )(idx, *bias_halves, keys, values, query, gate, own_rows, validity, amino, exit_)


def column_kernel(idx, *refs, sub, far, rows, block, depth, width):
    piece_refs, refs = refs[:far], refs[far:]
    entry, twin, *sources = refs[:9]
    updated, left, right, start_rows, gated, rounded, *held = refs[9:-1]
    sems = refs[-1]
    copies = [pltpu.make_async_copy(src, dst, sems.at[n]) for n, (src, dst) in enumerate(zip(sources, held))]
    steps = rows // block

    def begin():
        for copy in copies:
            copy.start()

    def arrived(*which):
        def wait():
            for n in which:
                copies[n].wait()

        if steps == 1:
            wait()
        else:
            pl.when(pl.program_id(0) == 0)(wait)
        return [held[n][...] for n in which]

    if steps == 1:
        begin()
    else:
        pl.when(pl.program_id(0) == 0)(begin)
    me = idx[0]
    z = me // sub
    first = me * rows + (0 if steps == 1 else pl.program_id(0) * block)
    scale = (width // HEADS) ** -0.5 * LOG2E
    total = block * depth
    for b in range(far):
        here = pl.ds(pl.multiple_of((z ^ b) * sub, sub), sub)
        start_rows[:, here, :] = piece_refs[b][...].astype(F32)
    x = start_rows[...].reshape(total, width)
    (col_gain,) = arrived(0)
    normed = layer_norm(x, col_gain).astype(BF16)
    proj = dot(normed, entry[...])
    query = proj[:, :width] * scale
    keys = proj[:, width : 2 * width].astype(BF16)
    values = proj[:, 2 * width : 3 * width].astype(BF16)
    gate = jax.nn.sigmoid(proj[:, 3 * width :])

    (validity,) = arrived(1)
    length = validity.shape[1]
    lanes = 128
    pick = one_hot(iota((length, lanes), 0) == first + iota((length, lanes), 1))
    valid = dot(validity.astype(F32).astype(BF16), pick)
    head_of = iota((1, width), 1) // (width // HEADS)
    head_mask = [jnp.where(head_of == h, 1.0, 0.0) for h in range(HEADS)]
    for i in range(block):
        here = slice(i * depth, (i + 1) * depth)
        q = jnp.concatenate([query[here] * mask for mask in head_mask], 0).astype(BF16)
        masked = jnp.where(valid[:, i : i + 1] > 0, 0.0, MASKED)
        scores = dot_nt(keys[here], q) + masked
        expo = jnp.exp2(scores - jnp.max(scores, 0, keepdims=True))
        weights = (expo * (1.0 / jnp.sum(expo, 0, keepdims=True))).astype(BF16)
        mixed = dot_tn(weights, values[here])
        merged = mixed[:depth] * head_mask[0]
        for h in range(1, HEADS):
            merged += mixed[h * depth : (h + 1) * depth] * head_mask[h]
        gated[here, :] = merged * gate[here]
    exit_, ff_gain, widen, narrow, product_gain = arrived(2, 3, 4, 5, 6)
    x = x + dot(gated[...].astype(BF16), exit_)
    hidden = jnp.maximum(dot(layer_norm(x, ff_gain).astype(BF16), widen).astype(BF16), 0.0)
    x = x + dot(hidden, narrow)
    rounded[...] = x.astype(BF16).reshape(block, depth, width)
    here = pl.ds(0 if steps == 1 else pl.program_id(0) * block, block)
    leave = pltpu.make_async_copy(rounded, updated.at[here], sems.at[len(copies)])
    leave.start()
    outer = layer_norm(x, product_gain).astype(BF16)
    both = dot(outer, twin[...])
    channels = twin.shape[1] // 2
    spread = iota((depth, channels * depth), 1)
    channel = spread // depth
    repeat = one_hot(
        iota((2 * channels, channels * depth), 0) - channels == iota((2 * channels, channels * depth), 1) // depth
    )
    mine = jnp.where(spread - channel * depth == iota((depth, channels * depth), 0), 1.0, 0.0)
    for i in range(block):
        here = slice(i * depth, (i + 1) * depth)
        part = (both[here] * valid[:, i : i + 1]).astype(BF16)
        left[here, :] = part[:, :channels]
        right[0, i : i + 1, :] = jnp.sum(dot(part, repeat) * mine, axis=0, keepdims=True).astype(BF16)
    leave.wait()


def column_call(idx, pieces, validity, col_gain, entry, exit_, ff_gain, widen, narrow, product_gain, twin):
    far = len(pieces)
    rows, sub, width = pieces[0].shape
    depth, length = validity.shape
    block = rows
    while block * depth > 320 and block % 2 == 0:
        block //= 2
    channels = twin.shape[1] // 2
    steps = rows // block
    here = [entry, twin]
    sources = [
        col_gain[None, :],
        validity,
        exit_,
        ff_gain[None, :],
        widen,
        narrow,
        product_gain[None, :],
    ]
    if steps == 1:
        grid, spec = {}, lambda shape, index: pl.BlockSpec(memory_space=pltpu.VMEM)
    else:
        grid, spec = {"grid": (steps,)}, pl.BlockSpec
    return pl.pallas_call(
        functools.partial(column_kernel, sub=sub, far=far, rows=rows, block=block, depth=depth, width=width),
        **grid,
        in_specs=[pl.BlockSpec(memory_space=pltpu.SMEM)]
        + [spec((block, sub, width), lambda s: (s, 0, 0))] * far
        + [spec(a.shape, lambda s: (0, 0)) for a in here]
        + [pl.BlockSpec(memory_space=pltpu.HBM)] * len(sources),
        out_specs=[
            pl.BlockSpec(memory_space=pl.ANY),
            spec((block * depth, channels), lambda s: (s, 0)),
            spec((1, block, channels * depth), lambda s: (s, 0, 0)),
        ],
        out_shape=[
            jax.ShapeDtypeStruct((rows, depth, width), BF16),
            jax.ShapeDtypeStruct((rows * depth, channels), BF16),
            jax.ShapeDtypeStruct((steps, block, channels * depth), BF16),
        ],
        scratch_shapes=[
            pltpu.VMEM((block, depth, width), F32),
            pltpu.VMEM((block * depth, width), F32),
            pltpu.VMEM((block, depth, width), BF16),
        ]
        + [pltpu.VMEM(a.shape, a.dtype) for a in sources]
        + [pltpu.SemaphoreType.DMA((len(sources) + 1,))],
        compiler_params=pltpu.CompilerParams(vmem_limit_bytes=vmem_limit(length)),
        cost_estimate=pl.CostEstimate(flops=5 * 10**9, bytes_accessed=4000000, transcendentals=10**5),
        name="column_attention",
    )(idx, *pieces, *here, *sources)


def mix_kernel(idx, left, factors, validity, out, inverse, *, rows, depth, steps):
    lanes = out.shape[1] // rows
    for e in range(0, out.shape[0] // depth, 2):
        y = dot(left[...], factors[:, e * lanes : (e + 2) * lanes]).astype(BF16)
        for i in range(rows):
            for f in range(2):
                block = y[i * depth : (i + 1) * depth, f * lanes : (f + 1) * lanes]
                out[(e + f) * depth : (e + f + 1) * depth, i * lanes : (i + 1) * lanes] = block

    def count():
        length = validity.shape[1]
        valid = validity[...].astype(F32)
        target = idx[0] * rows + iota((length, rows * lanes), 1) // lanes
        mine = dot(valid.astype(BF16), one_hot(iota((length, rows * lanes), 0) == target))
        mine, turned = mine.astype(BF16), valid.T.astype(BF16)
        part = min(length, 320)
        for start in range(0, length, part):
            inverse[start : start + part, :] = 1.0 / (dot(turned[start : start + part], mine) + OUTER_EPS)

    if steps == 1:
        count()
    else:
        pl.when(pl.program_id(0) == 0)(count)


def mix_call(idx, left, factors, validity, rows):
    total, channels = left.shape
    depth, length = validity.shape
    lanes = factors.shape[1] // channels
    steps = 1 if length <= 320 else 4
    block = channels // steps
    if steps == 1:
        grid, spec = {}, lambda shape, index: pl.BlockSpec(memory_space=pltpu.VMEM)
    else:
        grid, spec = {"grid": (steps,)}, pl.BlockSpec
    return pl.pallas_call(
        functools.partial(mix_kernel, rows=rows, depth=depth, steps=steps),
        **grid,
        in_specs=[
            pl.BlockSpec(memory_space=pltpu.SMEM),
            spec((total, channels), lambda s: (0, 0)),
            spec((channels, block * lanes), lambda s: (0, s)),
            spec((depth, length), lambda s: (0, 0)),
        ],
        out_specs=[
            spec((block * depth, rows * lanes), lambda s: (s, 0)),
            spec((length, rows * lanes), lambda s: (0, 0)),
        ],
        out_shape=[
            jax.ShapeDtypeStruct((channels * depth, rows * lanes), BF16),
            jax.ShapeDtypeStruct((length, rows * lanes), F32),
        ],
        compiler_params=pltpu.CompilerParams(vmem_limit_bytes=vmem_limit(length)),
        cost_estimate=pl.CostEstimate(flops=2 * 10**9, bytes_accessed=4000000, transcendentals=10**5),
        name="left_mix",
    )(idx, left, factors, validity)


def finish_kernel(idx, *refs, pieces, sub, far, rows, length, block):
    near_refs, across_refs, refs = refs[:pieces], refs[pieces : 2 * pieces], refs[2 * pieces :]
    mixed, inverse, pair_one, gain, widen, narrow, out, right, held, sems = refs
    me = idx[0]
    z, p = me // sub, me % sub
    half = far * rows * sub // 2
    lanes = pair_one.shape[2]
    part = min(length, 320)
    alone = block == rows

    def first():
        r = iota((part, half), 1)
        b = div_const(r, rows, half)
        i = r - b * rows
        across_sub = 2 * div_const(b, far, half // rows)
        across_far = b - far * (across_sub >> 1)
        core = jnp.where(across_sub > 0, 1, 0) ^ jnp.where(across_far > 0, 1, 0)
        home = ((z ^ across_far) * sub + (p ^ across_sub ^ core)) * rows + i
        away = ((z ^ across_far) * sub + (p ^ 1 ^ across_sub ^ core)) * rows + i
        near = jnp.concatenate([ref[...].astype(F32) for ref in near_refs], 0).astype(BF16)
        across = jnp.concatenate([ref[...].astype(F32) for ref in across_refs], 0).astype(BF16)

        def arrange(start):
            j = iota((part, half), 0) + start
            here = pl.ds(start, part)
            right[here, :] = (dot(one_hot(j == home), near) + dot(one_hot(j == away), across)).astype(BF16)

        chunks(length, part, arrange)

    if alone:
        first()
    else:
        pl.when(pl.program_id(0) == 0)(first)

    together = 2 if block % 2 == 0 else 1
    copies = []

    def finish(start):
        here = pl.ds(start, part)
        update = dot(right[here, :], mixed[...])
        for n, r in enumerate(range(0, block, together)):
            x = []
            for q in range(r, r + together):
                columns = slice(q * lanes, (q + 1) * lanes)
                x.append(pair_one[q, here, :] + update[:, columns] * inverse[here, columns])
            x = jnp.concatenate(x, 0)
            normed = layer_norm(x, gain[...]).astype(BF16)
            hidden = jnp.maximum(dot(normed, widen[...]).astype(BF16), 0.0)
            x = (x + dot(hidden, narrow[...])).astype(BF16)
            for q in range(together):
                (held if alone else out)[r + q, here, :] = x[q * part : (q + 1) * part]
            if alone:
                done = pl.ds(r, together)
                copies.append(pltpu.make_async_copy(held.at[done], out.at[done], sems.at[n]))
                copies[-1].start()

    chunks(length, part, finish)
    for copy in copies:
        copy.wait()


def finish_call(idx, near, across, mixed, inverse, pair_one, gain, widen, narrow, sub, far):
    rows, length, lanes = pair_one.shape
    block = rows if length <= 320 else 2 if rows % 2 == 0 else 1
    product = mixed.shape[0]
    gain = gain[None, :]
    if block == rows:
        grid, spec = {}, lambda shape, index: pl.BlockSpec(memory_space=pltpu.VMEM)
        out_spec = pl.BlockSpec(memory_space=pl.ANY)
    else:
        grid, spec = {"grid": (rows // block,)}, pl.BlockSpec
        out_spec = spec((block, length, lanes), lambda s: (s, 0, 0))
    whole = lambda a: spec(a.shape, lambda s: (0,) * a.ndim)
    return pl.pallas_call(
        functools.partial(
            finish_kernel, pieces=len(near), sub=sub, far=far, rows=rows, length=length, block=block
        ),
        **grid,
        in_specs=[
            pl.BlockSpec(memory_space=pltpu.SMEM),
            *[whole(a) for a in near + across],
            spec((product, block * lanes), lambda s: (0, s)),
            spec((length, block * lanes), lambda s: (0, s)),
            spec((block, length, lanes), lambda s: (s, 0, 0)),
            whole(gain),
            whole(widen),
            whole(narrow),
        ],
        out_specs=out_spec,
        out_shape=jax.ShapeDtypeStruct((rows, length, lanes), BF16),
        scratch_shapes=[
            pltpu.VMEM((length, product), BF16),
            pltpu.VMEM((rows, length, lanes) if block == rows else (1, 16, 128), BF16),
            pltpu.SemaphoreType.DMA((rows,)),
        ],
        compiler_params=pltpu.CompilerParams(vmem_limit_bytes=vmem_limit(length)),
        cost_estimate=pl.CostEstimate(flops=4 * 10**9, bytes_accessed=4000000, transcendentals=10**5),
        name="pair_update",
    )(idx, *near, *across, mixed, inverse, pair_one, gain, widen, narrow)


def on_device(
    devices,
    alignment_embedding,
    couple_embedding,
    amino_strand,
    amino_validity,
    alignment_validity,
    separation_embedding,
    couple_shift_scaling,
    couple_shift_factors,
    horizontal_scaling_factor,
    horizontal_entry_factors,
    horizontal_exit_factors,
    vertical_scaling_factor,
    vertical_entry_factors,
    vertical_exit_factors,
    alignment_feedforward_scaling,
    alignment_widen_factors,
    alignment_narrow_factors,
    product_scaling_factor,
    product_twin_factors,
    product_exit_factors,
    couple_feedforward_scaling,
    couple_widen_factors,
    couple_narrow_factors,
):
    far = devices // SUB
    idx = lax.axis_index("dap").astype(jnp.int32).reshape(1)

    def swap(x, distance):
        return lax.ppermute(x, "dap", [(d, d ^ distance) for d in range(devices)])

    width = alignment_embedding.shape[2]
    rows = couple_embedding.shape[0]
    depth = alignment_validity.shape[0]

    near = [swap(alignment_embedding, k ^ 1) for k in range(2, SUB, 2)]
    pair_one, bias = pair_call(
        idx, amino_strand, couple_embedding, separation_embedding, couple_shift_scaling, couple_shift_factors
    )
    entry = horizontal_entry_factors.reshape(width, 4 * width)
    order, distance = [0], far // 2
    mine, theirs = bias, swap(bias, SUB * distance ^ 1)
    order += [b ^ distance for b in order]
    while distance > 1:
        distance //= 2
        mine = jnp.concatenate([mine, theirs], 0)
        theirs = swap(mine, SUB * distance ^ 1)
        order += [b ^ distance for b in order]
    near = jnp.concatenate([alignment_embedding, *near], 0)
    entry, mine, near = lax.optimization_barrier((entry, mine, near))
    across = swap(near, 1)
    projected = project_call(idx, [near, across], horizontal_scaling_factor, entry, far, rows)
    sent = row_call(
        idx, [mine, theirs], order, projected, alignment_validity, amino_validity, horizontal_exit_factors
    )
    pieces = [swap(sent[k], SUB * k ^ core_of(k, far)) for k in [*range(2, far), 1]]
    pieces = lax.optimization_barrier(pieces)
    pieces = [sent[0]] + [part for _, part in sorted(zip([*range(2, far), 1], pieces), key=lambda pair: pair[0])]
    updated, left, right = column_call(
        idx,
        pieces,
        alignment_validity,
        vertical_scaling_factor,
        vertical_entry_factors.reshape(width, 4 * width),
        vertical_exit_factors,
        alignment_feedforward_scaling,
        alignment_widen_factors,
        alignment_narrow_factors,
        product_scaling_factor,
        product_twin_factors,
    )
    channels = left.shape[1]
    right = right.reshape(rows, channels * depth)
    factors = product_exit_factors.reshape(channels, -1)
    mixed, inverse = mix_call(idx, left, factors, alignment_validity, rows)
    parts = [swap(right, SUB * k ^ 1) for k in [*range(2, far), 1]]
    mixed, right, *parts = lax.optimization_barrier((mixed, right, *parts))
    parts = [right] + [part for _, part in sorted(zip([*range(2, far), 1], parts), key=lambda pair: pair[0])]
    column = jnp.concatenate(parts, 0)
    near = [swap(column, k ^ 1) for k in [6, 2, 4]]
    beside = swap(column, 1)
    *near, beside = lax.optimization_barrier((*near, beside))
    near = [part for _, part in sorted(zip([6, 2, 4], near), key=lambda pair: pair[0])]
    near = [column, jnp.concatenate(near, 0)]
    across = [beside, swap(near[1], 1)]
    updated_pairs = finish_call(
        idx,
        near,
        across,
        mixed,
        inverse,
        pair_one,
        couple_feedforward_scaling,
        couple_widen_factors,
        couple_narrow_factors,
        SUB,
        far,
    )
    return updated.transpose(1, 0, 2), updated_pairs


def solution(mesh):
    split = P("dap", None, None)
    return jax.shard_map(
        functools.partial(on_device, mesh.shape["dap"]),
        mesh=mesh,
        in_specs=(split, split) + (P(),) * 21,
        out_specs=(P(None, "dap", None), split),
        check_vma=False,
    )
```
